32 devices in a mesh: grp: 8 (over y, x, core), dp: 4 (over z).
Axes of the slice: x: 2, y: 2, z: 4, core: 2. Of those that a mesh axis runs over, the one named last changes fastest.
Arguments:
- tokens: bfloat16 [192, 197, 384], P(('grp', 'dp')), may hold values from -6 to 6
- kinds: int32 [192], P(('grp', 'dp')), may hold values from 0 to 2
- interp: float32 [3, 197, 197], replicated, may hold values from -0.4375 to 0.4375
- pos_base: bfloat16 [197, 384], replicated, may hold values from -5 to 5
- ln_gain: bfloat16 [2, 2, 384], replicated, may hold values from 0.5 to 1.5
- ln_bias: bfloat16 [2, 2, 384], replicated, may hold values from -2 to 2
- w_qkv: bfloat16 [2, 384, 1152], replicated, may hold values from -0.3125 to 0.3125
- qv_bias: bfloat16 [2, 2, 384], replicated, may hold values from -2 to 2
- w_out: bfloat16 [2, 384, 384], replicated, may hold values from -1.25 to 1.25
- out_bias: bfloat16 [2, 384], replicated, may hold values from -2 to 2
- w_fc1: bfloat16 [2, 384, 1536], replicated, may hold values from -0.3125 to 0.3125
- fc1_bias: bfloat16 [2, 1536], replicated, may hold values from -2 to 2
- w_fc2: bfloat16 [2, 1536, 384], replicated, may hold values from -0.15625 to 0.15625
- fc2_bias: bfloat16 [2, 384], replicated, may hold values from -2 to 2
- cotangent: bfloat16 [192, 197, 384], P(('grp', 'dp')), may hold values from -6 to 6
Outputs:
- mixed: bfloat16 [192, 197, 384], P(('grp', 'dp'))
- grad_tokens: float32 [192, 197, 384], P(('grp', 'dp'))
- grad_pos: float32 [197, 384], replicated
- grad_ln_gain: float32 [2, 2, 384], replicated
- grad_ln_bias: float32 [2, 2, 384], replicated
- grad_w_qkv: float32 [2, 384, 1152], replicated
- grad_qv_bias: float32 [2, 2, 384], replicated
- grad_w_out: float32 [2, 384, 384], replicated
- grad_out_bias: float32 [2, 384], replicated
- grad_w_fc1: float32 [2, 384, 1536], replicated
- grad_fc1_bias: float32 [2, 1536], replicated
- grad_w_fc2: float32 [2, 1536, 384], replicated
- grad_fc2_bias: float32 [2, 384], replicated
The draws below stay inside these ranges and needn't reach their ends.
All inputs are finite; a program needn't handle non-finite values.
Results may differ from the reference program's by a relative error of at most 0.0085.
Values sent between devices are 32-bit elements; how exact they have to be, the bound alone decides.
No kernel may reach another device: no remote copies, remote signals or barrier semaphores. Data moves between devices by JAX's collectives and lax.ppermute only.
A program may use at most 192 MiB of HBM per device.

```python
import jax
import jax.numpy as jnp
from jax import lax

D = 384
HEADS = 6
HEAD = 64
FF = 1536
BASE = 197
CROP_B = 181
CROP_C = 193
LAYERS = 2
IMG_DEV = 6
IMAGES = 192


def plant(drawn, stream_key, smallest, largest):
    longest = drawn.shape.index(max(drawn.shape))
    spots = []
    for shift in (0, 1):
        where = [jax.random.randint(jax.random.fold_in(stream_key, axis), (), 0, length) for axis, length in enumerate(drawn.shape)]
        where[longest] = (where[longest] + shift) % drawn.shape[longest]
        spots.append(tuple(where))
    return drawn.at[spots[0]].set(smallest).at[spots[1]].set(largest)


def strengthened(values, rng, source, target, shards_of, factor):
    owner, partner = [(jnp.arange(values.shape[position]) // (values.shape[position] // shards_of)).reshape([-1 if axis == position else 1 for axis in range(values.ndim)]) for position in (source, target)]
    chosen = jax.random.permutation(rng, shards_of)[partner]
    strong = (owner == chosen) | (owner == (partner + shards_of // 2) % shards_of)
    return jnp.where(strong, factor * values, values)


def level_of(stream_key, dims, cuts, smallest, top_value):
    level, own = 1.0, jax.random.fold_in(stream_key, 6)
    for position, blocks in cuts:
        heights = jnp.exp(jax.random.uniform(jax.random.fold_in(own, position), (blocks,), jnp.float32, smallest / len(cuts), top_value / len(cuts)))
        level = level * jnp.repeat(heights, dims[position] // blocks).reshape([-1 if axis == position else 1 for axis in range(len(dims))])
    return level


def scatter_about(key, shape, deviation, limit, split=(), held_as=jnp.bfloat16):
    level = level_of(key, shape, split, -0.22, 0.18) if split else 1.0
    array = jax.random.normal(key, shape, jnp.float32) * deviation * level
    return jnp.minimum(jnp.maximum(array, -limit), limit).astype(held_as)


def noise_with(rng, shape, deviation, limit, cuts, heavy, held_as=jnp.bfloat16):
    array = deviation * jax.random.normal(rng, shape, jnp.float32)
    if cuts:
        array = array * level_of(rng, shape, cuts, -0.22, 0.18)
    return jnp.clip(strengthened(array, jax.random.fold_in(rng, 3), *heavy), -limit, limit).astype(held_as)


def setup_inputs(seed: int = 0) -> dict:
    seeds = jax.random.split(jax.random.key(seed), 16)
    return {
        "tokens": scatter_about(seeds[0], (IMAGES, BASE, D), 1.0, 6.0, ((0, 32),)),
        "kinds": plant(jax.random.randint(seeds[1], (IMAGES,), 0, 3), jax.random.fold_in(seeds[1], 1), 0, 2).astype(jnp.int32),
        "interp": scatter_about(seeds[2], (3, BASE, BASE), BASE ** -0.5, 0.4375, (), jnp.float32),
        "pos_base": scatter_about(seeds[3], (BASE, D), 1.0, 5.0),
        "ln_gain": jnp.clip(1.0 + 0.1 * jax.random.normal(seeds[4], (LAYERS, 2, D), jnp.float32), 0.5, 1.5).astype(jnp.bfloat16),
        "ln_bias": scatter_about(seeds[5], (LAYERS, 2, D), 0.3, 2.0),
        "w_qkv": scatter_about(seeds[6], (LAYERS, D, 3 * D), D ** -0.5, 0.3125),
        "qv_bias": scatter_about(seeds[7], (LAYERS, 2, D), 0.3, 2.0),
        "w_out": scatter_about(seeds[8], (LAYERS, D, D), (D // 16) ** -0.5, 1.25),
        "out_bias": scatter_about(seeds[9], (LAYERS, D), 0.3, 2.0),
        "w_fc1": scatter_about(seeds[10], (LAYERS, D, FF), D ** -0.5, 0.3125),
        "fc1_bias": scatter_about(seeds[11], (LAYERS, FF), 0.3, 2.0),
        "w_fc2": scatter_about(seeds[12], (LAYERS, FF, D), FF ** -0.5, 0.15625),
        "fc2_bias": scatter_about(seeds[13], (LAYERS, D), 0.3, 2.0),
        "cotangent": noise_with(seeds[14], (IMAGES, BASE, D), 1.0, 6.0, ((0, 32),), (0, 2, 32, 2.75)),
    }


@jax.custom_vjp
def low(v):
    return lax.optimization_barrier(v.astype(jnp.bfloat16)).astype(jnp.float32)

@jax.custom_vjp
def low_back(v):
    return v

def low_keep(v):
    return (low(v), None)

def low_pass(kept, grad):
    return (grad,)

def back_keep(v):
    return (v, None)

def back_low(kept, grad):
    return (low(grad),)
low.defvjp(low_keep, low_pass)
low_back.defvjp(back_keep, back_low)
EPS = 1e-06
HIGH = lax.Precision.HIGHEST

def crop_lengths(kinds):
    return jnp.where(kinds == 0, BASE, jnp.where(kinds == 1, CROP_B, CROP_C)).astype(jnp.int32)

def normalize(input_rows, norm_gain, shift_bias):
    row_mean = lax.optimization_barrier(jnp.mean(input_rows, -1, keepdims=True))
    centered_input = input_rows - row_mean
    var = lax.optimization_barrier(jnp.mean(centered_input * centered_input, -1, keepdims=True))
    return centered_input * lax.rsqrt(var + EPS) * norm_gain + shift_bias

def layer(input_rows, valid, norm_gains, norm_biases, w_qkv, qv_bias, w_out, out_bias, w_fc1, fc1_bias, w_fc2, fc2_bias):
    count, rows, width = input_rows.shape
    norm_output = low(normalize(input_rows, norm_gains[0], norm_biases[0]))
    bias_full = jnp.concatenate([qv_bias[0], jnp.zeros_like(qv_bias[0]), qv_bias[1]])
    qkv = jnp.einsum('nld,de->nle', norm_output, w_qkv, precision=HIGH) + bias_full
    qkv = low(low_back(qkv)).reshape(count, rows, 3, HEADS, HEAD)
    query, keys, values = (qkv[:, :, 0], qkv[:, :, 1], qkv[:, :, 2])
    scores = low_back(jnp.einsum('nqhd,nkhd->nhqk', query, keys, precision=HIGH) * HEAD ** (-0.5))
    scores = jnp.where(valid[:, None, None, :], scores, -1000000000.0)
    probs = low(jax.nn.softmax(scores, axis=-1))
    attended = jnp.einsum('nhqk,nkhd->nqhd', probs, values, precision=HIGH).reshape(count, rows, width)
    attended = low(low_back(attended))
    input_rows = input_rows + low_back(jnp.einsum('nld,de->nle', attended, w_out, precision=HIGH) + out_bias)
    second_moment = low(normalize(input_rows, norm_gains[1], norm_biases[1]))
    pre = low_back(jnp.einsum('nld,df->nlf', second_moment, w_fc1, precision=HIGH) + fc1_bias)
    hidden = low(jax.nn.gelu(pre, approximate=False))
    return input_rows + low_back(jnp.einsum('nlf,fd->nld', hidden, w_fc2, precision=HIGH) + fc2_bias)

def block_forward(tok, kin, interp, params):
    pos_base, ln_gain, ln_bias, w_qkv, qv_bias, w_out, out_bias, w_fc1, fc1_bias, w_fc2, fc2_bias = params
    lengths = crop_lengths(kin)
    valid = jnp.arange(BASE).astype(jnp.int32)[None, :] < lengths[:, None]
    mask = valid.astype(jnp.float32)[:, :, None]
    positions = jnp.einsum('nlb,bd->nld', interp[kin], pos_base, precision=HIGH)
    state = (tok + positions) * mask
    for index in range(LAYERS):
        state = layer(state, valid, ln_gain[index], ln_bias[index], w_qkv[index], qv_bias[index], w_out[index], out_bias[index], w_fc1[index], fc1_bias[index], w_fc2[index], fc2_bias[index])
    return state * mask

def reference(tokens, kinds, interp, pos_base, ln_gain, ln_bias, w_qkv, qv_bias, w_out, out_bias, w_fc1, fc1_bias, w_fc2, fc2_bias, cotangent):
    params = tuple((item.astype(jnp.float32) for item in (pos_base, ln_gain, ln_bias, w_qkv, qv_bias, w_out, out_bias, w_fc1, fc1_bias, w_fc2, fc2_bias)))
    blocks = IMAGES // IMG_DEV
    tok = tokens.astype(jnp.float32).reshape(blocks, IMG_DEV, BASE, D)
    kin = kinds.astype(jnp.int32).reshape(blocks, IMG_DEV)
    stepper = jax.checkpoint(block_forward)

    def whole(tok_all, params_all):
        return lax.map(lambda item: stepper(item[0], item[1], interp, params_all), (tok_all, kin))
    output, pull = jax.vjp(whole, tok, params)
    grad_tok, grads = pull(cotangent.astype(jnp.float32).reshape(blocks, IMG_DEV, BASE, D))
    mixed = output.reshape(IMAGES, BASE, D).astype(jnp.bfloat16)
    grad_tokens = grad_tok.reshape(IMAGES, BASE, D)
    return (mixed, grad_tokens, grads[0], grads[1], grads[2], grads[3], grads[4], grads[5], grads[6], grads[7], grads[8], grads[9], grads[10])
```

```python
from functools import partial

import jax
import jax.numpy as jnp
from jax import lax
from jax.experimental import pallas as pl
from jax.experimental.pallas import tpu as pltpu
from jax.sharding import PartitionSpec as P

HEADS = 6
HEAD = 64
BASE = 197
CROP_B = 181
CROP_C = 193
EPS = 1e-06
F32 = jnp.float32
BF16 = jnp.bfloat16
VMEM_LIMIT = 60 * 1024 * 1024

ERF_P = 0.39
ERF_C = (0.11766263, 0.04569411, 0.32477995, -0.31770045, 0.44333237, -0.11376861)


def dot(a, b):
    return lax.dot_general(a, b, (((1,), (0,)), ((), ())), preferred_element_type=F32)


def dot_bt(a, b):
    return lax.dot_general(a, b, (((1,), (1,)), ((), ())), preferred_element_type=F32)


def dot_at(a, b):
    return lax.dot_general(a, b, (((0,), (0,)), ((), ())), preferred_element_type=F32)


def split3(x):
    hi = x.astype(BF16)
    rest = x - hi.astype(F32)
    mid = rest.astype(BF16)
    low = (rest - mid.astype(F32)).astype(BF16)
    return hi, mid, low


def length_of(kind):
    return jnp.where(kind == 0, BASE, jnp.where(kind == 1, CROP_B, CROP_C)).astype(jnp.int32)


def pick(ref, layer):
    row = ref[0:1].astype(F32)
    for index in range(1, ref.shape[0]):
        row = jnp.where(layer == index, ref[index : index + 1].astype(F32), row)
    return row


def norm(x):
    width = x.shape[-1]
    mean = jnp.sum(x, -1, keepdims=True) * (1.0 / width)
    centered = x - mean
    var = jnp.sum(centered * centered, -1, keepdims=True) * (1.0 / width)
    rstd = lax.rsqrt(var + EPS)
    return centered * rstd, rstd


def norm_back(dc, xhat, rstd, gain):
    width = dc.shape[-1]
    dxh = dc * gain
    m1 = jnp.sum(dxh, -1, keepdims=True) * (1.0 / width)
    m2 = jnp.sum(dxh * xhat, -1, keepdims=True) * (1.0 / width)
    return rstd * (dxh - m1 - xhat * m2)


def gelu_parts(x):
    d = 1.0 + (ERF_P * 0.5**0.5) * jnp.abs(x)
    r = pl.reciprocal(d, approx=True)
    t = r * (2.0 - d * r)
    e = jnp.exp(x * x * -0.5)
    q = ERF_C[5]
    for k in (4, 3, 2, 1, 0):
        q = q * t + ERF_C[k]
    q = q * t * e
    phi = jnp.where(x > 0, 1.0 - q, q)
    return x * phi, phi + x * e * 0.3989422804014327


def fwd_kernel(
    kinds, tok, interp, pos, gain, bias, w_qkv, qvb, w_out, outb, w1, b1, w2, b2,
    mixed, a_o, qkv_o, lse_o, o_o, c_o, gp_o, gh_o, xh1_o, r1_o, xh2_o, r2_o,
    x_s, table_s, mid_s, o_s,
):
    block, layer = pl.program_id(0), pl.program_id(1)
    images, rows, width = tok.shape
    padded = x_s.shape[1]
    flat = images * padded
    heads_pair = 2 * HEAD

    @pl.when((block == 0) & (layer == 0))
    def _():
        for kind in range(interp.shape[0]):
            total = jnp.zeros((rows, width), F32)
            for part in split3(interp[kind])[::-1]:
                total += dot(part, pos[...])
            table_s[kind, 0:rows, :] = total

    @pl.when(layer == 0)
    def _():
        for i in range(images):
            kind = kinds[block * images + i]
            here = lax.broadcasted_iota(jnp.int32, (rows, 1), 0) < length_of(kind)
            h0 = tok[i].astype(F32) + table_s[kind, 0:rows, :]
            x_s[i] = jnp.zeros((padded, width), F32)
            x_s[i, 0:rows, :] = jnp.where(here, h0, 0.0)

    x = x_s[...].reshape(flat, width)
    xhat, rstd = norm(x)
    a = (xhat * gain[0, 0:1].astype(F32) + bias[0, 0:1].astype(F32)).astype(BF16)
    a_o[0] = a
    xh1_o[0] = xhat.astype(BF16)
    r1_o[0] = rstd
    for part in range(3):
        cols = slice(part * width, (part + 1) * width)
        part_out = dot(a, w_qkv[0, :, cols])
        if part != 1:
            part_out += qvb[0, part // 2 : part // 2 + 1].astype(F32)
        qkv_o[0, :, cols] = part_out.astype(BF16)
    lane = lax.broadcasted_iota(jnp.int32, (1, heads_pair), 1)
    low_lanes = lane < HEAD
    for i in range(images):
        r0 = i * padded
        length = length_of(kinds[block * images + i])
        key_ok = lax.broadcasted_iota(jnp.int32, (padded, 1), 0) < length
        for pair in range(HEADS // 2):
            c0 = pair * heads_pair
            q2 = qkv_o[0, r0 : r0 + padded, c0 : c0 + heads_pair]
            k2 = qkv_o[0, r0 : r0 + padded, width + c0 : width + c0 + heads_pair]
            v2 = qkv_o[0, r0 : r0 + padded, 2 * width + c0 : 2 * width + c0 + heads_pair]
            outs = []
            for sub in range(2):
                mine = low_lanes if sub == 0 else jnp.logical_not(low_lanes)
                km = k2 * jnp.where(mine, HEAD**-0.5, 0.0).astype(BF16)
                s = jnp.where(key_ok, dot_bt(km, q2), -1e9)
                top = jnp.max(s, 0, keepdims=True)
                e = jnp.exp(s - top)
                total = jnp.sum(e, 0, keepdims=True)
                head = 2 * pair + sub
                lse_o[0, i, head : head + 1, :] = top + jnp.log(total)
                p = (e * (1.0 / total)).astype(BF16)
                outs.append(dot_at(p, v2))
            o_s[r0 : r0 + padded, c0 : c0 + heads_pair] = jnp.where(low_lanes, outs[0], outs[1]).astype(BF16)
    o = o_s[...]
    o_o[0] = o
    mid = x_s[...].reshape(flat, width) + dot(o, w_out[0]) + pick(outb, layer)
    mid_s[...] = mid
    xhat, rstd = norm(mid)
    c = (xhat * gain[0, 1:2].astype(F32) + bias[0, 1:2].astype(F32)).astype(BF16)
    c_o[0] = c
    xh2_o[0] = xhat.astype(BF16)
    r2_o[0] = rstd
    hidden = w1.shape[2]
    bias1 = pick(b1, layer)
    step = width
    total = mid_s[...] + pick(b2, layer)
    for f in range(0, hidden, step):
        pre = dot(c, w1[0, :, f : f + step]) + bias1[:, f : f + step]
        gh, gp = gelu_parts(pre)
        gh = gh.astype(BF16)
        gh_o[0, :, f : f + step] = gh
        gp_o[0, :, f : f + step] = gp.astype(BF16)
        total += dot(gh, w2[0, f : f + step, :])
    x_s[...] = total.reshape(images, padded, width)

    @pl.when(layer == pl.num_programs(1) - 1)
    def _():
        for i in range(images):
            kind = kinds[block * images + i]
            here = lax.broadcasted_iota(jnp.int32, (rows, 1), 0) < length_of(kind)
            mixed[i] = jnp.where(here, x_s[i, 0:rows, :], 0.0).astype(BF16)


def forward(kinds, tokens, interp, pos_base, ln_gain, ln_bias, w_qkv, qv_bias, w_out, out_bias, w_fc1, fc1_bias, w_fc2, fc2_bias, padded, per):
    count, rows, width = tokens.shape
    layers, _, hidden = w_fc1.shape
    blocks = count // per
    flat = per * padded
    whole = lambda shape: pl.BlockSpec(shape, lambda b, l, k: (0,) * len(shape))
    by_layer = lambda shape: pl.BlockSpec((1,) + shape, lambda b, l, k: (l,) + (0,) * len(shape))
    by_image = lambda: pl.BlockSpec((per, rows, width), lambda b, l, k: (b, 0, 0))
    saved = lambda feat: pl.BlockSpec((1, flat, feat), lambda b, l, k: (l, b, 0))
    shape = lambda feat, dtype: jax.ShapeDtypeStruct((layers, count * padded, feat), dtype)
    return pl.pallas_call(
        fwd_kernel,
        grid_spec=pltpu.PrefetchScalarGridSpec(
            num_scalar_prefetch=1,
            grid=(blocks, layers),
            in_specs=[
                by_image(),
                whole(interp.shape),
                whole(pos_base.shape),
                by_layer((2, width)),
                by_layer((2, width)),
                by_layer((width, 3 * width)),
                by_layer((2, width)),
                by_layer((width, width)),
                whole(out_bias.shape),
                by_layer((width, hidden)),
                whole(fc1_bias.shape),
                by_layer((hidden, width)),
                whole(fc2_bias.shape),
            ],
            out_specs=[
                by_image(),
                saved(width),
                saved(3 * width),
                pl.BlockSpec((1, per, 8, padded), lambda b, l, k: (l, b, 0, 0)),
                saved(width),
                saved(width),
                saved(hidden),
                saved(hidden),
                saved(width),
                saved(1),
                saved(width),
                saved(1),
            ],
            scratch_shapes=[
                pltpu.VMEM((per, padded, width), F32),
                pltpu.VMEM((3, padded, width), F32),
                pltpu.VMEM((flat, width), F32),
                pltpu.VMEM((flat, width), BF16),
            ],
        ),
        out_shape=[
            jax.ShapeDtypeStruct(tokens.shape, BF16),
            shape(width, BF16),
            shape(3 * width, BF16),
            jax.ShapeDtypeStruct((layers, count, 8, padded), F32),
            shape(width, BF16),
            shape(width, BF16),
            shape(hidden, BF16),
            shape(hidden, BF16),
            shape(width, BF16),
            shape(1, F32),
            shape(width, BF16),
            shape(1, F32),
        ],
        compiler_params=pltpu.CompilerParams(vmem_limit_bytes=VMEM_LIMIT),
        name="encoder_forward",
    )(kinds, tokens, interp, pos_base, ln_gain, ln_bias, w_qkv, qv_bias, w_out, out_bias, w_fc1, fc1_bias, w_fc2, fc2_bias)


def mlp_back_kernel(top, kinds, dx_ref, c, gh, gp, xh, rstd, gain, w1, w2, dmid, gw1, gw2, sums, dx_s):
    block = pl.program_id(0)

    @pl.when(block == 0)
    def _():
        gw1[...] = jnp.zeros_like(gw1)
        gw2[...] = jnp.zeros_like(gw2)
        sums[...] = jnp.zeros_like(sums)

    if top:
        images, rows, width = dx_ref.shape
        padded = dx_s.shape[1]
        for i in range(images):
            kind = kinds[block * images + i]
            here = lax.broadcasted_iota(jnp.int32, (rows, 1), 0) < length_of(kind)
            dx_s[i] = jnp.zeros((padded, width), F32)
            dx_s[i, 0:rows, :] = jnp.where(here, dx_ref[i].astype(F32), 0.0)
        dx = dx_s[...].reshape(images * padded, width)
    else:
        dx = dx_ref[...]
    flat, width = dx.shape
    hidden = w1.shape[2]
    dz = dx.astype(BF16)
    sums[0:1, 0:width] += jnp.sum(dz.astype(F32), 0, keepdims=True)
    step = width
    dc = jnp.zeros((flat, width), F32)
    for f in range(0, hidden, step):
        cols = slice(f, f + step)
        dgh = dot_bt(dz, w2[0, cols, :])
        dpre = (dgh * gp[0, :, cols].astype(F32)).astype(BF16)
        sums[1:2, cols] += jnp.sum(dpre.astype(F32), 0, keepdims=True)
        gw1[:, cols] += dot_at(c[0], dpre)
        gw2[cols, :] += dot_at(gh[0, :, cols], dz)
        dc += dot_bt(dpre, w1[0, :, cols])
    xhat = xh[0].astype(F32)
    sums[2:3, 0:width] += jnp.sum(dc * xhat, 0, keepdims=True)
    sums[3:4, 0:width] += jnp.sum(dc, 0, keepdims=True)
    dmid[...] = dx + norm_back(dc, xhat, rstd[0], gain[0, 1:2].astype(F32))


def mlp_back(layer, top, kinds, dx, c, gh, gp, xh, rstd, gain, w1, w2, padded, per):
    layers, width, hidden = w1.shape
    total = c.shape[1]
    flat = per * padded
    blocks = total // flat
    saved = lambda feat: pl.BlockSpec((1, flat, feat), lambda b, k: (layer, b, 0))
    param = lambda *shape: pl.BlockSpec((1,) + shape, lambda b, k: (layer, 0, 0))
    fixed = lambda *shape: pl.BlockSpec(shape, lambda b, k: (0, 0))
    if top:
        dx_spec = pl.BlockSpec((per,) + dx.shape[1:], lambda b, k: (b, 0, 0))
    else:
        dx_spec = pl.BlockSpec((flat, width), lambda b, k: (b, 0))
    return pl.pallas_call(
        partial(mlp_back_kernel, top),
        grid_spec=pltpu.PrefetchScalarGridSpec(
            num_scalar_prefetch=1,
            grid=(blocks,),
            in_specs=[
                dx_spec,
                saved(width),
                saved(hidden),
                saved(hidden),
                saved(width),
                saved(1),
                param(2, width),
                param(width, hidden),
                param(hidden, width),
            ],
            out_specs=[
                pl.BlockSpec((flat, width), lambda b, k: (b, 0)),
                fixed(width, hidden),
                fixed(hidden, width),
                fixed(8, hidden),
            ],
            scratch_shapes=[pltpu.VMEM((per, padded, width), F32)],
        ),
        out_shape=[
            jax.ShapeDtypeStruct((total, width), F32),
            jax.ShapeDtypeStruct((width, hidden), F32),
            jax.ShapeDtypeStruct((hidden, width), F32),
            jax.ShapeDtypeStruct((8, hidden), F32),
        ],
        compiler_params=pltpu.CompilerParams(vmem_limit_bytes=VMEM_LIMIT),
        name="mlp_backward",
    )(kinds, dx, c, gh, gp, xh, rstd, gain, w1, w2)


def attn_back_kernel(bottom, kinds, dmid, o, qkv, lse, a, xh, rstd, gain, w_qkv, w_out, *rest):
    if bottom:
        interp, dx_ref, gqkv, gout, sums, gpos, dqkv_s, do_s, kind_s = rest
    else:
        dx_ref, gqkv, gout, sums, dqkv_s, do_s = rest
    block = pl.program_id(0)
    images = lse.shape[1]
    flat, width = dmid.shape
    padded = flat // images

    @pl.when(block == 0)
    def _():
        gqkv[...] = jnp.zeros_like(gqkv)
        gout[...] = jnp.zeros_like(gout)
        sums[...] = jnp.zeros_like(sums)
        if bottom:
            kind_s[...] = jnp.zeros_like(kind_s)

    dy = dmid[...].astype(BF16)
    sums[0:1, 0:width] += jnp.sum(dy.astype(F32), 0, keepdims=True)
    do_s[...] = dot_bt(dy, w_out[0]).astype(BF16)
    gout[...] += dot_at(o[0], dy)
    pair_width = 2 * HEAD
    low_lanes = lax.broadcasted_iota(jnp.int32, (1, pair_width), 1) < HEAD
    scale = HEAD**-0.5
    for i in range(images):
        rows = slice(i * padded, (i + 1) * padded)
        length = length_of(kinds[block * images + i])
        key_ok = lax.broadcasted_iota(jnp.int32, (padded, 1), 0) < length
        for pair in range(HEADS // 2):
            c0 = pair * pair_width
            part = lambda base: slice(base + c0, base + c0 + pair_width)
            q2, k2, v2 = qkv[0, rows, part(0)], qkv[0, rows, part(width)], qkv[0, rows, part(2 * width)]
            do2 = do_s[rows, part(0)]
            dq, dk, dv = [], [], []
            for sub in range(2):
                mine = low_lanes if sub == 0 else jnp.logical_not(low_lanes)
                head = 2 * pair + sub
                km = k2 * jnp.where(mine, scale, 0.0).astype(BF16)
                vm = v2 * jnp.where(mine, 1.0, 0.0).astype(BF16)
                s = jnp.where(key_ok, dot_bt(km, q2), -1e9)
                p = jnp.exp(s - lse[0, i, head : head + 1, :])
                dp = dot_bt(vm, do2)
                delta = jnp.sum(dp * p, 0, keepdims=True)
                ds = (p * (dp - delta)).astype(BF16)
                dv.append(dot(p.astype(BF16), do2))
                dk.append(dot(ds, q2))
                dq.append(dot_at(ds, k2))
            dqkv_s[rows, part(0)] = (jnp.where(low_lanes, dq[0], dq[1]) * scale).astype(BF16)
            dqkv_s[rows, part(width)] = (jnp.where(low_lanes, dk[0], dk[1]) * scale).astype(BF16)
            dqkv_s[rows, part(2 * width)] = jnp.where(low_lanes, dv[0], dv[1]).astype(BF16)
    da = jnp.zeros((flat, width), F32)
    for index in range(3):
        cols = slice(index * width, (index + 1) * width)
        d = dqkv_s[:, cols]
        if index != 1:
            sums[1 + index // 2 : 2 + index // 2, 0:width] += jnp.sum(d.astype(F32), 0, keepdims=True)
        gqkv[:, cols] += dot_at(a[0], d)
        da += dot_bt(d, w_qkv[0, :, cols])
    xhat = xh[0].astype(F32)
    sums[3:4, 0:width] += jnp.sum(da * xhat, 0, keepdims=True)
    sums[4:5, 0:width] += jnp.sum(da, 0, keepdims=True)
    dx = dmid[...] + norm_back(da, xhat, rstd[0], gain[0, 0:1].astype(F32))
    if not bottom:
        dx_ref[...] = dx
        return
    real = dx_ref.shape[1]
    for i in range(images):
        kind = kinds[block * images + i]
        here = lax.broadcasted_iota(jnp.int32, (padded, 1), 0) < length_of(kind)
        mine = jnp.where(here, dx[i * padded : (i + 1) * padded], 0.0)
        dx_ref[i] = mine[0:real]
        kind_s[kind] += mine

    @pl.when(block == pl.num_programs(0) - 1)
    def _():
        total = jnp.zeros((real, width), F32)
        for kind in range(interp.shape[0]):
            hi, mid, _ = split3(interp[kind])
            ghi, gmid, _ = split3(kind_s[kind, 0:real, :])
            total += dot_at(mid, ghi) + dot_at(hi, gmid) + dot_at(hi, ghi)
        gpos[...] = total


def attn_back(layer, bottom, kinds, dmid, o, qkv, lse, a, xh, rstd, gain, w_qkv, w_out, interp, like, padded, per):
    width = dmid.shape[1]
    total = dmid.shape[0]
    flat = per * padded
    blocks = total // flat
    saved = lambda feat: pl.BlockSpec((1, flat, feat), lambda b, k: (layer, b, 0))
    param = lambda *shape: pl.BlockSpec((1,) + shape, lambda b, k: (layer, 0, 0))
    fixed = lambda *shape: pl.BlockSpec(shape, lambda b, k: (0,) * len(shape))
    in_specs = [
        pl.BlockSpec((flat, width), lambda b, k: (b, 0)),
        saved(width),
        saved(3 * width),
        pl.BlockSpec((1, per, 8, padded), lambda b, k: (layer, b, 0, 0)),
        saved(width),
        saved(width),
        saved(1),
        param(2, width),
        param(width, 3 * width),
        param(width, width),
    ]
    grads_specs = [fixed(width, 3 * width), fixed(width, width), fixed(8, width)]
    grads = [
        jax.ShapeDtypeStruct((width, 3 * width), F32),
        jax.ShapeDtypeStruct((width, width), F32),
        jax.ShapeDtypeStruct((8, width), F32),
    ]
    scratch = [pltpu.VMEM((flat, 3 * width), BF16), pltpu.VMEM((flat, width), BF16)]
    args = [kinds, dmid, o, qkv, lse, a, xh, rstd, gain, w_qkv, w_out]
    if bottom:
        rows = like.shape[1]
        in_specs.append(fixed(*interp.shape))
        args.append(interp)
        out_specs = [pl.BlockSpec((per, rows, width), lambda b, k: (b, 0, 0))] + grads_specs + [fixed(rows, width)]
        out_shape = [jax.ShapeDtypeStruct(like.shape, F32)] + grads + [jax.ShapeDtypeStruct((rows, width), F32)]
        scratch.append(pltpu.VMEM((3, padded, width), F32))
    else:
        out_specs = [pl.BlockSpec((flat, width), lambda b, k: (b, 0))] + grads_specs
        out_shape = [jax.ShapeDtypeStruct((total, width), F32)] + grads
    return pl.pallas_call(
        partial(attn_back_kernel, bottom),
        grid_spec=pltpu.PrefetchScalarGridSpec(
            num_scalar_prefetch=1,
            grid=(blocks,),
            in_specs=in_specs,
            out_specs=out_specs,
            scratch_shapes=scratch,
        ),
        out_shape=out_shape,
        compiler_params=pltpu.CompilerParams(vmem_limit_bytes=VMEM_LIMIT),
        name="attention_backward",
    )(*args)


def on_device(tokens, kinds, interp, pos_base, ln_gain, ln_bias, w_qkv, qv_bias, w_out, out_bias, w_fc1, fc1_bias, w_fc2, fc2_bias, cotangent):
    count, rows, width = tokens.shape
    layers = w_qkv.shape[0]
    padded = -(-rows // 16) * 16
    per = 2 if count % 2 == 0 else 1
    mixed, a, qkv, lse, o, c, gp, gh, xh1, r1, xh2, r2 = forward(
        kinds, tokens, interp, pos_base, ln_gain, ln_bias, w_qkv, qv_bias, w_out, out_bias, w_fc1, fc1_bias, w_fc2, fc2_bias, padded, per
    )
    dx = cotangent
    grads = [None] * layers
    for layer in reversed(range(layers)):
        dmid, gw1, gw2, mlp_sums = mlp_back(
            layer, layer == layers - 1, kinds, dx, c, gh, gp, xh2, r2, ln_gain, w_fc1, w_fc2, padded, per
        )
        out = attn_back(
            layer, layer == 0, kinds, dmid, o, qkv, lse, a, xh1, r1, ln_gain, w_qkv, w_out, interp, tokens, padded, per
        )
        dx, gqkv, gout, attn_sums = out[:4]
        grads[layer] = (
            jnp.stack([attn_sums[3], mlp_sums[2, :width]]),
            jnp.stack([attn_sums[4], mlp_sums[3, :width]]),
            gqkv,
            attn_sums[1:3],
            gout,
            attn_sums[0],
            gw1,
            mlp_sums[1],
            gw2,
            mlp_sums[0, :width],
        )
    stacked = tuple(jnp.stack([grads[layer][member] for layer in range(layers)]) for member in range(10))
    summed = lax.psum((out[4],) + stacked, ("grp", "dp"))
    return (mixed, dx) + tuple(summed)


def solution(mesh):
    split = P(("grp", "dp"), None, None)
    return jax.shard_map(
        on_device,
        mesh=mesh,
        in_specs=(split, P(("grp", "dp"))) + (P(),) * 12 + (split,),
        out_specs=(split, split) + (P(),) * 11,
        check_vma=False,
    )
```

```python
from functools import partial

import jax
import jax.numpy as jnp
from jax import lax
from jax.experimental import pallas as pl
from jax.experimental.pallas import tpu as pltpu
from jax.sharding import PartitionSpec as P

HEADS = 6
HEAD = 64
BASE = 197
CROP_B = 181
CROP_C = 193
EPS = 1e-06
F32 = jnp.float32
BF16 = jnp.bfloat16
VMEM_LIMIT = 60 * 1024 * 1024

ERF_P = 0.39
ERF_C = (0.11766263, 0.04569411, 0.32477995, -0.31770045, 0.44333237, -0.11376861)


def dot(a, b):
    return lax.dot_general(a, b, (((1,), (0,)), ((), ())), preferred_element_type=F32)


def dot_bt(a, b):
    return lax.dot_general(a, b, (((1,), (1,)), ((), ())), preferred_element_type=F32)


def dot_at(a, b):
    return lax.dot_general(a, b, (((0,), (0,)), ((), ())), preferred_element_type=F32)


def split3(x):
    hi = x.astype(BF16)
    rest = x - hi.astype(F32)
    mid = rest.astype(BF16)
    low = (rest - mid.astype(F32)).astype(BF16)
    return hi, mid, low


def length_of(kind):
    return jnp.where(kind == 0, BASE, jnp.where(kind == 1, CROP_B, CROP_C)).astype(jnp.int32)


def pick(ref, layer):
    row = ref[0:1].astype(F32)
    for index in range(1, ref.shape[0]):
        row = jnp.where(layer == index, ref[index : index + 1].astype(F32), row)
    return row


def norm(x):
    width = x.shape[-1]
    mean = jnp.sum(x, -1, keepdims=True) * (1.0 / width)
    centered = x - mean
    var = jnp.sum(centered * centered, -1, keepdims=True) * (1.0 / width)
    rstd = lax.rsqrt(var + EPS)
    return centered * rstd, rstd


def norm_back(dc, xhat, rstd, gain):
    width = dc.shape[-1]
    dxh = dc * gain
    m1 = jnp.sum(dxh, -1, keepdims=True) * (1.0 / width)
    m2 = jnp.sum(dxh * xhat, -1, keepdims=True) * (1.0 / width)
    return rstd * (dxh - m1 - xhat * m2)


def gelu_parts(x):
    d = 1.0 + (ERF_P * 0.5**0.5) * jnp.abs(x)
    r = pl.reciprocal(d, approx=True)
    t = r * (2.0 - d * r)
    e = jnp.exp(x * x * -0.5)
    q = ERF_C[5]
    for k in (4, 3, 2, 1, 0):
        q = q * t + ERF_C[k]
    q = q * t * e
    phi = jnp.where(x > 0, 1.0 - q, q)
    return x * phi, phi + x * e * 0.3989422804014327


def fwd_kernel(
    kinds, tok, interp, pos, gain, bias, w_qkv, qvb, w_out, outb, w1, b1, w2, b2,
    mixed, a_o, qkv_o, lse_o, o_o, c_o, gp_o, gh_o, xh1_o, r1_o, xh2_o, r2_o,
    x_s, table_s, mid_s, o_s,
):
    block, layer = pl.program_id(0), pl.program_id(1)
    images, rows, width = tok.shape
    padded = x_s.shape[1]
    flat = images * padded
    heads_pair = 2 * HEAD

    @pl.when((block == 0) & (layer == 0))
    def _():
        for kind in range(interp.shape[0]):
            total = jnp.zeros((rows, width), F32)
            for part in split3(interp[kind])[::-1]:
                total += dot(part, pos[...])
            table_s[kind, 0:rows, :] = total

    @pl.when(layer == 0)
    def _():
        for i in range(images):
            kind = kinds[block * images + i]
            here = lax.broadcasted_iota(jnp.int32, (rows, 1), 0) < length_of(kind)
            h0 = tok[i].astype(F32) + table_s[kind, 0:rows, :]
            x_s[i] = jnp.zeros((padded, width), F32)
            x_s[i, 0:rows, :] = jnp.where(here, h0, 0.0)

    x = x_s[...].reshape(flat, width)
    xhat, rstd = norm(x)
    a = (xhat * gain[0, 0:1].astype(F32) + bias[0, 0:1].astype(F32)).astype(BF16)
    a_o[0] = a
    xh1_o[0] = xhat.astype(BF16)
    r1_o[0] = rstd
    for part in range(3):
        cols = slice(part * width, (part + 1) * width)
        part_out = dot(a, w_qkv[0, :, cols])
        if part != 1:
            part_out += qvb[0, part // 2 : part // 2 + 1].astype(F32)
        qkv_o[0, :, cols] = part_out.astype(BF16)
    lane = lax.broadcasted_iota(jnp.int32, (1, heads_pair), 1)
    low_lanes = lane < HEAD
    for i in range(images):
        r0 = i * padded
        length = length_of(kinds[block * images + i])
        key_ok = lax.broadcasted_iota(jnp.int32, (padded, 1), 0) < length
        for pair in range(HEADS // 2):
            c0 = pair * heads_pair
            q2 = qkv_o[0, r0 : r0 + padded, c0 : c0 + heads_pair]
            k2 = qkv_o[0, r0 : r0 + padded, width + c0 : width + c0 + heads_pair]
            v2 = qkv_o[0, r0 : r0 + padded, 2 * width + c0 : 2 * width + c0 + heads_pair]
            outs = []
            for sub in range(2):
                mine = low_lanes if sub == 0 else jnp.logical_not(low_lanes)
                km = k2 * jnp.where(mine, HEAD**-0.5, 0.0).astype(BF16)
                s = jnp.where(key_ok, dot_bt(km, q2), -1e9)
                top = jnp.max(s, 0, keepdims=True)
                e = jnp.exp(s - top)
                total = jnp.sum(e, 0, keepdims=True)
                head = 2 * pair + sub
                lse_o[0, i, head : head + 1, :] = top + jnp.log(total)
                p = (e * (1.0 / total)).astype(BF16)
                outs.append(dot_at(p, v2))
            o_s[r0 : r0 + padded, c0 : c0 + heads_pair] = jnp.where(low_lanes, outs[0], outs[1]).astype(BF16)
    o = o_s[...]
    o_o[0] = o
    mid = x_s[...].reshape(flat, width) + dot(o, w_out[0]) + pick(outb, layer)
    mid_s[...] = mid
    xhat, rstd = norm(mid)
    c = (xhat * gain[0, 1:2].astype(F32) + bias[0, 1:2].astype(F32)).astype(BF16)
    c_o[0] = c
    xh2_o[0] = xhat.astype(BF16)
    r2_o[0] = rstd
    hidden = w1.shape[2]
    bias1 = pick(b1, layer)
    step = width
    total = mid_s[...] + pick(b2, layer)
    for f in range(0, hidden, step):
        pre = dot(c, w1[0, :, f : f + step]) + bias1[:, f : f + step]
        gh, gp = gelu_parts(pre)
        gh = gh.astype(BF16)
        gh_o[0, :, f : f + step] = gh
        gp_o[0, :, f : f + step] = gp.astype(BF16)
        total += dot(gh, w2[0, f : f + step, :])
    x_s[...] = total.reshape(images, padded, width)

    @pl.when(layer == pl.num_programs(1) - 1)
    def _():
        for i in range(images):
            kind = kinds[block * images + i]
            here = lax.broadcasted_iota(jnp.int32, (rows, 1), 0) < length_of(kind)
            mixed[i] = jnp.where(here, x_s[i, 0:rows, :], 0.0).astype(BF16)


def forward(kinds, tokens, interp, pos_base, ln_gain, ln_bias, w_qkv, qv_bias, w_out, out_bias, w_fc1, fc1_bias, w_fc2, fc2_bias, padded, per):
    count, rows, width = tokens.shape
    layers, _, hidden = w_fc1.shape
    blocks = count // per
    flat = per * padded
    whole = lambda shape: pl.BlockSpec(shape, lambda b, l, k: (0,) * len(shape))
    by_layer = lambda shape: pl.BlockSpec((1,) + shape, lambda b, l, k: (l,) + (0,) * len(shape))
    by_image = lambda: pl.BlockSpec((per, rows, width), lambda b, l, k: (b, 0, 0))
    saved = lambda feat: pl.BlockSpec((1, flat, feat), lambda b, l, k: (l, b, 0))
    shape = lambda feat, dtype: jax.ShapeDtypeStruct((layers, count * padded, feat), dtype)
    return pl.pallas_call(
        fwd_kernel,
        grid_spec=pltpu.PrefetchScalarGridSpec(
            num_scalar_prefetch=1,
            grid=(blocks, layers),
            in_specs=[
                by_image(),
                whole(interp.shape),
                whole(pos_base.shape),
                by_layer((2, width)),
                by_layer((2, width)),
                by_layer((width, 3 * width)),
                by_layer((2, width)),
                by_layer((width, width)),
                whole(out_bias.shape),
                by_layer((width, hidden)),
                whole(fc1_bias.shape),
                by_layer((hidden, width)),
                whole(fc2_bias.shape),
            ],
            out_specs=[
                by_image(),
                saved(width),
                saved(3 * width),
                pl.BlockSpec((1, per, 8, padded), lambda b, l, k: (l, b, 0, 0)),
                saved(width),
                saved(width),
                saved(hidden),
                saved(hidden),
                saved(width),
                saved(1),
                saved(width),
                saved(1),
            ],
            scratch_shapes=[
                pltpu.VMEM((per, padded, width), F32),
                pltpu.VMEM((3, padded, width), F32),
                pltpu.VMEM((flat, width), F32),
                pltpu.VMEM((flat, width), BF16),
            ],
        ),
        out_shape=[
            jax.ShapeDtypeStruct(tokens.shape, BF16),
            shape(width, BF16),
            shape(3 * width, BF16),
            jax.ShapeDtypeStruct((layers, count, 8, padded), F32),
            shape(width, BF16),
            shape(width, BF16),
            shape(hidden, BF16),
            shape(hidden, BF16),
            shape(width, BF16),
            shape(1, F32),
            shape(width, BF16),
            shape(1, F32),
        ],
        compiler_params=pltpu.CompilerParams(vmem_limit_bytes=VMEM_LIMIT),
        name="encoder_forward",
    )(kinds, tokens, interp, pos_base, ln_gain, ln_bias, w_qkv, qv_bias, w_out, out_bias, w_fc1, fc1_bias, w_fc2, fc2_bias)


PIECES = 32
GROUP = 8


def xor(value, index):
    return lax.bitwise_xor(value, jnp.int32(index))


def copy_all(copies):
    for item in copies:
        item.start()
    for item in copies:
        item.wait()


def mlp_back_kernel(
    top, kinds, me, dx_ref, c, gh, gp, xh, rstd, gain, w1, w2,
    dmid, keep1, send1, keep2, send2, sums, dx_s, gw1, gw2, sems,
):
    block = pl.program_id(0)

    @pl.when(block == 0)
    def _():
        gw1[...] = jnp.zeros_like(gw1)
        gw2[...] = jnp.zeros_like(gw2)
        sums[...] = jnp.zeros_like(sums)

    if top:
        images, rows, width = dx_ref.shape
        padded = dx_s.shape[1]
        for i in range(images):
            kind = kinds[block * images + i]
            here = lax.broadcasted_iota(jnp.int32, (rows, 1), 0) < length_of(kind)
            dx_s[i] = jnp.zeros((padded, width), F32)
            dx_s[i, 0:rows, :] = jnp.where(here, dx_ref[i].astype(F32), 0.0)
        dx = dx_s[...].reshape(images * padded, width)
    else:
        dx = dx_ref[...]
    flat, width = dx.shape
    hidden = w1.shape[2]
    dz = dx.astype(BF16)
    sums[11:12, :] += jnp.sum(dz.astype(F32), 0, keepdims=True)
    dc = jnp.zeros((flat, width), F32)
    for index in range(hidden // width):
        cols = slice(index * width, (index + 1) * width)
        dgh = dot_bt(dz, w2[0, cols, :])
        dpre = (dgh * gp[0, :, cols].astype(F32)).astype(BF16)
        sums[7 + index : 8 + index, :] += jnp.sum(dpre.astype(F32), 0, keepdims=True)
        gw1[index] += dot_at(c[0], dpre)
        gw2[cols, :] += dot_at(gh[0, :, cols], dz)
        dc += dot_bt(dpre, w1[0, :, cols])
    xhat = xh[0].astype(F32)
    sums[1:2, :] += jnp.sum(dc * xhat, 0, keepdims=True)
    sums[3:4, :] += jnp.sum(dc, 0, keepdims=True)
    dmid[...] = dx + norm_back(dc, xhat, rstd[0], gain[0, 1:2].astype(F32))

    @pl.when(block == pl.num_programs(0) - 1)
    def _():
        piece = hidden // PIECES
        half = PIECES // 2
        copies = []
        for r in range(PIECES):
            first, second = xor(me[0], r), xor(me[1], r)
            out1, out2 = (keep1, keep2) if r < half else (send1, send2)
            row = pl.multiple_of(lax.bitwise_and(first, GROUP - 1) * piece, 8)
            col = lax.shift_right_logical(first, 3)
            copies.append(pltpu.make_async_copy(gw1.at[col, pl.ds(row, piece)], out1.at[r % half], sems.at[2 * r]))
            row = pl.multiple_of(second * piece, 8)
            copies.append(pltpu.make_async_copy(gw2.at[pl.ds(row, piece)], out2.at[r % half], sems.at[2 * r + 1]))
        copy_all(copies)


def halves(piece, width):
    return [jax.ShapeDtypeStruct((PIECES // 2, piece, width), F32)] * 2


def drop(kernel, fixed, first, count):
    def body(*refs):
        return kernel(*fixed, *refs[:first], *refs[first + count :])

    return body


def mlp_back(layer, top, kinds, me, dx, c, gh, gp, xh, rstd, gain, w1, w2, padded, per, after):
    layers, width, hidden = w1.shape
    total = c.shape[1]
    flat = per * padded
    blocks = total // flat
    saved = lambda feat: pl.BlockSpec((1, flat, feat), lambda b, k, m: (layer, b, 0))
    param = lambda *shape: pl.BlockSpec((1,) + shape, lambda b, k, m: (layer, 0, 0))
    if top:
        dx_spec = pl.BlockSpec((per,) + dx.shape[1:], lambda b, k, m: (b, 0, 0))
    else:
        dx_spec = pl.BlockSpec((flat, width), lambda b, k, m: (b, 0))
    anywhere = pl.BlockSpec(memory_space=pl.ANY)
    return pl.pallas_call(
        drop(mlp_back_kernel, (top,), 11, len(after)),
        grid_spec=pltpu.PrefetchScalarGridSpec(
            num_scalar_prefetch=2,
            grid=(blocks,),
            in_specs=[
                dx_spec,
                saved(width),
                saved(hidden),
                saved(hidden),
                saved(width),
                saved(1),
                param(2, width),
                param(width, hidden),
                param(hidden, width),
            ]
            + [anywhere] * len(after),
            out_specs=[
                pl.BlockSpec((flat, width), lambda b, k, m: (b, 0)),
                anywhere,
                anywhere,
                anywhere,
                anywhere,
                pl.BlockSpec((16, width), lambda b, k, m: (0, 0)),
            ],
            scratch_shapes=[
                pltpu.VMEM((per, padded, width), F32),
                pltpu.VMEM((hidden // width, width, width), F32),
                pltpu.VMEM((hidden, width), F32),
                pltpu.SemaphoreType.DMA((2 * PIECES,)),
            ],
        ),
        out_shape=[jax.ShapeDtypeStruct((total, width), F32)]
        + halves(hidden // PIECES, width)
        + halves(hidden // PIECES, width)
        + [jax.ShapeDtypeStruct((16, width), F32)],
        compiler_params=pltpu.CompilerParams(vmem_limit_bytes=VMEM_LIMIT),
        cost_estimate=pl.CostEstimate(flops=8 * total * width * hidden, bytes_accessed=30 * total * width, transcendentals=0),
        name="mlp_backward",
    )(kinds, me, dx, c, gh, gp, xh, rstd, gain, w1, w2, *after)


def attn_back_kernel(bottom, layers, kinds, me, dmid, o, qkv, lse, a, xh, rstd, gain, w_qkv, w_out, *rest):
    if bottom:
        interp, dx_ref, keep1, send1, keep2, send2, dqkv_s, do_s, gw, sems, sums, kind_s, misc = rest[:1] + rest[2 * layers :]
        others = rest[1 : 2 * layers]
    else:
        dx_ref, keep1, send1, keep2, send2, sums, dqkv_s, do_s, gw, sems = rest
    block = pl.program_id(0)
    images = lse.shape[1]
    flat, width = dmid.shape
    padded = flat // images

    @pl.when(block == 0)
    def _():
        gw[...] = jnp.zeros_like(gw)
        sums[...] = jnp.zeros_like(sums)
        if bottom:
            kind_s[...] = jnp.zeros_like(kind_s)

    dy = dmid[...].astype(BF16)
    sums[6:7, :] += jnp.sum(dy.astype(F32), 0, keepdims=True)
    do_s[...] = dot_bt(dy, w_out[0]).astype(BF16)
    gw[3] += dot_at(o[0], dy)
    pair_width = 2 * HEAD
    low_lanes = lax.broadcasted_iota(jnp.int32, (1, pair_width), 1) < HEAD
    scale = HEAD**-0.5
    for i in range(images):
        rows = slice(i * padded, (i + 1) * padded)
        length = length_of(kinds[block * images + i])
        key_ok = lax.broadcasted_iota(jnp.int32, (padded, 1), 0) < length
        for pair in range(HEADS // 2):
            c0 = pair * pair_width
            part = lambda base: slice(base + c0, base + c0 + pair_width)
            q2, k2, v2 = qkv[0, rows, part(0)], qkv[0, rows, part(width)], qkv[0, rows, part(2 * width)]
            do2 = do_s[rows, part(0)]
            dq, dk, dv = [], [], []
            for sub in range(2):
                mine = low_lanes if sub == 0 else jnp.logical_not(low_lanes)
                head = 2 * pair + sub
                km = k2 * jnp.where(mine, scale, 0.0).astype(BF16)
                vm = v2 * jnp.where(mine, 1.0, 0.0).astype(BF16)
                s = jnp.where(key_ok, dot_bt(km, q2), -1e9)
                p = jnp.exp(s - lse[0, i, head : head + 1, :])
                dp = dot_bt(vm, do2)
                delta = jnp.sum(dp * p, 0, keepdims=True)
                ds = (p * (dp - delta)).astype(BF16)
                dv.append(dot(p.astype(BF16), do2))
                dk.append(dot(ds, q2))
                dq.append(dot_at(ds, k2))
            dqkv_s[rows, part(0)] = (jnp.where(low_lanes, dq[0], dq[1]) * scale).astype(BF16)
            dqkv_s[rows, part(width)] = (jnp.where(low_lanes, dk[0], dk[1]) * scale).astype(BF16)
            dqkv_s[rows, part(2 * width)] = jnp.where(low_lanes, dv[0], dv[1]).astype(BF16)
    da = jnp.zeros((flat, width), F32)
    for index in range(3):
        cols = slice(index * width, (index + 1) * width)
        d = dqkv_s[:, cols]
        if index != 1:
            row = 4 + index // 2
            sums[row : row + 1, :] += jnp.sum(d.astype(F32), 0, keepdims=True)
        gw[index] += dot_at(a[0], d)
        da += dot_bt(d, w_qkv[0, :, cols])
    xhat = xh[0].astype(F32)
    sums[0:1, :] += jnp.sum(da * xhat, 0, keepdims=True)
    sums[2:3, :] += jnp.sum(da, 0, keepdims=True)
    dx = dmid[...] + norm_back(da, xhat, rstd[0], gain[0, 0:1].astype(F32))
    if bottom:
        real = dx_ref.shape[1]
        for i in range(images):
            kind = kinds[block * images + i]
            here = lax.broadcasted_iota(jnp.int32, (padded, 1), 0) < length_of(kind)
            mine = jnp.where(here, dx[i * padded : (i + 1) * padded], 0.0)
            dx_ref[i] = mine[0:real]
            kind_s[kind] += mine
    else:
        dx_ref[...] = dx

    @pl.when(block == pl.num_programs(0) - 1)
    def _():
        half = PIECES // 2
        piece = gw.shape[0] * width // PIECES
        part = piece // 2
        copies = []
        for r in range(PIECES):
            for which, out in ((0, keep1 if r < half else send1), (1, keep2 if r < half else send2)):
                j = xor(me[which], r)
                row = pl.multiple_of(lax.bitwise_and(j, GROUP - 1) * piece + which * part, 8)
                col = lax.shift_right_logical(j, 3)
                copies.append(
                    pltpu.make_async_copy(
                        gw.at[col, pl.ds(row, part)], out.at[r % half, pl.ds(0, part)], sems.at[2 * r + which]
                    )
                )
        for item in copies:
            item.start()
        if bottom:
            total = jnp.zeros((real, width), F32)
            for kind in range(interp.shape[0]):
                hi, mid, _ = split3(interp[kind])
                ghi, gmid, _ = split3(kind_s[kind, 0:real, :])
                total += dot_at(mid, ghi) + dot_at(hi, gmid) + dot_at(hi, ghi)
            misc[...] = jnp.zeros_like(misc)
            misc[0:real, :] = total
            misc[200:216, :] = sums[...] + others[0][...]
            for layer in range(1, layers):
                misc[200 + 16 * layer : 216 + 16 * layer, :] = others[2 * layer - 1][...] + others[2 * layer][...]
            tail = misc.shape[0] // PIECES
            more = []
            for r in range(PIECES):
                j = xor(me[1], r)
                more.append(
                    pltpu.make_async_copy(
                        misc.at[pl.ds(pl.multiple_of(j * tail, 8), tail)],
                        (keep2 if r < half else send2).at[r % half, pl.ds(part, tail)],
                        sems.at[2 * PIECES + r],
                    )
                )
            copy_all(more)
        for item in copies:
            item.wait()


MISC_ROWS = 256


def attn_back(layer, bottom, kinds, me, dmid, o, qkv, lse, a, xh, rstd, gain, w_qkv, w_out, interp, like, others, padded, per, after):
    width = dmid.shape[1]
    total = dmid.shape[0]
    layers = w_qkv.shape[0]
    flat = per * padded
    blocks = total // flat
    saved = lambda feat: pl.BlockSpec((1, flat, feat), lambda b, k, m: (layer, b, 0))
    param = lambda *shape: pl.BlockSpec((1,) + shape, lambda b, k, m: (layer, 0, 0))
    fixed = lambda *shape: pl.BlockSpec(shape, lambda b, k, m: (0,) * len(shape))
    anywhere = pl.BlockSpec(memory_space=pl.ANY)
    in_specs = [
        pl.BlockSpec((flat, width), lambda b, k, m: (b, 0)),
        saved(width),
        saved(3 * width),
        pl.BlockSpec((1, per, 8, padded), lambda b, k, m: (layer, b, 0, 0)),
        saved(width),
        saved(width),
        saved(1),
        param(2, width),
        param(width, 3 * width),
        param(width, width),
    ]
    part = 4 * width // PIECES // 2
    tail = MISC_ROWS // PIECES if bottom else 0
    grads = halves(part, width) + halves(part + tail, width)
    grads_specs = [anywhere] * 4
    scratch = [
        pltpu.VMEM((flat, 3 * width), BF16),
        pltpu.VMEM((flat, width), BF16),
        pltpu.VMEM((4, width, width), F32),
        pltpu.SemaphoreType.DMA(((3 if bottom else 2) * PIECES,)),
    ]
    args = [kinds, me, dmid, o, qkv, lse, a, xh, rstd, gain, w_qkv, w_out]
    if bottom:
        rows = like.shape[1]
        in_specs += [fixed(*interp.shape)] + [fixed(16, width)] * len(others)
        args += [interp] + others
        out_specs = [pl.BlockSpec((per, rows, width), lambda b, k, m: (b, 0, 0))] + grads_specs
        out_shape = [jax.ShapeDtypeStruct(like.shape, F32)] + grads
        scratch += [pltpu.VMEM((16, width), F32), pltpu.VMEM((3, padded, width), F32), pltpu.VMEM((MISC_ROWS, width), F32)]
    else:
        out_specs = [pl.BlockSpec((flat, width), lambda b, k, m: (b, 0))] + grads_specs + [fixed(16, width)]
        out_shape = [jax.ShapeDtypeStruct((total, width), F32)] + grads + [jax.ShapeDtypeStruct((16, width), F32)]
    first = len(args)
    in_specs += [anywhere] * len(after)
    args += after
    return pl.pallas_call(
        drop(attn_back_kernel, (bottom, layers), first, len(after)),
        grid_spec=pltpu.PrefetchScalarGridSpec(
            num_scalar_prefetch=2,
            grid=(blocks,),
            in_specs=in_specs,
            out_specs=out_specs,
            scratch_shapes=scratch,
        ),
        out_shape=out_shape,
        compiler_params=pltpu.CompilerParams(vmem_limit_bytes=VMEM_LIMIT),
        cost_estimate=pl.CostEstimate(flops=32 * total * width * width, bytes_accessed=30 * total * width, transcendentals=0),
        name="attention_backward",
    )(*args)


def exchange(x, axis, bits, size):
    return lax.ppermute(x, axis, [(i, i ^ bits) for i in range(size)])


class Round:
    def __init__(self, streams, sizes):
        self.streams, self.sizes, self.stage = streams, sizes, 0

    def swap(self, x, axis, bits):
        return exchange(x, axis, bits, self.sizes[axis])

    def advance(self):
        stage = self.stage
        self.stage += 1
        if stage == 0:
            self.keep = [stream[0] for stream in self.streams]
            sent = [stream[1] for stream in self.streams]
            self.got = [self.swap(x, "grp", 1) for x in sent]
        elif stage <= 2:
            half = self.keep[0].shape[0] // 2
            sent = [keep[half:] + got[half:] for keep, got in zip(self.keep, self.got)]
            self.keep = [keep[:half] + got[:half] for keep, got in zip(self.keep, self.got)]
            self.got = [self.swap(x, "grp", stream[1 + stage]) for x, stream in zip(sent, self.streams)]
        elif stage == 3:
            joined = jnp.concatenate([keep + got for keep, got in zip(self.keep, self.got)], 1)
            self.keep = joined[0]
            sent = [joined[k] for k in range(1, 4)]
            self.got = [self.swap(x, "dp", k + 1) for k, x in enumerate(sent)]
        elif stage == 4:
            total = self.keep + self.got[0] + self.got[1] + self.got[2]
            for axis, bit in (("grp", 8), ("dp", 4)):
                while bit < self.sizes[axis]:
                    total = total + self.swap(total, axis, bit)
                    bit *= 2
            sent = [total]
            self.keep = total
            self.got = [self.swap(total, "dp", k) for k in range(1, 4)]
        elif stage == 5:
            every = jnp.stack([self.keep] + self.got)
            start, sent = 0, []
            for stream in self.streams:
                rows = stream[0].shape[1]
                sent.append(every[:, start : start + rows])
                start += rows
            self.keep = sent
            self.got = [self.swap(x, "grp", stream[3]) for x, stream in zip(sent, self.streams)]
        elif stage == 6:
            sent = [jnp.concatenate([keep, got]) for keep, got in zip(self.keep, self.got)]
            self.keep = sent
            self.got = [self.swap(x, "grp", stream[2]) for x, stream in zip(sent, self.streams)]
        else:
            self.keep = [[keep, got] for keep, got in zip(self.keep, self.got)]
            sent = sum(self.keep, [])
            self.got = [[self.swap(x, "grp", 1) for x in pair] for pair in self.keep]
        return sent

    def finish(self):
        while self.stage < 8:
            self.advance()
        return [keep + got for keep, got in zip(self.keep, self.got)]


def place_mlp_kernel(layer, me, *refs):
    alphas, betas = refs[0:4], refs[4:8]
    out1, out2, sems = refs[-3:]
    piece = alphas[0].shape[1]
    width = alphas[0].shape[2]
    copies = []
    for r in range(PIECES):
        j = xor(me[0], r)
        row = pl.multiple_of(lax.bitwise_and(j, GROUP - 1) * piece, 8)
        col = pl.multiple_of(lax.shift_right_logical(j, 3) * width, 128)
        copies.append(
            pltpu.make_async_copy(
                alphas[r // GROUP].at[r % GROUP], out1.at[layer, pl.ds(row, piece), pl.ds(col, width)], sems.at[2 * r]
            )
        )
        j = xor(me[1], r)
        row = pl.multiple_of(j * piece, 8)
        copies.append(
            pltpu.make_async_copy(betas[r // GROUP].at[r % GROUP], out2.at[layer, pl.ds(row, piece)], sems.at[2 * r + 1])
        )
    copy_all(copies)


def place_mlp(layer, me, pieces, before, shapes):
    anywhere = pl.BlockSpec(memory_space=pl.ANY)
    args = [me] + pieces[0] + pieces[1] + list(before)
    return pl.pallas_call(
        partial(place_mlp_kernel, layer),
        grid_spec=pltpu.PrefetchScalarGridSpec(
            num_scalar_prefetch=1,
            grid=(1,),
            in_specs=[pl.BlockSpec(x.shape, lambda b, m: (0, 0, 0)) for x in args[1:9]] + [anywhere] * len(before),
            out_specs=[anywhere] * 2,
            scratch_shapes=[pltpu.SemaphoreType.DMA((2 * PIECES,))],
        ),
        out_shape=[jax.ShapeDtypeStruct(shape, F32) for shape in shapes],
        input_output_aliases={9: 0, 10: 1} if before else {},
        compiler_params=pltpu.CompilerParams(vmem_limit_bytes=VMEM_LIMIT),
        name="place_mlp",
    )(*args)


def place_attn_kernel(layer, layers, last, me, *refs):
    alphas, betas = refs[0:4], refs[4:8]
    if last:
        gqkv, gout, gpos, ggain, gbias, gqvb, goutb, gb1, gb2, sems, misc, tail_sems = refs[-12:]
    else:
        gqkv, gout, sems = refs[-3:]
    part = alphas[0].shape[1]
    width = alphas[0].shape[2]
    waits = []
    tails = []
    for r in range(PIECES):
        for which, group in ((0, alphas), (1, betas)):
            j = xor(me[which], r)
            row = pl.multiple_of(lax.bitwise_and(j, GROUP - 1) * 2 * part + which * part, 8)
            col = lax.shift_right_logical(j, 3)
            source = group[r // GROUP].at[r % GROUP, pl.ds(0, part)]
            sem = sems.at[2 * r + which]

            @pl.when(col < 3)
            def _():
                wide = pl.multiple_of(col * width, 128)
                pltpu.make_async_copy(source, gqkv.at[layer, pl.ds(row, part), pl.ds(wide, width)], sem).start()

            @pl.when(col == 3)
            def _():
                pltpu.make_async_copy(source, gout.at[layer, pl.ds(row, part)], sem).start()

            waits.append(pltpu.make_async_copy(source, gout.at[layer, pl.ds(row, part)], sem))
        if last:
            tail = misc.shape[0] // PIECES
            j = xor(me[1], r)
            item = pltpu.make_async_copy(
                betas[r // GROUP].at[r % GROUP, pl.ds(part, tail)],
                misc.at[pl.ds(pl.multiple_of(j * tail, 8), tail)],
                tail_sems.at[r],
            )
            item.start()
            tails.append(item)
    if last:
        for item in tails:
            item.wait()
        gpos[...] = misc[0 : gpos.shape[0], :]
        for index in range(layers):
            base = 200 + 16 * index
            ggain[index] = misc[base : base + 2, :]
            gbias[index] = misc[base + 2 : base + 4, :]
            gqvb[index] = misc[base + 4 : base + 6, :]
            goutb[index : index + 1, :] = misc[base + 6 : base + 7, :]
            for k in range(gb1.shape[1] // width):
                gb1[index : index + 1, k * width : (k + 1) * width] = misc[base + 7 + k : base + 8 + k, :]
            gb2[index : index + 1, :] = misc[base + 11 : base + 12, :]
    for item in waits:
        item.wait()


def place_attn(layer, layers, me, pieces, before, shapes, small):
    anywhere = pl.BlockSpec(memory_space=pl.ANY)
    args = [me] + pieces[0] + pieces[1] + list(before)
    last = bool(small)
    scratch = [pltpu.SemaphoreType.DMA((2 * PIECES,))]
    if last:
        scratch += [pltpu.VMEM((MISC_ROWS, shapes[1][-1]), F32), pltpu.SemaphoreType.DMA((PIECES,))]
    return pl.pallas_call(
        partial(place_attn_kernel, layer, layers, last),
        grid_spec=pltpu.PrefetchScalarGridSpec(
            num_scalar_prefetch=1,
            grid=(1,),
            in_specs=[pl.BlockSpec(x.shape, lambda b, m: (0, 0, 0)) for x in args[1:9]] + [anywhere] * len(before),
            out_specs=[anywhere] * 2 + [pl.BlockSpec(s, lambda b, m, n=len(s): (0,) * n) for s in small],
            scratch_shapes=scratch,
        ),
        out_shape=[jax.ShapeDtypeStruct(shape, F32) for shape in list(shapes) + list(small)],
        input_output_aliases={9: 0, 10: 1} if before else {},
        compiler_params=pltpu.CompilerParams(vmem_limit_bytes=VMEM_LIMIT),
        name="place_attention",
    )(*args)


def on_device(sizes, tokens, kinds, interp, pos_base, ln_gain, ln_bias, w_qkv, qv_bias, w_out, out_bias, w_fc1, fc1_bias, w_fc2, fc2_bias, cotangent):
    count, rows, width = tokens.shape
    layers = w_qkv.shape[0]
    padded = -(-rows // 16) * 16
    per = 2 if count % 2 == 0 else 1
    g, d = lax.axis_index("grp"), lax.axis_index("dp")
    bit = lambda value, index: lax.bitwise_and(lax.shift_right_logical(value, index), 1)
    low = lax.bitwise_and(d, 3)
    me = jnp.stack(
        [
            bit(g, 0) * 16 + bit(g, 1) * 8 + bit(g, 2) * 4 + low,
            bit(g, 0) * 16 + bit(g, 2) * 8 + bit(g, 1) * 4 + low,
        ]
    ).astype(jnp.int32)
    mixed, a, qkv, lse, o, c, gp, gh, xh1, r1, xh2, r2 = forward(
        kinds, tokens, interp, pos_base, ln_gain, ln_bias, w_qkv, qv_bias, w_out, out_bias, w_fc1, fc1_bias, w_fc2, fc2_bias, padded, per
    )
    args = (kinds, me)
    small = (pos_base.shape, ln_gain.shape, ln_bias.shape, qv_bias.shape, out_bias.shape, fc1_bias.shape, fc2_bias.shape)
    dx, after, sums, rounds = cotangent, [], [], {}
    for layer in reversed(range(layers)):
        dmid, keep1, send1, keep2, send2, mlp_sums = mlp_back(
            layer, layer == layers - 1, *args, dx, c, gh, gp, xh2, r2, ln_gain, w_fc1, w_fc2, padded, per, after
        )
        after = sum([item.advance() for item in rounds.values()], [])
        item = rounds["mlp", layer] = Round(((keep1, send1, 2, 4), (keep2, send2, 4, 2)), sizes)
        item.advance()
        after += item.advance()
        out = attn_back(
            layer, layer == 0, *args, dmid, o, qkv, lse, a, xh1, r1, ln_gain, w_qkv, w_out, interp, tokens, [mlp_sums] + sums, padded, per, after
        )
        dx, keep1, send1, keep2, send2 = out[:5]
        after = sum([item.advance() for item in rounds.values()], [])
        item = rounds["attn", layer] = Round(((keep1, send1, 2, 4), (keep2, send2, 4, 2)), sizes)
        item.advance()
        after += item.advance()
        sums = [mlp_sums] + list(out[5:]) + sums
    while any(item.stage < 8 for item in rounds.values()):
        for item in rounds.values():
            if item.stage < 8:
                item.advance()
    mlp_out, attn_out = (), ()
    for layer in reversed(range(layers)):
        mlp_out = place_mlp(layer, me, rounds["mlp", layer].finish(), mlp_out, (w_fc1.shape, w_fc2.shape))
        attn_out = place_attn(
            layer, layers, me, rounds["attn", layer].finish(), attn_out[:2], (w_qkv.shape, w_out.shape), () if layer else small
        )
    gqkv, gout, gpos, ggain, gbias, gqvb, goutb, gb1, gb2 = attn_out
    return mixed, dx, gpos, ggain, gbias, gqkv, gqvb, gout, goutb, mlp_out[0], gb1, mlp_out[1], gb2


def solution(mesh):
    split = P(("grp", "dp"), None, None)
    return jax.shard_map(
        partial(on_device, dict(mesh.shape)),
        mesh=mesh,
        in_specs=(split, P(("grp", "dp"))) + (P(),) * 12 + (split,),
        out_specs=(split, split) + (P(),) * 11,
        check_vma=False,
    )
```

```python
from functools import partial

import jax
import jax.numpy as jnp
from jax import lax
from jax.experimental import pallas as pl
from jax.experimental.pallas import tpu as pltpu
from jax.sharding import PartitionSpec as P

HEADS = 6
HEAD = 64
BASE = 197
CROP_B = 181
CROP_C = 193
EPS = 1e-06
F32 = jnp.float32
BF16 = jnp.bfloat16
VMEM_LIMIT = 60 * 1024 * 1024

ERF_P = 0.39
ERF_C = (0.11766263, 0.04569411, 0.32477995, -0.31770045, 0.44333237, -0.11376861)


def dot(a, b):
    return lax.dot_general(a, b, (((1,), (0,)), ((), ())), preferred_element_type=F32)


def dot_bt(a, b):
    return lax.dot_general(a, b, (((1,), (1,)), ((), ())), preferred_element_type=F32)


def dot_at(a, b):
    return lax.dot_general(a, b, (((0,), (0,)), ((), ())), preferred_element_type=F32)


def split3(x):
    hi = x.astype(BF16)
    rest = x - hi.astype(F32)
    mid = rest.astype(BF16)
    low = (rest - mid.astype(F32)).astype(BF16)
    return hi, mid, low


def length_of(kind):
    return jnp.where(kind == 0, BASE, jnp.where(kind == 1, CROP_B, CROP_C)).astype(jnp.int32)


def pick(ref, layer):
    row = ref[0:1].astype(F32)
    for index in range(1, ref.shape[0]):
        row = jnp.where(layer == index, ref[index : index + 1].astype(F32), row)
    return row


def norm(x):
    width = x.shape[-1]
    mean = jnp.sum(x, -1, keepdims=True) * (1.0 / width)
    centered = x - mean
    var = jnp.sum(centered * centered, -1, keepdims=True) * (1.0 / width)
    rstd = lax.rsqrt(var + EPS)
    return centered * rstd, rstd


def norm_back(dc, xhat, rstd, gain):
    width = dc.shape[-1]
    dxh = dc * gain
    m1 = jnp.sum(dxh, -1, keepdims=True) * (1.0 / width)
    m2 = jnp.sum(dxh * xhat, -1, keepdims=True) * (1.0 / width)
    return rstd * (dxh - m1 - xhat * m2)


def gelu_parts(x):
    phi = 0.5 + 0.5 * lax.erf(x * 0.5**0.5)
    return x * phi, phi + x * (jnp.exp2(x * x * (-0.5 * 1.4426950408889634)) * 0.3989422804014327)


def head_masks():
    first = lax.broadcasted_iota(jnp.int32, (1, 2 * HEAD), 1) < HEAD
    plain = [jnp.where(first, 1.0, 0.0), jnp.where(first, 0.0, 1.0)]
    return [x.astype(BF16) for x in plain], [(x * HEAD**-0.5).astype(BF16) for x in plain]


def fwd_kernel(
    kinds, tok, interp, pos, gain, bias, w_qkv, qvb, w_out, outb, w1, b1, w2, b2,
    mixed, a_o, qkv_o, lse_o, o_o, c_o, gp_o, gh_o, xh1_o, r1_o, xh2_o, r2_o,
    x_all, table_s, mid_s, o_s,
):
    layer, block = pl.program_id(0), pl.program_id(1)
    x_s = x_all.at[block]
    images, rows, width = tok.shape
    padded = x_all.shape[2]
    flat = images * padded
    heads_pair = 2 * HEAD

    @pl.when((block == 0) & (layer == 0))
    def _():
        for kind in range(interp.shape[0]):
            total = jnp.zeros((rows, width), F32)
            for part in split3(interp[kind])[::-1]:
                total += dot(part, pos[...])
            table_s[kind, 0:rows, :] = total

    @pl.when(layer == 0)
    def _():
        for i in range(images):
            kind = kinds[block * images + i]
            here = lax.broadcasted_iota(jnp.int32, (rows, 1), 0) < length_of(kind)
            h0 = tok[i].astype(F32) + table_s[kind, 0:rows, :]
            x_s[i] = jnp.zeros((padded, width), F32)
            x_s[i, 0:rows, :] = jnp.where(here, h0, 0.0)

    x = x_s[...].reshape(flat, width)
    xhat, rstd = norm(x)
    a = (xhat * gain[0, 0:1].astype(F32) + bias[0, 0:1].astype(F32)).astype(BF16)
    a_o[0] = a
    xh1_o[0] = xhat.astype(BF16)
    r1_o[0] = rstd
    bias_row = qvb[0].astype(F32)
    bias_row = jnp.concatenate([bias_row[0:1], jnp.zeros((1, width), F32), bias_row[1:2]], 1)
    qkv_o[0] = (dot(a, w_qkv[0]) + bias_row).astype(BF16)
    plain, scaled = head_masks()
    for i in range(images):
        r0 = i * padded
        length = length_of(kinds[block * images + i])
        key_ok = lax.broadcasted_iota(jnp.int32, (1, padded, 1), 1) < length
        for pair in range(HEADS // 2):
            c0 = pair * heads_pair
            q2 = qkv_o[0, r0 : r0 + padded, c0 : c0 + heads_pair]
            k2 = qkv_o[0, r0 : r0 + padded, width + c0 : width + c0 + heads_pair]
            v2 = qkv_o[0, r0 : r0 + padded, 2 * width + c0 : 2 * width + c0 + heads_pair]
            ks = jnp.concatenate([k2 * keep for keep in scaled], 0)
            vs = jnp.concatenate([v2 * keep for keep in plain], 0)
            s = jnp.where(key_ok, dot_bt(ks, q2).reshape(2, padded, padded), -1e9)
            top = jnp.max(s, 1, keepdims=True)
            e = jnp.exp(s - top)
            total = jnp.sum(e, 1, keepdims=True)
            lse_o[0, i, 2 * pair : 2 * pair + 2, :] = (top + jnp.log(total)).reshape(2, padded)
            p = (e * (1.0 / total)).astype(BF16).reshape(2 * padded, padded)
            o_s[r0 : r0 + padded, c0 : c0 + heads_pair] = dot_at(p, vs).astype(BF16)
    o = o_s[...]
    o_o[0] = o
    mid = x_s[...].reshape(flat, width) + dot(o, w_out[0]) + pick(outb, layer)
    mid_s[...] = mid
    xhat, rstd = norm(mid)
    c = (xhat * gain[0, 1:2].astype(F32) + bias[0, 1:2].astype(F32)).astype(BF16)
    c_o[0] = c
    xh2_o[0] = xhat.astype(BF16)
    r2_o[0] = rstd
    hidden = w1.shape[2]
    bias1 = pick(b1, layer)
    step = 256
    total = mid_s[...] + pick(b2, layer)
    for f in range(0, hidden, step):
        pre = dot(c, w1[0, :, f : f + step]) + bias1[:, f : f + step]
        gh, gp = gelu_parts(pre)
        gh = gh.astype(BF16)
        gh_o[0, :, f : f + step] = gh
        gp_o[0, :, f : f + step] = gp.astype(BF16)
        total += dot(gh, w2[0, f : f + step, :])
    x_s[...] = total.reshape(images, padded, width)

    @pl.when(layer == pl.num_programs(0) - 1)
    def _():
        for i in range(images):
            kind = kinds[block * images + i]
            here = lax.broadcasted_iota(jnp.int32, (rows, 1), 0) < length_of(kind)
            mixed[i] = jnp.where(here, x_s[i, 0:rows, :], 0.0).astype(BF16)


def forward(kinds, tokens, interp, pos_base, ln_gain, ln_bias, w_qkv, qv_bias, w_out, out_bias, w_fc1, fc1_bias, w_fc2, fc2_bias, padded, per):
    count, rows, width = tokens.shape
    layers, _, hidden = w_fc1.shape
    blocks = count // per
    flat = per * padded
    whole = lambda shape: pl.BlockSpec(shape, lambda l, b, k: (0,) * len(shape))
    by_layer = lambda shape: pl.BlockSpec((1,) + shape, lambda l, b, k: (l,) + (0,) * len(shape))
    read_image = pl.BlockSpec((per, rows, width), lambda l, b, k: (jnp.where(l == 0, b, blocks - 1), 0, 0))
    write_image = pl.BlockSpec((per, rows, width), lambda l, b, k: (jnp.where(l == layers - 1, b, 0), 0, 0))
    saved = lambda feat: pl.BlockSpec((1, flat, feat), lambda l, b, k: (l, b, 0))
    shape = lambda feat, dtype: jax.ShapeDtypeStruct((layers, count * padded, feat), dtype)
    return pl.pallas_call(
        fwd_kernel,
        grid_spec=pltpu.PrefetchScalarGridSpec(
            num_scalar_prefetch=1,
            grid=(layers, blocks),
            in_specs=[
                read_image,
                whole(interp.shape),
                whole(pos_base.shape),
                by_layer((2, width)),
                by_layer((2, width)),
                by_layer((width, 3 * width)),
                by_layer((2, width)),
                by_layer((width, width)),
                whole(out_bias.shape),
                by_layer((width, hidden)),
                whole(fc1_bias.shape),
                by_layer((hidden, width)),
                whole(fc2_bias.shape),
            ],
            out_specs=[
                write_image,
                saved(width),
                saved(3 * width),
                pl.BlockSpec((1, per, 8, padded), lambda l, b, k: (l, b, 0, 0)),
                saved(width),
                saved(width),
                saved(hidden),
                saved(hidden),
                saved(width),
                saved(1),
                saved(width),
                saved(1),
            ],
            scratch_shapes=[
                pltpu.VMEM((blocks, per, padded, width), F32),
                pltpu.VMEM((3, padded, width), F32),
                pltpu.VMEM((flat, width), F32),
                pltpu.VMEM((flat, width), BF16),
            ],
        ),
        out_shape=[
            jax.ShapeDtypeStruct(tokens.shape, BF16),
            shape(width, BF16),
            shape(3 * width, BF16),
            jax.ShapeDtypeStruct((layers, count, 8, padded), F32),
            shape(width, BF16),
            shape(width, BF16),
            shape(hidden, BF16),
            shape(hidden, BF16),
            shape(width, BF16),
            shape(1, F32),
            shape(width, BF16),
            shape(1, F32),
        ],
        compiler_params=pltpu.CompilerParams(vmem_limit_bytes=VMEM_LIMIT),
        name="encoder_forward",
    )(kinds, tokens, interp, pos_base, ln_gain, ln_bias, w_qkv, qv_bias, w_out, out_bias, w_fc1, fc1_bias, w_fc2, fc2_bias)


PIECES = 32
GROUP = 8


def xor(value, index):
    return lax.bitwise_xor(value, jnp.int32(index))


def copy_all(copies):
    for item in copies:
        item.start()
    for item in copies:
        item.wait()


def mlp_back_kernel(
    top, kinds, me, dx_ref, c, gh, gp, xh, rstd, gain, w1, w2,
    dmid, keep1, send1, keep2, send2, sums, dx_s, gw1, gw2, sems,
):
    block = pl.program_id(0)

    @pl.when(block == 0)
    def _():
        gw1[...] = jnp.zeros_like(gw1)
        gw2[...] = jnp.zeros_like(gw2)
        sums[...] = jnp.zeros_like(sums)

    if top:
        images, rows, width = dx_ref.shape
        padded = dx_s.shape[1]
        for i in range(images):
            kind = kinds[block * images + i]
            here = lax.broadcasted_iota(jnp.int32, (rows, 1), 0) < length_of(kind)
            dx_s[i] = jnp.zeros((padded, width), F32)
            dx_s[i, 0:rows, :] = jnp.where(here, dx_ref[i].astype(F32), 0.0)
        dx = dx_s[...].reshape(images * padded, width)
    else:
        dx = dx_ref[...]
    flat, width = dx.shape
    hidden = w1.shape[2]
    dz = dx.astype(BF16)
    sums[11:12, :] += jnp.sum(dz.astype(F32), 0, keepdims=True)
    dc = jnp.zeros((flat, width), F32)
    together = 4
    for index in range(0, hidden // width, together):
        cols = slice(index * width, (index + together) * width)
        dgh = dot_bt(dz, w2[0, cols, :])
        dpre = (dgh * gp[0, :, cols].astype(F32)).astype(BF16)
        column = jnp.sum(dpre.astype(F32), 0, keepdims=True)
        grad = dot_at(c[0], dpre)
        for k in range(together):
            here = slice(k * width, (k + 1) * width)
            sums[7 + index + k : 8 + index + k, :] += column[:, here]
            gw1[index + k] += grad[:, here]
        gw2[cols, :] += dot_at(gh[0, :, cols], dz)
        dc += dot_bt(dpre, w1[0, :, cols])
    xhat = xh[0].astype(F32)
    sums[1:2, :] += jnp.sum(dc * xhat, 0, keepdims=True)
    sums[3:4, :] += jnp.sum(dc, 0, keepdims=True)
    dmid[...] = dx + norm_back(dc, xhat, rstd[0], gain[0, 1:2].astype(F32))

    @pl.when(block == pl.num_programs(0) - 1)
    def _():
        piece = hidden // PIECES
        half = PIECES // 2
        copies = []
        for r in range(PIECES):
            first, second = xor(me[0], r), xor(me[1], r)
            out1, out2 = (keep1, keep2) if r < half else (send1, send2)
            row = pl.multiple_of(lax.bitwise_and(first, GROUP - 1) * piece, 8)
            col = lax.shift_right_logical(first, 3)
            copies.append(pltpu.make_async_copy(gw1.at[col, pl.ds(row, piece)], out1.at[r % half], sems.at[2 * r]))
            row = pl.multiple_of(second * piece, 8)
            copies.append(pltpu.make_async_copy(gw2.at[pl.ds(row, piece)], out2.at[r % half], sems.at[2 * r + 1]))
        copy_all(copies)


def halves(piece, width):
    return [jax.ShapeDtypeStruct((PIECES // 2, piece, width), F32)] * 2


def drop(kernel, fixed, first, count):
    def body(*refs):
        return kernel(*fixed, *refs[:first], *refs[first + count :])

    return body


def mlp_back(layer, top, kinds, me, dx, c, gh, gp, xh, rstd, gain, w1, w2, padded, per, after):
    layers, width, hidden = w1.shape
    total = c.shape[1]
    flat = per * padded
    blocks = total // flat
    saved = lambda feat: pl.BlockSpec((1, flat, feat), lambda b, k, m: (layer, b, 0))
    param = lambda *shape: pl.BlockSpec((1,) + shape, lambda b, k, m: (layer, 0, 0))
    if top:
        dx_spec = pl.BlockSpec((per,) + dx.shape[1:], lambda b, k, m: (b, 0, 0))
    else:
        dx_spec = pl.BlockSpec((flat, width), lambda b, k, m: (b, 0))
    anywhere = pl.BlockSpec(memory_space=pl.ANY)
    return pl.pallas_call(
        drop(mlp_back_kernel, (top,), 11, len(after)),
        grid_spec=pltpu.PrefetchScalarGridSpec(
            num_scalar_prefetch=2,
            grid=(blocks,),
            in_specs=[
                dx_spec,
                saved(width),
                saved(hidden),
                saved(hidden),
                saved(width),
                saved(1),
                param(2, width),
                param(width, hidden),
                param(hidden, width),
            ]
            + [anywhere] * len(after),
            out_specs=[
                pl.BlockSpec((flat, width), lambda b, k, m: (b, 0)),
                anywhere,
                anywhere,
                anywhere,
                anywhere,
                pl.BlockSpec((16, width), lambda b, k, m: (0, 0)),
            ],
            scratch_shapes=[
                pltpu.VMEM((per, padded, width), F32),
                pltpu.VMEM((hidden // width, width, width), F32),
                pltpu.VMEM((hidden, width), F32),
                pltpu.SemaphoreType.DMA((2 * PIECES,)),
            ],
        ),
        out_shape=[jax.ShapeDtypeStruct((total, width), F32)]
        + halves(hidden // PIECES, width)
        + halves(hidden // PIECES, width)
        + [jax.ShapeDtypeStruct((16, width), F32)],
        compiler_params=pltpu.CompilerParams(vmem_limit_bytes=VMEM_LIMIT),
        cost_estimate=pl.CostEstimate(flops=8 * total * width * hidden, bytes_accessed=30 * total * width, transcendentals=0),
        name="mlp_backward",
    )(kinds, me, dx, c, gh, gp, xh, rstd, gain, w1, w2, *after)


def attn_back_kernel(bottom, layers, kinds, me, dmid, o, qkv, lse, a, xh, rstd, gain, w_qkv, w_out, *rest):
    if bottom:
        interp, dx_ref, keep1, send1, keep2, send2, dqkv_s, do_s, gw, sems, sums, kind_s, misc = rest[:1] + rest[2 * layers :]
        others = rest[1 : 2 * layers]
    else:
        dx_ref, keep1, send1, keep2, send2, sums, dqkv_s, do_s, gw, sems = rest
    block = pl.program_id(0)
    images = lse.shape[1]
    flat, width = dmid.shape
    padded = flat // images

    @pl.when(block == 0)
    def _():
        gw[...] = jnp.zeros_like(gw)
        sums[...] = jnp.zeros_like(sums)
        if bottom:
            kind_s[...] = jnp.zeros_like(kind_s)

    dy = dmid[...].astype(BF16)
    sums[6:7, :] += jnp.sum(dy.astype(F32), 0, keepdims=True)
    do_s[...] = dot_bt(dy, w_out[0]).astype(BF16)
    gw[3] += dot_at(o[0], dy)
    pair_width = 2 * HEAD
    plain, scaled = head_masks()
    first = lax.broadcasted_iota(jnp.int32, (1, pair_width), 1) < HEAD
    for i in range(images):
        rows = slice(i * padded, (i + 1) * padded)
        length = length_of(kinds[block * images + i])
        key_ok = lax.broadcasted_iota(jnp.int32, (1, padded, 1), 1) < length
        for pair in range(HEADS // 2):
            c0 = pair * pair_width
            part = lambda base: slice(base + c0, base + c0 + pair_width)
            q2, k2, v2 = qkv[0, rows, part(0)], qkv[0, rows, part(width)], qkv[0, rows, part(2 * width)]
            do2 = do_s[rows, part(0)]
            ks = jnp.concatenate([k2 * keep for keep in scaled], 0)
            vs = jnp.concatenate([v2 * keep for keep in plain], 0)
            s = jnp.where(key_ok, dot_bt(ks, q2).reshape(2, padded, padded), -1e9)
            p = jnp.exp(s - lse[0, i, 2 * pair : 2 * pair + 2, :].reshape(2, 1, padded))
            dp = dot_bt(vs, do2).reshape(2, padded, padded)
            delta = jnp.sum(dp * p, 1, keepdims=True)
            ds = (p * (dp - delta)).astype(BF16).reshape(2 * padded, padded)
            dv = dot(p.astype(BF16).reshape(2 * padded, padded), do2)
            dk = dot(ds, q2)
            dqkv_s[rows, part(0)] = dot_at(ds, ks).astype(BF16)
            dqkv_s[rows, part(width)] = (jnp.where(first, dk[:padded], dk[padded:]) * HEAD**-0.5).astype(BF16)
            dqkv_s[rows, part(2 * width)] = jnp.where(first, dv[:padded], dv[padded:]).astype(BF16)
    d = dqkv_s[...]
    for index in (0, 2):
        row = 4 + index // 2
        sums[row : row + 1, :] += jnp.sum(d[:, index * width : (index + 1) * width].astype(F32), 0, keepdims=True)
    grad = dot_at(a[0], d)
    for index in range(3):
        gw[index] += grad[:, index * width : (index + 1) * width]
    da = dot_bt(d, w_qkv[0])
    xhat = xh[0].astype(F32)
    sums[0:1, :] += jnp.sum(da * xhat, 0, keepdims=True)
    sums[2:3, :] += jnp.sum(da, 0, keepdims=True)
    dx = dmid[...] + norm_back(da, xhat, rstd[0], gain[0, 0:1].astype(F32))
    if bottom:
        real = dx_ref.shape[1]
        for i in range(images):
            kind = kinds[block * images + i]
            here = lax.broadcasted_iota(jnp.int32, (padded, 1), 0) < length_of(kind)
            mine = jnp.where(here, dx[i * padded : (i + 1) * padded], 0.0)
            dx_ref[i] = mine[0:real]
            kind_s[kind] += mine
    else:
        dx_ref[...] = dx

    @pl.when(block == pl.num_programs(0) - 1)
    def _():
        half = PIECES // 2
        piece = gw.shape[0] * width // PIECES
        part = piece // 2
        copies = []
        for r in range(PIECES):
            for which, out in ((0, keep1 if r < half else send1), (1, keep2 if r < half else send2)):
                j = xor(me[which], r)
                row = pl.multiple_of(lax.bitwise_and(j, GROUP - 1) * piece + which * part, 8)
                col = lax.shift_right_logical(j, 3)
                copies.append(
                    pltpu.make_async_copy(
                        gw.at[col, pl.ds(row, part)], out.at[r % half, pl.ds(0, part)], sems.at[2 * r + which]
                    )
                )
        for item in copies:
            item.start()
        if bottom:
            total = jnp.zeros((real, width), F32)
            for kind in range(interp.shape[0]):
                hi, mid, _ = split3(interp[kind])
                ghi, gmid, _ = split3(kind_s[kind, 0:real, :])
                total += dot_at(mid, ghi) + dot_at(hi, gmid) + dot_at(hi, ghi)
            misc[...] = jnp.zeros_like(misc)
            misc[0:real, :] = total
            misc[200:216, :] = sums[...] + others[0][...]
            for layer in range(1, layers):
                misc[200 + 16 * layer : 216 + 16 * layer, :] = others[2 * layer - 1][...] + others[2 * layer][...]
            tail = misc.shape[0] // PIECES
            more = []
            for r in range(PIECES):
                j = xor(me[1], r)
                more.append(
                    pltpu.make_async_copy(
                        misc.at[pl.ds(pl.multiple_of(j * tail, 8), tail)],
                        (keep2 if r < half else send2).at[r % half, pl.ds(part, tail)],
                        sems.at[2 * PIECES + r],
                    )
                )
            copy_all(more)
        for item in copies:
            item.wait()


MISC_ROWS = 256


def attn_back(layer, bottom, kinds, me, dmid, o, qkv, lse, a, xh, rstd, gain, w_qkv, w_out, interp, like, others, padded, per, after):
    width = dmid.shape[1]
    total = dmid.shape[0]
    layers = w_qkv.shape[0]
    flat = per * padded
    blocks = total // flat
    saved = lambda feat: pl.BlockSpec((1, flat, feat), lambda b, k, m: (layer, b, 0))
    param = lambda *shape: pl.BlockSpec((1,) + shape, lambda b, k, m: (layer, 0, 0))
    fixed = lambda *shape: pl.BlockSpec(shape, lambda b, k, m: (0,) * len(shape))
    anywhere = pl.BlockSpec(memory_space=pl.ANY)
    in_specs = [
        pl.BlockSpec((flat, width), lambda b, k, m: (b, 0)),
        saved(width),
        saved(3 * width),
        pl.BlockSpec((1, per, 8, padded), lambda b, k, m: (layer, b, 0, 0)),
        saved(width),
        saved(width),
        saved(1),
        param(2, width),
        param(width, 3 * width),
        param(width, width),
    ]
    part = 4 * width // PIECES // 2
    tail = MISC_ROWS // PIECES if bottom else 0
    grads = halves(part, width) + halves(part + tail, width)
    grads_specs = [anywhere] * 4
    scratch = [
        pltpu.VMEM((flat, 3 * width), BF16),
        pltpu.VMEM((flat, width), BF16),
        pltpu.VMEM((4, width, width), F32),
        pltpu.SemaphoreType.DMA(((3 if bottom else 2) * PIECES,)),
    ]
    args = [kinds, me, dmid, o, qkv, lse, a, xh, rstd, gain, w_qkv, w_out]
    if bottom:
        rows = like.shape[1]
        in_specs += [fixed(*interp.shape)] + [fixed(16, width)] * len(others)
        args += [interp] + others
        out_specs = [pl.BlockSpec((per, rows, width), lambda b, k, m: (b, 0, 0))] + grads_specs
        out_shape = [jax.ShapeDtypeStruct(like.shape, F32)] + grads
        scratch += [pltpu.VMEM((16, width), F32), pltpu.VMEM((3, padded, width), F32), pltpu.VMEM((MISC_ROWS, width), F32)]
    else:
        out_specs = [pl.BlockSpec((flat, width), lambda b, k, m: (b, 0))] + grads_specs + [fixed(16, width)]
        out_shape = [jax.ShapeDtypeStruct((total, width), F32)] + grads + [jax.ShapeDtypeStruct((16, width), F32)]
    first = len(args)
    in_specs += [anywhere] * len(after)
    args += after
    return pl.pallas_call(
        drop(attn_back_kernel, (bottom, layers), first, len(after)),
        grid_spec=pltpu.PrefetchScalarGridSpec(
            num_scalar_prefetch=2,
            grid=(blocks,),
            in_specs=in_specs,
            out_specs=out_specs,
            scratch_shapes=scratch,
        ),
        out_shape=out_shape,
        compiler_params=pltpu.CompilerParams(vmem_limit_bytes=VMEM_LIMIT),
        cost_estimate=pl.CostEstimate(flops=32 * total * width * width, bytes_accessed=30 * total * width, transcendentals=0),
        name="attention_backward",
    )(*args)


def exchange(x, axis, bits, size):
    return lax.ppermute(x, axis, [(i, i ^ bits) for i in range(size)])


class Round:
    def __init__(self, streams, sizes):
        self.streams, self.sizes, self.stage = streams, sizes, 0

    def swap(self, x, axis, bits):
        return exchange(x, axis, bits, self.sizes[axis])

    def advance(self):
        stage = self.stage
        self.stage += 1
        if stage == 0:
            self.keep = [stream[0] for stream in self.streams]
            sent = [stream[1] for stream in self.streams]
            self.got = [self.swap(x, "grp", 1) for x in sent]
        elif stage <= 2:
            half = self.keep[0].shape[0] // 2
            sent = [keep[half:] + got[half:] for keep, got in zip(self.keep, self.got)]
            self.keep = [keep[:half] + got[:half] for keep, got in zip(self.keep, self.got)]
            self.got = [self.swap(x, "grp", stream[1 + stage]) for x, stream in zip(sent, self.streams)]
        elif stage == 3:
            joined = jnp.concatenate([keep + got for keep, got in zip(self.keep, self.got)], 1)
            self.keep = joined[0]
            sent = [joined[k] for k in range(1, 4)]
            self.got = [self.swap(x, "dp", k + 1) for k, x in enumerate(sent)]
        elif stage == 4:
            total = self.keep + self.got[0] + self.got[1] + self.got[2]
            for axis, bit in (("grp", 8), ("dp", 4)):
                while bit < self.sizes[axis]:
                    total = total + self.swap(total, axis, bit)
                    bit *= 2
            sent = [total]
            self.keep = total
            self.got = [self.swap(total, "dp", k) for k in range(1, 4)]
        elif stage == 5:
            every = jnp.stack([self.keep] + self.got)
            start, sent = 0, []
            for stream in self.streams:
                rows = stream[0].shape[1]
                sent.append(every[:, start : start + rows])
                start += rows
            self.keep = sent
            self.got = [self.swap(x, "grp", stream[3]) for x, stream in zip(sent, self.streams)]
        elif stage == 6:
            sent = [jnp.concatenate([keep, got]) for keep, got in zip(self.keep, self.got)]
            self.keep = sent
            self.got = [self.swap(x, "grp", stream[2]) for x, stream in zip(sent, self.streams)]
        else:
            self.keep = [[keep, got] for keep, got in zip(self.keep, self.got)]
            sent = sum(self.keep, [])
            self.got = [[self.swap(x, "grp", 1) for x in pair] for pair in self.keep]
        return sent

    def finish(self):
        while self.stage < 8:
            self.advance()
        return [keep + got for keep, got in zip(self.keep, self.got)]


def place_mlp_kernel(layer, me, *refs):
    alphas, betas = refs[0:4], refs[4:8]
    out1, out2, sems = refs[-3:]
    piece = alphas[0].shape[1]
    width = alphas[0].shape[2]
    copies = []
    for r in range(PIECES):
        j = xor(me[0], r)
        row = pl.multiple_of(lax.bitwise_and(j, GROUP - 1) * piece, 8)
        col = pl.multiple_of(lax.shift_right_logical(j, 3) * width, 128)
        copies.append(
            pltpu.make_async_copy(
                alphas[r // GROUP].at[r % GROUP], out1.at[layer, pl.ds(row, piece), pl.ds(col, width)], sems.at[2 * r]
            )
        )
        j = xor(me[1], r)
        row = pl.multiple_of(j * piece, 8)
        copies.append(
            pltpu.make_async_copy(betas[r // GROUP].at[r % GROUP], out2.at[layer, pl.ds(row, piece)], sems.at[2 * r + 1])
        )
    copy_all(copies)


def place_mlp(layer, me, pieces, before, shapes):
    anywhere = pl.BlockSpec(memory_space=pl.ANY)
    args = [me] + pieces[0] + pieces[1] + list(before)
    return pl.pallas_call(
        partial(place_mlp_kernel, layer),
        grid_spec=pltpu.PrefetchScalarGridSpec(
            num_scalar_prefetch=1,
            grid=(1,),
            in_specs=[pl.BlockSpec(x.shape, lambda b, m: (0, 0, 0)) for x in args[1:9]] + [anywhere] * len(before),
            out_specs=[anywhere] * 2,
            scratch_shapes=[pltpu.SemaphoreType.DMA((2 * PIECES,))],
        ),
        out_shape=[jax.ShapeDtypeStruct(shape, F32) for shape in shapes],
        input_output_aliases={9: 0, 10: 1} if before else {},
        compiler_params=pltpu.CompilerParams(vmem_limit_bytes=VMEM_LIMIT),
        name="place_mlp",
    )(*args)


def place_attn_kernel(layer, layers, last, me, *refs):
    alphas, betas = refs[0:4], refs[4:8]
    if last:
        gqkv, gout, gpos, ggain, gbias, gqvb, goutb, gb1, gb2, sems, misc, tail_sems = refs[-12:]
    else:
        gqkv, gout, sems = refs[-3:]
    part = alphas[0].shape[1]
    width = alphas[0].shape[2]
    waits = []
    tails = []
    for r in range(PIECES):
        for which, group in ((0, alphas), (1, betas)):
            j = xor(me[which], r)
            row = pl.multiple_of(lax.bitwise_and(j, GROUP - 1) * 2 * part + which * part, 8)
            col = lax.shift_right_logical(j, 3)
            source = group[r // GROUP].at[r % GROUP, pl.ds(0, part)]
            sem = sems.at[2 * r + which]

            @pl.when(col < 3)
            def _():
                wide = pl.multiple_of(col * width, 128)
                pltpu.make_async_copy(source, gqkv.at[layer, pl.ds(row, part), pl.ds(wide, width)], sem).start()

            @pl.when(col == 3)
            def _():
                pltpu.make_async_copy(source, gout.at[layer, pl.ds(row, part)], sem).start()

            waits.append(pltpu.make_async_copy(source, gout.at[layer, pl.ds(row, part)], sem))
        if last:
            tail = misc.shape[0] // PIECES
            j = xor(me[1], r)
            item = pltpu.make_async_copy(
                betas[r // GROUP].at[r % GROUP, pl.ds(part, tail)],
                misc.at[pl.ds(pl.multiple_of(j * tail, 8), tail)],
                tail_sems.at[r],
            )
            item.start()
            tails.append(item)
    if last:
        for item in tails:
            item.wait()
        gpos[...] = misc[0 : gpos.shape[0], :]
        for index in range(layers):
            base = 200 + 16 * index
            ggain[index] = misc[base : base + 2, :]
            gbias[index] = misc[base + 2 : base + 4, :]
            gqvb[index] = misc[base + 4 : base + 6, :]
            goutb[index : index + 1, :] = misc[base + 6 : base + 7, :]
            for k in range(gb1.shape[1] // width):
                gb1[index : index + 1, k * width : (k + 1) * width] = misc[base + 7 + k : base + 8 + k, :]
            gb2[index : index + 1, :] = misc[base + 11 : base + 12, :]
    for item in waits:
        item.wait()


def place_attn(layer, layers, me, pieces, before, shapes, small):
    anywhere = pl.BlockSpec(memory_space=pl.ANY)
    args = [me] + pieces[0] + pieces[1] + list(before)
    last = bool(small)
    scratch = [pltpu.SemaphoreType.DMA((2 * PIECES,))]
    if last:
        scratch += [pltpu.VMEM((MISC_ROWS, shapes[1][-1]), F32), pltpu.SemaphoreType.DMA((PIECES,))]
    return pl.pallas_call(
        partial(place_attn_kernel, layer, layers, last),
        grid_spec=pltpu.PrefetchScalarGridSpec(
            num_scalar_prefetch=1,
            grid=(1,),
            in_specs=[pl.BlockSpec(x.shape, lambda b, m: (0, 0, 0)) for x in args[1:9]] + [anywhere] * len(before),
            out_specs=[anywhere] * 2 + [pl.BlockSpec(s, lambda b, m, n=len(s): (0,) * n) for s in small],
            scratch_shapes=scratch,
        ),
        out_shape=[jax.ShapeDtypeStruct(shape, F32) for shape in list(shapes) + list(small)],
        input_output_aliases={9: 0, 10: 1} if before else {},
        compiler_params=pltpu.CompilerParams(vmem_limit_bytes=VMEM_LIMIT),
        name="place_attention",
    )(*args)


def on_device(sizes, tokens, kinds, interp, pos_base, ln_gain, ln_bias, w_qkv, qv_bias, w_out, out_bias, w_fc1, fc1_bias, w_fc2, fc2_bias, cotangent):
    count, rows, width = tokens.shape
    layers = w_qkv.shape[0]
    padded = -(-rows // 16) * 16
    per = 2 if count % 2 == 0 else 1
    g, d = lax.axis_index("grp"), lax.axis_index("dp")
    bit = lambda value, index: lax.bitwise_and(lax.shift_right_logical(value, index), 1)
    low = lax.bitwise_and(d, 3)
    me = jnp.stack(
        [
            bit(g, 0) * 16 + bit(g, 1) * 8 + bit(g, 2) * 4 + low,
            bit(g, 0) * 16 + bit(g, 2) * 8 + bit(g, 1) * 4 + low,
        ]
    ).astype(jnp.int32)
    mixed, a, qkv, lse, o, c, gp, gh, xh1, r1, xh2, r2 = forward(
        kinds, tokens, interp, pos_base, ln_gain, ln_bias, w_qkv, qv_bias, w_out, out_bias, w_fc1, fc1_bias, w_fc2, fc2_bias, padded, per
    )
    args = (kinds, me)
    small = (pos_base.shape, ln_gain.shape, ln_bias.shape, qv_bias.shape, out_bias.shape, fc1_bias.shape, fc2_bias.shape)
    dx, after, sums, rounds = cotangent, [], [], {}
    for layer in reversed(range(layers)):
        dmid, keep1, send1, keep2, send2, mlp_sums = mlp_back(
            layer, layer == layers - 1, *args, dx, c, gh, gp, xh2, r2, ln_gain, w_fc1, w_fc2, padded, per, after
        )
        after = sum([item.advance() for item in rounds.values()], [])
        item = rounds["mlp", layer] = Round(((keep1, send1, 2, 4), (keep2, send2, 4, 2)), sizes)
        item.advance()
        after += item.advance()
        out = attn_back(
            layer, layer == 0, *args, dmid, o, qkv, lse, a, xh1, r1, ln_gain, w_qkv, w_out, interp, tokens, [mlp_sums] + sums, padded, per, after
        )
        dx, keep1, send1, keep2, send2 = out[:5]
        after = sum([item.advance() for item in rounds.values()], [])
        item = rounds["attn", layer] = Round(((keep1, send1, 2, 4), (keep2, send2, 4, 2)), sizes)
        item.advance()
        after += item.advance()
        sums = [mlp_sums] + list(out[5:]) + sums
    while any(item.stage < 8 for item in rounds.values()):
        for item in rounds.values():
            if item.stage < 8:
                item.advance()
    mlp_out, attn_out = (), ()
    for layer in reversed(range(layers)):
        mlp_out = place_mlp(layer, me, rounds["mlp", layer].finish(), mlp_out, (w_fc1.shape, w_fc2.shape))
        attn_out = place_attn(
            layer, layers, me, rounds["attn", layer].finish(), attn_out[:2], (w_qkv.shape, w_out.shape), () if layer else small
        )
    gqkv, gout, gpos, ggain, gbias, gqvb, goutb, gb1, gb2 = attn_out
    return mixed, dx, gpos, ggain, gbias, gqkv, gqvb, gout, goutb, mlp_out[0], gb1, mlp_out[1], gb2


def solution(mesh):
    split = P(("grp", "dp"), None, None)
    return jax.shard_map(
        partial(on_device, dict(mesh.shape)),
        mesh=mesh,
        in_specs=(split, P(("grp", "dp"))) + (P(),) * 12 + (split,),
        out_specs=(split, split) + (P(),) * 11,
        check_vma=False,
    )
```

```python
from functools import partial

import jax
import jax.numpy as jnp
from jax import lax
from jax.experimental import pallas as pl
from jax.experimental.pallas import tpu as pltpu
from jax.sharding import PartitionSpec as P

HEADS = 6
HEAD = 64
BASE = 197
CROP_B = 181
CROP_C = 193
EPS = 1e-06
F32 = jnp.float32
BF16 = jnp.bfloat16
VMEM_LIMIT = 60 * 1024 * 1024

ERF_P = 0.39
ERF_C = (0.11766263, 0.04569411, 0.32477995, -0.31770045, 0.44333237, -0.11376861)


def dot(a, b):
    return lax.dot_general(a, b, (((1,), (0,)), ((), ())), preferred_element_type=F32)


def dot_bt(a, b):
    return lax.dot_general(a, b, (((1,), (1,)), ((), ())), preferred_element_type=F32)


def dot_at(a, b):
    return lax.dot_general(a, b, (((0,), (0,)), ((), ())), preferred_element_type=F32)


def split3(x):
    hi = x.astype(BF16)
    rest = x - hi.astype(F32)
    mid = rest.astype(BF16)
    low = (rest - mid.astype(F32)).astype(BF16)
    return hi, mid, low


def length_of(kind):
    return jnp.where(kind == 0, BASE, jnp.where(kind == 1, CROP_B, CROP_C)).astype(jnp.int32)


def pick(ref, layer):
    row = ref[0:1].astype(F32)
    for index in range(1, ref.shape[0]):
        row = jnp.where(layer == index, ref[index : index + 1].astype(F32), row)
    return row


def norm(x):
    width = x.shape[-1]
    mean = jnp.sum(x, -1, keepdims=True) * (1.0 / width)
    centered = x - mean
    var = jnp.sum(centered * centered, -1, keepdims=True) * (1.0 / width)
    rstd = lax.rsqrt(var + EPS)
    return centered * rstd, rstd


def norm_back(dc, xhat, rstd, gain):
    width = dc.shape[-1]
    dxh = dc * gain
    m1 = jnp.sum(dxh, -1, keepdims=True) * (1.0 / width)
    m2 = jnp.sum(dxh * xhat, -1, keepdims=True) * (1.0 / width)
    return rstd * (dxh - m1 - xhat * m2)


def gelu_parts(x):
    phi = 0.5 + 0.5 * lax.erf(x * 0.5**0.5)
    return x * phi, phi + x * (jnp.exp2(x * x * (-0.5 * 1.4426950408889634)) * 0.3989422804014327)


def head_masks():
    first = lax.broadcasted_iota(jnp.int32, (1, 2 * HEAD), 1) < HEAD
    plain = [jnp.where(first, 1.0, 0.0), jnp.where(first, 0.0, 1.0)]
    return [x.astype(BF16) for x in plain], [(x * HEAD**-0.5).astype(BF16) for x in plain]


def fwd_kernel(
    kinds, tok, interp, pos, gain, bias, w_qkv, qvb, w_out, outb, w1, b1, w2, b2,
    mixed, a_o, qkv_o, lse_o, o_o, c_o, gp_o, gh_o, xh1_o, r1_o, xh2_o, r2_o,
    x_all, table_s, mid_s, o_s,
):
    layer, block = pl.program_id(0), pl.program_id(1)
    x_s = x_all.at[block]
    images, rows, width = tok.shape
    padded = x_all.shape[2]
    flat = images * padded
    heads_pair = 2 * HEAD

    @pl.when((block == 0) & (layer == 0))
    def _():
        for kind in range(interp.shape[0]):
            total = jnp.zeros((rows, width), F32)
            for part in split3(interp[kind])[::-1]:
                total += dot(part, pos[...])
            table_s[kind, 0:rows, :] = total

    @pl.when(layer == 0)
    def _():
        for i in range(images):
            kind = kinds[block * images + i]
            here = lax.broadcasted_iota(jnp.int32, (rows, 1), 0) < length_of(kind)
            h0 = tok[i].astype(F32) + table_s[kind, 0:rows, :]
            x_s[i] = jnp.zeros((padded, width), F32)
            x_s[i, 0:rows, :] = jnp.where(here, h0, 0.0)

    x = x_s[...].reshape(flat, width)
    xhat, rstd = norm(x)
    a = (xhat * gain[0, 0:1].astype(F32) + bias[0, 0:1].astype(F32)).astype(BF16)
    a_o[0] = a
    xh1_o[0] = xhat.astype(BF16)
    r1_o[0] = rstd
    bias_row = qvb[0].astype(F32)
    bias_row = jnp.concatenate([bias_row[0:1], jnp.zeros((1, width), F32), bias_row[1:2]], 1)
    qkv_o[0] = (dot(a, w_qkv[0]) + bias_row).astype(BF16)
    plain, scaled = head_masks()
    for i in range(images):
        r0 = i * padded
        length = length_of(kinds[block * images + i])
        key_ok = lax.broadcasted_iota(jnp.int32, (1, padded, 1), 1) < length
        for pair in range(HEADS // 2):
            c0 = pair * heads_pair
            q2 = qkv_o[0, r0 : r0 + padded, c0 : c0 + heads_pair]
            k2 = qkv_o[0, r0 : r0 + padded, width + c0 : width + c0 + heads_pair]
            v2 = qkv_o[0, r0 : r0 + padded, 2 * width + c0 : 2 * width + c0 + heads_pair]
            ks = jnp.concatenate([k2 * keep for keep in scaled], 0)
            vs = jnp.concatenate([v2 * keep for keep in plain], 0)
            s = jnp.where(key_ok, dot_bt(ks, q2).reshape(2, padded, padded), -1e9)
            top = jnp.max(s, 1, keepdims=True)
            e = jnp.exp(s - top)
            total = jnp.sum(e, 1, keepdims=True)
            lse_o[0, i, 2 * pair : 2 * pair + 2, :] = (top + jnp.log(total)).reshape(2, padded)
            p = (e * (1.0 / total)).astype(BF16).reshape(2 * padded, padded)
            o_s[r0 : r0 + padded, c0 : c0 + heads_pair] = dot_at(p, vs).astype(BF16)
    o = o_s[...]
    o_o[0] = o
    mid = x_s[...].reshape(flat, width) + dot(o, w_out[0]) + pick(outb, layer)
    mid_s[...] = mid
    xhat, rstd = norm(mid)
    c = (xhat * gain[0, 1:2].astype(F32) + bias[0, 1:2].astype(F32)).astype(BF16)
    c_o[0] = c
    xh2_o[0] = xhat.astype(BF16)
    r2_o[0] = rstd
    hidden = w1.shape[2]
    bias1 = pick(b1, layer)
    step = 256
    total = mid_s[...] + pick(b2, layer)
    for f in range(0, hidden, step):
        pre = dot(c, w1[0, :, f : f + step]) + bias1[:, f : f + step]
        gh, gp = gelu_parts(pre)
        gh = gh.astype(BF16)
        gh_o[0, :, f : f + step] = gh
        gp_o[0, :, f : f + step] = gp.astype(BF16)
        total += dot(gh, w2[0, f : f + step, :])
    x_s[...] = total.reshape(images, padded, width)

    @pl.when(layer == pl.num_programs(0) - 1)
    def _():
        for i in range(images):
            kind = kinds[block * images + i]
            here = lax.broadcasted_iota(jnp.int32, (rows, 1), 0) < length_of(kind)
            mixed[i] = jnp.where(here, x_s[i, 0:rows, :], 0.0).astype(BF16)


def forward(kinds, tokens, interp, pos_base, ln_gain, ln_bias, w_qkv, qv_bias, w_out, out_bias, w_fc1, fc1_bias, w_fc2, fc2_bias, padded, per):
    count, rows, width = tokens.shape
    layers, _, hidden = w_fc1.shape
    blocks = count // per
    flat = per * padded
    whole = lambda shape: pl.BlockSpec(shape, lambda l, b, k: (0,) * len(shape))
    by_layer = lambda shape: pl.BlockSpec((1,) + shape, lambda l, b, k: (l,) + (0,) * len(shape))
    read_image = pl.BlockSpec((per, rows, width), lambda l, b, k: (jnp.where(l == 0, b, blocks - 1), 0, 0))
    write_image = pl.BlockSpec((per, rows, width), lambda l, b, k: (jnp.where(l == layers - 1, b, 0), 0, 0))
    saved = lambda feat: pl.BlockSpec((1, flat, feat), lambda l, b, k: (l, b, 0))
    shape = lambda feat, dtype: jax.ShapeDtypeStruct((layers, count * padded, feat), dtype)
    return pl.pallas_call(
        fwd_kernel,
        grid_spec=pltpu.PrefetchScalarGridSpec(
            num_scalar_prefetch=1,
            grid=(layers, blocks),
            in_specs=[
                read_image,
                whole(interp.shape),
                whole(pos_base.shape),
                by_layer((2, width)),
                by_layer((2, width)),
                by_layer((width, 3 * width)),
                by_layer((2, width)),
                by_layer((width, width)),
                whole(out_bias.shape),
                by_layer((width, hidden)),
                whole(fc1_bias.shape),
                by_layer((hidden, width)),
                whole(fc2_bias.shape),
            ],
            out_specs=[
                write_image,
                saved(width),
                saved(3 * width),
                pl.BlockSpec((1, per, 8, padded), lambda l, b, k: (l, b, 0, 0)),
                saved(width),
                saved(width),
                saved(hidden),
                saved(hidden),
                saved(width),
                saved(1),
                saved(width),
                saved(1),
            ],
            scratch_shapes=[
                pltpu.VMEM((blocks, per, padded, width), F32),
                pltpu.VMEM((3, padded, width), F32),
                pltpu.VMEM((flat, width), F32),
                pltpu.VMEM((flat, width), BF16),
            ],
        ),
        out_shape=[
            jax.ShapeDtypeStruct(tokens.shape, BF16),
            shape(width, BF16),
            shape(3 * width, BF16),
            jax.ShapeDtypeStruct((layers, count, 8, padded), F32),
            shape(width, BF16),
            shape(width, BF16),
            shape(hidden, BF16),
            shape(hidden, BF16),
            shape(width, BF16),
            shape(1, F32),
            shape(width, BF16),
            shape(1, F32),
        ],
        compiler_params=pltpu.CompilerParams(vmem_limit_bytes=VMEM_LIMIT),
        name="encoder_forward",
    )(kinds, tokens, interp, pos_base, ln_gain, ln_bias, w_qkv, qv_bias, w_out, out_bias, w_fc1, fc1_bias, w_fc2, fc2_bias)


PIECES = 32
HALF = PIECES // 2
GROUP = 4
MISC_ROWS = 256
MISC_BASE = 200
MISC_LAYER = 16


def spot(me, r, rows):
    j = lax.bitwise_xor(me, jnp.int32(r))
    return lax.shift_right_logical(j, 3), pl.multiple_of(lax.bitwise_and(j, 7) * rows, 8)


def emit(me, source, keep, send, first, sems):
    rows = source.shape[1] // 8
    copies = []
    for r in range(PIECES):
        block, row = spot(me[r // HALF], r % HALF, rows)
        target = (keep, send)[r // HALF].at[r % HALF, pl.ds(first, rows)]
        copies.append(pltpu.make_async_copy(source.at[block, pl.ds(row, rows)], target, sems.at[r]))
    for item in copies:
        item.start()
    return copies


def mlp_back_kernel(top, kinds, me, dx_ref, c, gh, gp, xh, rstd, gain, w1, w2, dmid, *rest):
    if top:
        keep, send, sums, gw1, sems, gw2, dx_s = rest
    else:
        keep, send, sums, gw1, sems = rest
    block = pl.program_id(0)

    @pl.when(block == 0)
    def _():
        gw1[...] = jnp.zeros_like(gw1)
        if top:
            gw2[...] = jnp.zeros_like(gw2)
        sums[...] = jnp.zeros_like(sums)

    if top:
        images, rows, width = dx_ref.shape
        padded = dx_s.shape[1]
        for i in range(images):
            kind = kinds[block * images + i]
            here = lax.broadcasted_iota(jnp.int32, (rows, 1), 0) < length_of(kind)
            dx_s[i] = jnp.zeros((padded, width), F32)
            dx_s[i, 0:rows, :] = jnp.where(here, dx_ref[i].astype(F32), 0.0)
        dx = dx_s[...].reshape(images * padded, width)
    else:
        dx = dx_ref[...]
    flat, width = dx.shape
    hidden = w1.shape[2]
    dz = dx.astype(BF16)
    sums[11:12, :] += jnp.sum(dz.astype(F32), 0, keepdims=True)
    if top:
        for k in range(gw2.shape[0]):
            gw2[k] += dot_at(gh[0, :, k * width : (k + 1) * width], dz)
    dgh = dot_bt(dz, w2[0])
    dpre = (dgh * gp[0].astype(F32)).astype(BF16)
    column = jnp.sum(dpre.astype(F32), 0, keepdims=True)
    grad = dot_at(c[0], dpre)
    for k in range(hidden // width):
        here = slice(k * width, (k + 1) * width)
        sums[7 + k : 8 + k, :] += column[:, here]
        gw1[k] += grad[:, here]
    dc = dot_bt(dpre, w1[0])
    xhat = xh[0].astype(F32)
    sums[1:2, :] += jnp.sum(dc * xhat, 0, keepdims=True)
    sums[3:4, :] += jnp.sum(dc, 0, keepdims=True)
    dmid[...] = dx + norm_back(dc, xhat, rstd[0], gain[0, 1:2].astype(F32))

    @pl.when(block == pl.num_programs(0) - 1)
    def _():
        copies = emit(me, gw1, keep, send, 0, sems)
        if top:
            copies += emit(me, gw2, keep, send, width // 8, sems.at[pl.ds(PIECES, PIECES)])
        for item in copies:
            item.wait()


def drop(kernel, fixed, first, count):
    def body(*refs):
        return kernel(*fixed, *refs[:first], *refs[first + count :])

    return body


def pieces_of(rows, width):
    return [jax.ShapeDtypeStruct((HALF, rows, width), F32)] * 2


def mlp_back(layer, top, kinds, me, dx, c, gh, gp, xh, rstd, gain, w1, w2, padded, per, after):
    layers, width, hidden = w1.shape
    total = c.shape[1]
    flat = per * padded
    saved = lambda feat: pl.BlockSpec((1, flat, feat), lambda b, k, m: (layer, b, 0))
    param = lambda *shape: pl.BlockSpec((1,) + shape, lambda b, k, m: (layer, 0, 0))
    fixed = lambda *shape: pl.BlockSpec(shape, lambda b, k, m: (0,) * len(shape))
    rows_spec = pl.BlockSpec((flat, width), lambda b, k, m: (b, 0))
    anywhere = pl.BlockSpec(memory_space=pl.ANY)
    if top:
        dx_spec = pl.BlockSpec((per,) + dx.shape[1:], lambda b, k, m: (b, 0, 0))
        scratch = [pltpu.VMEM((hidden // width, width, width), F32), pltpu.VMEM((per, padded, width), F32)]
    else:
        dx_spec = rows_spec
        scratch = []
    out_specs = [anywhere] * 2
    out_shape = pieces_of((2 if top else 1) * hidden // PIECES, width)
    scratch = [pltpu.VMEM((hidden // width, width, width), F32), pltpu.SemaphoreType.DMA((2 * PIECES,))] + scratch
    return pl.pallas_call(
        drop(mlp_back_kernel, (top,), 11, len(after)),
        grid_spec=pltpu.PrefetchScalarGridSpec(
            num_scalar_prefetch=2,
            grid=(total // flat,),
            in_specs=[
                dx_spec,
                saved(width),
                saved(hidden) if top else anywhere,
                saved(hidden),
                saved(width),
                saved(1),
                param(2, width),
                param(width, hidden),
                param(hidden, width),
            ]
            + [anywhere] * len(after),
            out_specs=[rows_spec] + out_specs + [fixed(16, width)],
            scratch_shapes=scratch,
        ),
        out_shape=[jax.ShapeDtypeStruct((total, width), F32)] + out_shape + [jax.ShapeDtypeStruct((16, width), F32)],
        compiler_params=pltpu.CompilerParams(vmem_limit_bytes=VMEM_LIMIT),
        cost_estimate=pl.CostEstimate(flops=8 * total * width * hidden, bytes_accessed=30 * total * width, transcendentals=0),
        name="mlp_backward",
    )(kinds, me, dx, c, gh, gp, xh, rstd, gain, w1, w2, *after)


def attn_back_kernel(bottom, layers, kinds, me, dmid, o, qkv, lse, a, xh, rstd, gain, w_qkv, w_out, *rest):
    if bottom:
        interp, dx_ref, keep, send, dqkv_s, do_s, gw, sems, sums, kind_s, misc = rest[:1] + rest[2 * layers :]
        others = rest[1 : 2 * layers]
    else:
        gh_next, dx_ref, keep, send, sums, dqkv_s, do_s, gw, sems, gw2 = rest
    block = pl.program_id(0)
    images = lse.shape[1]
    flat, width = dmid.shape
    padded = flat // images

    @pl.when(block == 0)
    def _():
        gw[...] = jnp.zeros_like(gw)
        sums[...] = jnp.zeros_like(sums)
        if bottom:
            kind_s[...] = jnp.zeros_like(kind_s)
        else:
            gw2[...] = jnp.zeros_like(gw2)

    dy = dmid[...].astype(BF16)
    sums[6:7, :] += jnp.sum(dy.astype(F32), 0, keepdims=True)
    do_s[...] = dot_bt(dy, w_out[0]).astype(BF16)
    gw[3] += dot_at(o[0], dy)
    pair_width = 2 * HEAD
    plain, scaled = head_masks()
    first = lax.broadcasted_iota(jnp.int32, (1, pair_width), 1) < HEAD
    for i in range(images):
        rows = slice(i * padded, (i + 1) * padded)
        length = length_of(kinds[block * images + i])
        key_ok = lax.broadcasted_iota(jnp.int32, (1, padded, 1), 1) < length
        for pair in range(HEADS // 2):
            c0 = pair * pair_width
            part = lambda base: slice(base + c0, base + c0 + pair_width)
            q2, k2, v2 = qkv[0, rows, part(0)], qkv[0, rows, part(width)], qkv[0, rows, part(2 * width)]
            do2 = do_s[rows, part(0)]
            ks = jnp.concatenate([k2 * keep for keep in scaled], 0)
            vs = jnp.concatenate([v2 * keep for keep in plain], 0)
            s = jnp.where(key_ok, dot_bt(ks, q2).reshape(2, padded, padded), -1e9)
            p = jnp.exp(s - lse[0, i, 2 * pair : 2 * pair + 2, :].reshape(2, 1, padded))
            dp = dot_bt(vs, do2).reshape(2, padded, padded)
            delta = jnp.sum(dp * p, 1, keepdims=True)
            ds = (p * (dp - delta)).astype(BF16).reshape(2 * padded, padded)
            dv = dot(p.astype(BF16).reshape(2 * padded, padded), do2)
            dk = dot(ds, q2)
            dqkv_s[rows, part(0)] = dot_at(ds, ks).astype(BF16)
            dqkv_s[rows, part(width)] = (jnp.where(first, dk[:padded], dk[padded:]) * HEAD**-0.5).astype(BF16)
            dqkv_s[rows, part(2 * width)] = jnp.where(first, dv[:padded], dv[padded:]).astype(BF16)
    d = dqkv_s[...]
    for index in (0, 2):
        row = 4 + index // 2
        sums[row : row + 1, :] += jnp.sum(d[:, index * width : (index + 1) * width].astype(F32), 0, keepdims=True)
    grad = dot_at(a[0], d)
    for index in range(3):
        gw[index] += grad[:, index * width : (index + 1) * width]
    da = dot_bt(d, w_qkv[0])
    xhat = xh[0].astype(F32)
    sums[0:1, :] += jnp.sum(da * xhat, 0, keepdims=True)
    sums[2:3, :] += jnp.sum(da, 0, keepdims=True)
    dx = dmid[...] + norm_back(da, xhat, rstd[0], gain[0, 0:1].astype(F32))
    if bottom:
        real = dx_ref.shape[1]
        for i in range(images):
            kind = kinds[block * images + i]
            here = lax.broadcasted_iota(jnp.int32, (padded, 1), 0) < length_of(kind)
            mine = jnp.where(here, dx[i * padded : (i + 1) * padded], 0.0)
            dx_ref[i] = mine[0:real]
            kind_s[kind] += mine
    else:
        dx_ref[...] = dx
        dz = dx.astype(BF16)
        for k in range(gw2.shape[0]):
            gw2[k] += dot_at(gh_next[0, :, k * width : (k + 1) * width], dz)

    @pl.when(block == pl.num_programs(0) - 1)
    def _():
        rows = width // 8
        copies = emit(me, gw, keep, send, 0, sems)
        if not bottom:
            copies += emit(me, gw2, keep, send, rows, sems.at[pl.ds(PIECES, PIECES)])
        if bottom:
            total = jnp.zeros((real, width), F32)
            for kind in range(interp.shape[0]):
                hi, mid, _ = split3(interp[kind])
                ghi, gmid, _ = split3(kind_s[kind, 0:real, :])
                total += dot_at(mid, ghi) + dot_at(hi, gmid) + dot_at(hi, ghi)
            misc[...] = jnp.zeros_like(misc)
            misc[0:real, :] = total
            misc[MISC_BASE : MISC_BASE + 16, :] = sums[...] + others[0][...]
            for layer in range(1, layers):
                start = MISC_BASE + MISC_LAYER * layer
                misc[start : start + 16, :] = others[2 * layer - 1][...] + others[2 * layer][...]
            tail = misc.shape[0] // PIECES
            for r in range(PIECES):
                j = lax.bitwise_xor(me[r // HALF], jnp.int32(r % HALF))
                target = (keep, send)[r // HALF].at[r % HALF, pl.ds(rows, tail)]
                item = pltpu.make_async_copy(misc.at[pl.ds(pl.multiple_of(j * tail, 8), tail)], target, sems.at[PIECES + r])
                item.start()
                copies.append(item)
        for item in copies:
            item.wait()


def attn_back(layer, bottom, kinds, me, dmid, o, qkv, lse, a, xh, rstd, gain, w_qkv, w_out, gh, interp, like, others, padded, per, after):
    width = dmid.shape[1]
    total = dmid.shape[0]
    layers = w_qkv.shape[0]
    flat = per * padded
    blocks = total // flat
    saved = lambda feat: pl.BlockSpec((1, flat, feat), lambda b, k, m: (layer, b, 0))
    param = lambda *shape: pl.BlockSpec((1,) + shape, lambda b, k, m: (layer, 0, 0))
    fixed = lambda *shape: pl.BlockSpec(shape, lambda b, k, m: (0,) * len(shape))
    anywhere = pl.BlockSpec(memory_space=pl.ANY)
    in_specs = [
        pl.BlockSpec((flat, width), lambda b, k, m: (b, 0)),
        saved(width),
        saved(3 * width),
        pl.BlockSpec((1, per, 8, padded), lambda b, k, m: (layer, b, 0, 0)),
        saved(width),
        saved(width),
        saved(1),
        param(2, width),
        param(width, 3 * width),
        param(width, width),
    ]
    tail = MISC_ROWS // PIECES if bottom else width // 8
    grads = pieces_of(width // 8 + tail, width)
    scratch = [
        pltpu.VMEM((flat, 3 * width), BF16),
        pltpu.VMEM((flat, width), BF16),
        pltpu.VMEM((4, width, width), F32),
        pltpu.SemaphoreType.DMA((2 * PIECES,)),
    ]
    args = [kinds, me, dmid, o, qkv, lse, a, xh, rstd, gain, w_qkv, w_out]
    if bottom:
        rows = like.shape[1]
        in_specs += [fixed(*interp.shape)] + [fixed(16, width)] * len(others)
        args += [interp] + others
        out_specs = [pl.BlockSpec((per, rows, width), lambda b, k, m: (b, 0, 0))] + [anywhere] * 2
        out_shape = [jax.ShapeDtypeStruct(like.shape, F32)] + grads
        scratch += [pltpu.VMEM((16, width), F32), pltpu.VMEM((3, padded, width), F32), pltpu.VMEM((MISC_ROWS, width), F32)]
    else:
        hidden = gh.shape[2]
        in_specs += [pl.BlockSpec((1, flat, hidden), lambda b, k, m: (layer - 1, b, 0))]
        args += [gh]
        out_specs = [pl.BlockSpec((flat, width), lambda b, k, m: (b, 0))] + [anywhere] * 2 + [fixed(16, width)]
        out_shape = [jax.ShapeDtypeStruct((total, width), F32)] + grads + [jax.ShapeDtypeStruct((16, width), F32)]
        scratch += [pltpu.VMEM((hidden // width, width, width), F32)]
    first = len(args)
    in_specs += [anywhere] * len(after)
    args += after
    return pl.pallas_call(
        drop(attn_back_kernel, (bottom, layers), first, len(after)),
        grid_spec=pltpu.PrefetchScalarGridSpec(
            num_scalar_prefetch=2,
            grid=(blocks,),
            in_specs=in_specs,
            out_specs=out_specs,
            scratch_shapes=scratch,
        ),
        out_shape=out_shape,
        compiler_params=pltpu.CompilerParams(vmem_limit_bytes=VMEM_LIMIT),
        cost_estimate=pl.CostEstimate(flops=32 * total * width * width, bytes_accessed=30 * total * width, transcendentals=0),
        name="attention_backward",
    )(*args)


def exchange(x, axis, bits, size):
    return lax.ppermute(x, axis, [(i, i ^ bits) for i in range(size)])


def combine(tasks, after, through):
    args = sum([list(inputs) for _, inputs, _ in tasks], [])
    shapes = sum([list(results) for _, _, results in tasks], [])

    def body(*refs):
        ins, outs = refs[: len(args)], refs[len(args) + len(through) + len(after) :]
        for function, inputs, results in tasks:
            function(ins[: len(inputs)], outs[: len(results)])
            ins, outs = ins[len(inputs) :], outs[len(results) :]

    vmem = pl.BlockSpec(memory_space=pltpu.VMEM)
    anywhere = pl.BlockSpec(memory_space=pl.ANY)
    moved = sum(x.size for x in args) * 4
    out = pl.pallas_call(
        body,
        in_specs=[vmem] * len(args) + [anywhere] * (len(through) + len(after)),
        out_specs=[vmem] * len(shapes) + [anywhere] * len(through),
        out_shape=[jax.ShapeDtypeStruct(shape, F32) for shape in shapes] + [jax.ShapeDtypeStruct(x.shape, F32) for x in through],
        input_output_aliases={len(args) + k: len(shapes) + k for k in range(len(through))},
        compiler_params=pltpu.CompilerParams(vmem_limit_bytes=VMEM_LIMIT),
        cost_estimate=pl.CostEstimate(flops=moved, bytes_accessed=2 * moved, transcendentals=0),
        name="combine",
    )(*args, *through, *after)
    result = []
    for _, _, results in tasks:
        result.append(list(out[: len(results)]))
        out = out[len(results) :]
    return result, list(out)


def halve(ins, outs):
    keep, got = ins
    half = keep.shape[0] // 2
    outs[0][...] = keep[half:] + got[half:]
    outs[1][...] = keep[:half] + got[:half]


def split_four(ins, outs):
    start = 0
    for keep, got in zip(ins[::2], ins[1::2]):
        rows = keep.shape[1]
        for k, out in enumerate(outs):
            out[start : start + rows] = keep[k] + got[k]
        start += rows


def total_of(ins, outs):
    start = 0
    for a, b, c, d in zip(ins[::4], ins[1::4], ins[2::4], ins[3::4]):
        rows = a.shape[0]
        outs[0][start : start + rows] = (a[...] + b[...]) + (c[...] + d[...])
        start += rows


def stack(ins, outs):
    for k, x in enumerate(ins):
        outs[0][k] = x[...]


class Round:
    def __init__(self, keep, send, sizes):
        self.keep, self.send, self.sizes, self.stage = keep, send, sizes, 0
        self.shape = keep.shape[1:]
        self.more = []

    def merge(self, other):
        assert self.stage == other.stage
        self.more = [other.keep, *other.got]
        self.shape = (self.shape[0] + other.shape[0], self.shape[1])
        return self

    def across(self, x, which):
        bits = lambda i: (2, 4)[(i & 1) ^ which]
        return lax.ppermute(x, "grp", [(i, i ^ bits(i)) for i in range(self.sizes["grp"])])

    def swap(self, x, axis, bits):
        return exchange(x, axis, bits, self.sizes[axis])

    def tasks(self):
        stage, n = self.stage, self.shape
        args = [self.keep, *getattr(self, "got", ()), *self.more]
        self.more = []
        if stage in (1, 2):
            return [(halve, args, ((PIECES >> (stage + 1),) + n,) * 2)]
        if stage == 3:
            return [(split_four, args, (n,) * 4)]
        if stage == 4:
            return [(total_of, args, (n,))]
        if stage == 5:
            return [(stack, args, ((4,) + n,))]
        return []

    def launch(self, done):
        stage = self.stage
        self.stage += 1
        if stage == 0:
            self.got = [self.swap(self.send, "grp", 1)]
        elif stage <= 2:
            self.keep, self.got = done[1], [self.across(done[0], stage - 1)]
        elif stage == 3:
            self.keep, self.got = done[0], [self.swap(done[k], "dp", k) for k in range(1, 4)]
        elif stage == 4:
            total = done[0]
            for axis, bit in (("grp", 8), ("dp", 4)):
                while bit < self.sizes[axis]:
                    total = total + self.swap(total, axis, bit)
                    bit *= 2
            self.keep, self.got = total, [self.swap(total, "dp", k) for k in range(1, 4)]
        elif stage == 5:
            self.own = done[0]
            self.second, self.first = self.across(self.own, 1), self.across(self.own, 0)
            self.pieces = [self.own, self.second, self.first, None, self.swap(self.own, "grp", 1)]
        elif stage == 6:
            self.pieces[3] = self.across(self.second, 0)
            self.pieces += [self.swap(self.second, "grp", 1), self.swap(self.first, "grp", 1)]
        else:
            self.pieces.append(self.swap(self.pieces[3], "grp", 1))


class Order:
    def __init__(self):
        self.after = []

    def step(self, *rounds, new=None):
        tasks = [item.tasks() for item in rounds]
        flat = sum(tasks, [])
        if flat:
            done, through = combine(flat, self.after, [new.send] if new else [])
            for item, own in zip(rounds, tasks):
                item.launch([x for result in done[: len(own)] for x in result])
                if own:
                    self.after = [done[0][0]]
                done = done[len(own) :]
            if new:
                new.send = through[0]
        else:
            for item in rounds:
                item.launch([])
        if new:
            new.launch([])


def place(me, pieces, parts, shapes, before, after, small=()):
    names = sorted({name for name, _ in parts} | ({"out"} if "qkv" in dict(parts) else set()))
    old = [name for name in names if name in before]
    width = shapes["out"][-1]
    rows = width // 8
    count = len(pieces)

    def body(me, *refs):
        here = refs[:count]
        refs = refs[count + len(old) + len(after) :]
        outs = dict(zip(names, refs))
        smalls, (sems, *more) = refs[len(names) : len(names) + len(small)], refs[len(names) + len(small) :]
        waits = []
        if small:
            misc, tail_sems = more
            tail = MISC_ROWS // PIECES
            tails = []
            for r in range(PIECES):
                j = lax.bitwise_xor(me[r // HALF], jnp.int32(r % HALF))
                source = here[r // GROUP].at[r % GROUP, pl.ds(len(parts) * rows, tail)]
                item = pltpu.make_async_copy(source, misc.at[pl.ds(pl.multiple_of(j * tail, 8), tail)], tail_sems.at[r])
                item.start()
                tails.append(item)
        for index, (name, layer) in enumerate(parts):
            for r in range(PIECES):
                block, row = spot(me[r // HALF], r % HALF, rows)
                source = here[r // GROUP].at[r % GROUP, pl.ds(index * rows, rows)]
                sem = sems.at[index * PIECES + r]
                column = pl.ds(pl.multiple_of(block * width, 128), width)
                if name == "fc1":
                    item = pltpu.make_async_copy(source, outs[name].at[layer, pl.ds(row, rows), column], sem)
                    item.start()
                elif name == "fc2":
                    item = pltpu.make_async_copy(source, outs[name].at[layer, pl.ds(pl.multiple_of(block * width + row, 8), rows)], sem)
                    item.start()
                else:
                    item = pltpu.make_async_copy(source, outs["out"].at[layer, pl.ds(row, rows)], sem)

                    @pl.when(block < 3)
                    def _():
                        pltpu.make_async_copy(source, outs["qkv"].at[layer, pl.ds(row, rows), column], sem).start()

                    @pl.when(block == 3)
                    def _():
                        item.start()

                waits.append(item)
        if small:
            for item in tails:
                item.wait()
            gpos, ggain, gbias, gqvb, goutb, gb1, gb2 = smalls
            gpos[...] = misc[0 : gpos.shape[0], :]
            for index in range(ggain.shape[0]):
                base = MISC_BASE + MISC_LAYER * index
                ggain[index] = misc[base : base + 2, :]
                gbias[index] = misc[base + 2 : base + 4, :]
                gqvb[index] = misc[base + 4 : base + 6, :]
                goutb[index : index + 1, :] = misc[base + 6 : base + 7, :]
                for k in range(gb1.shape[1] // width):
                    gb1[index : index + 1, k * width : (k + 1) * width] = misc[base + 7 + k : base + 8 + k, :]
                gb2[index : index + 1, :] = misc[base + 11 : base + 12, :]
        for item in waits:
            item.wait()

    anywhere = pl.BlockSpec(memory_space=pl.ANY)
    vmem = pl.BlockSpec(memory_space=pltpu.VMEM)
    scratch = [pltpu.SemaphoreType.DMA((len(parts) * PIECES,))]
    if small:
        scratch += [pltpu.VMEM((MISC_ROWS, width), F32), pltpu.SemaphoreType.DMA((PIECES,))]
    out = pl.pallas_call(
        body,
        in_specs=[pl.BlockSpec(memory_space=pltpu.SMEM)] + [vmem] * count + [anywhere] * (len(old) + len(after)),
        out_specs=[anywhere] * len(names) + [vmem] * len(small),
        out_shape=[jax.ShapeDtypeStruct(shapes[name], F32) for name in names] + [jax.ShapeDtypeStruct(shape, F32) for shape in small],
        scratch_shapes=scratch,
        input_output_aliases={1 + count + index: names.index(name) for index, name in enumerate(old)},
        compiler_params=pltpu.CompilerParams(vmem_limit_bytes=VMEM_LIMIT),
        name="place",
    )(me, *pieces, *[before[name] for name in old], *after)
    return {**before, **dict(zip(names, out))}, list(out[len(names) :])


def on_device(sizes, tokens, kinds, interp, pos_base, ln_gain, ln_bias, w_qkv, qv_bias, w_out, out_bias, w_fc1, fc1_bias, w_fc2, fc2_bias, cotangent):
    count, rows, width = tokens.shape
    layers = w_qkv.shape[0]
    padded = -(-rows // 16) * 16
    per = 2 if count % 2 == 0 else 1
    g, d = lax.axis_index("grp"), lax.axis_index("dp")
    core, x, y = [lax.bitwise_and(lax.shift_right_logical(g, k), 1) for k in range(3)]
    low = lax.bitwise_and(d, 3)
    on_first, on_second = x * 8 + y * 4 + low, 16 + y * 8 + x * 4 + low
    me = jnp.where(core == 0, jnp.stack([on_first, on_second]), jnp.stack([on_second, on_first])).astype(jnp.int32)
    mixed, a, qkv, lse, o, c, gp, gh, xh1, r1, xh2, r2 = forward(
        kinds, tokens, interp, pos_base, ln_gain, ln_bias, w_qkv, qv_bias, w_out, out_bias, w_fc1, fc1_bias, w_fc2, fc2_bias, padded, per
    )
    small = (pos_base.shape, ln_gain.shape, ln_bias.shape, qv_bias.shape, out_bias.shape, fc1_bias.shape, fc2_bias.shape)
    shapes = {"fc1": w_fc1.shape, "fc2": w_fc2.shape, "qkv": w_qkv.shape, "out": w_out.shape}
    top = layers - 1

    def mlp(layer, dx, after):
        return mlp_back(layer, layer == top, kinds, me, dx, c, gh, gp, xh2, r2, ln_gain, w_fc1, w_fc2, padded, per, after)

    def attention(layer, dmid, sums, after):
        return attn_back(
            layer, layer == 0, kinds, me, dmid, o, qkv, lse, a, xh1, r1, ln_gain, w_qkv, w_out, gh, interp, tokens, sums, padded, per, after
        )

    order = Order()
    step = order.step
    parts = ((("fc1", 1), ("fc2", 1)), (("qkv", 1), ("fc2", 0)), (("fc1", 0),), (("qkv", 0),))
    done = {}
    rest = ()
    dmid, keep, send, sums1 = mlp(1, cotangent, [])
    order.after = [sums1]
    q0 = Round(keep, send, sizes)
    step(q0)
    step(q0)
    dx, keep, send, sums2 = attention(1, dmid, [], order.after)
    order.after = [sums2]
    q1 = Round(keep, send, sizes)
    step(q0, new=q1)
    dmid, keep, send, sums0 = mlp(0, dx, order.after)
    order.after = [sums0]
    q2 = Round(keep, send, sizes)
    step(q1, q0, new=q2)
    dx, keep, send = attention(0, dmid, [sums0, sums1, sums2], order.after)
    order.after = [keep]
    q3 = Round(keep, send, sizes)
    step(q1, q2, new=q3)
    step(q3)
    step(q1)
    step(q2, q3)
    upper = q0.merge(q1)
    step(upper)
    lower = q2.merge(q3)
    step(lower)
    step(upper)
    step(lower)
    step(upper)
    step(upper)
    step(lower)
    done, _ = place(me, upper.pieces, (("fc1", 1), ("fc2", 1), ("qkv", 1), ("fc2", 0)), shapes, {}, order.after)
    step(lower)
    step(lower)
    done, rest = place(me, lower.pieces, (("fc1", 0), ("qkv", 0)), shapes, done, [], small)
    gpos, ggain, gbias, gqvb, goutb, gb1, gb2 = rest
    return mixed, dx, gpos, ggain, gbias, done["qkv"], gqvb, done["out"], goutb, done["fc1"], gb1, done["fc2"], gb2


def solution(mesh):
    split = P(("grp", "dp"), None, None)
    return jax.shard_map(
        partial(on_device, dict(mesh.shape)),
        mesh=mesh,
        in_specs=(split, P(("grp", "dp"))) + (P(),) * 12 + (split,),
        out_specs=(split, split) + (P(),) * 11,
        check_vma=False,
    )
```

```python
from functools import partial

import jax
import jax.numpy as jnp
from jax import lax
from jax.experimental import pallas as pl
from jax.experimental.pallas import tpu as pltpu
from jax.sharding import PartitionSpec as P

HEADS = 6
HEAD = 64
BASE = 197
CROP_B = 181
CROP_C = 193
EPS = 1e-06
F32 = jnp.float32
BF16 = jnp.bfloat16
VMEM_LIMIT = 60 * 1024 * 1024
STEP_LIMIT = 16 * 1024 * 1024

ERF_P = 0.39
ERF_C = (0.11766263, 0.04569411, 0.32477995, -0.31770045, 0.44333237, -0.11376861)


def dot(a, b):
    return lax.dot_general(a, b, (((1,), (0,)), ((), ())), preferred_element_type=F32)


def dot_bt(a, b):
    return lax.dot_general(a, b, (((1,), (1,)), ((), ())), preferred_element_type=F32)


def dot_at(a, b):
    return lax.dot_general(a, b, (((0,), (0,)), ((), ())), preferred_element_type=F32)


def split3(x):
    hi = x.astype(BF16)
    rest = x - hi.astype(F32)
    mid = rest.astype(BF16)
    low = (rest - mid.astype(F32)).astype(BF16)
    return hi, mid, low


def length_of(kind):
    return jnp.where(kind == 0, BASE, jnp.where(kind == 1, CROP_B, CROP_C)).astype(jnp.int32)


def pick(ref, layer):
    row = ref[0:1].astype(F32)
    for index in range(1, ref.shape[0]):
        row = jnp.where(layer == index, ref[index : index + 1].astype(F32), row)
    return row


def norm(x):
    width = x.shape[-1]
    mean = jnp.sum(x, -1, keepdims=True) * (1.0 / width)
    centered = x - mean
    var = jnp.sum(centered * centered, -1, keepdims=True) * (1.0 / width)
    rstd = lax.rsqrt(var + EPS)
    return centered * rstd, rstd


def norm_back(dc, xhat, rstd, gain):
    width = dc.shape[-1]
    dxh = dc * gain
    m1 = jnp.sum(dxh, -1, keepdims=True) * (1.0 / width)
    m2 = jnp.sum(dxh * xhat, -1, keepdims=True) * (1.0 / width)
    return rstd * (dxh - m1 - xhat * m2)


def gelu_parts(x):
    phi = 0.5 + 0.5 * lax.erf(x * 0.5**0.5)
    return x * phi, phi + x * (jnp.exp2(x * x * (-0.5 * 1.4426950408889634)) * 0.3989422804014327)


def head_masks():
    first = lax.broadcasted_iota(jnp.int32, (1, 2 * HEAD), 1) < HEAD
    plain = [jnp.where(first, 1.0, 0.0), jnp.where(first, 0.0, 1.0)]
    return [x.astype(BF16) for x in plain], [(x * HEAD**-0.5).astype(BF16) for x in plain]


def fwd_kernel(
    kinds, tok, interp, pos, gain, bias, w_qkv, qvb, w_out, outb, w1, b1, w2, b2,
    mixed, a_o, qkv_o, lse_o, o_o, c_o, gp_o, gh_o, xh1_o, r1_o, xh2_o, r2_o,
    x_all, table_s, mid_s, o_s,
):
    layer, block = pl.program_id(0), pl.program_id(1)
    x_s = x_all.at[block]
    images, rows, width = tok.shape
    padded = x_all.shape[2]
    flat = images * padded
    heads_pair = 2 * HEAD

    @pl.when((block == 0) & (layer == 0))
    def _():
        for kind in range(interp.shape[0]):
            total = jnp.zeros((rows, width), F32)
            for part in split3(interp[kind])[::-1]:
                total += dot(part, pos[...])
            table_s[kind, 0:rows, :] = total

    @pl.when(layer == 0)
    def _():
        for i in range(images):
            kind = kinds[block * images + i]
            here = lax.broadcasted_iota(jnp.int32, (rows, 1), 0) < length_of(kind)
            h0 = tok[i].astype(F32) + table_s[kind, 0:rows, :]
            x_s[i] = jnp.zeros((padded, width), F32)
            x_s[i, 0:rows, :] = jnp.where(here, h0, 0.0)

    x = x_s[...].reshape(flat, width)
    xhat, rstd = norm(x)
    a = (xhat * gain[0, 0:1].astype(F32) + bias[0, 0:1].astype(F32)).astype(BF16)
    a_o[0] = a
    xh1_o[0] = xhat.astype(BF16)
    r1_o[0] = rstd
    bias_row = qvb[0].astype(F32)
    bias_row = jnp.concatenate([bias_row[0:1], jnp.zeros((1, width), F32), bias_row[1:2]], 1)
    qkv_o[0] = (dot(a, w_qkv[0]) + bias_row).astype(BF16)
    plain, scaled = head_masks()
    for i in range(images):
        r0 = i * padded
        length = length_of(kinds[block * images + i])
        key_ok = lax.broadcasted_iota(jnp.int32, (1, padded, 1), 1) < length
        for pair in range(HEADS // 2):
            c0 = pair * heads_pair
            q2 = qkv_o[0, r0 : r0 + padded, c0 : c0 + heads_pair]
            k2 = qkv_o[0, r0 : r0 + padded, width + c0 : width + c0 + heads_pair]
            v2 = qkv_o[0, r0 : r0 + padded, 2 * width + c0 : 2 * width + c0 + heads_pair]
            ks = jnp.concatenate([k2 * keep for keep in scaled], 0)
            vs = jnp.concatenate([v2 * keep for keep in plain], 0)
            s = jnp.where(key_ok, dot_bt(ks, q2).reshape(2, padded, padded), -1e9)
            top = jnp.max(s, 1, keepdims=True)
            e = jnp.exp(s - top)
            total = jnp.sum(e, 1, keepdims=True)
            lse_o[0, i, 2 * pair : 2 * pair + 2, :] = (top + jnp.log(total)).reshape(2, padded)
            p = (e * (1.0 / total)).astype(BF16).reshape(2 * padded, padded)
            o_s[r0 : r0 + padded, c0 : c0 + heads_pair] = dot_at(p, vs).astype(BF16)
    o = o_s[...]
    o_o[0] = o
    mid = x_s[...].reshape(flat, width) + dot(o, w_out[0]) + pick(outb, layer)
    mid_s[...] = mid
    xhat, rstd = norm(mid)
    c = (xhat * gain[0, 1:2].astype(F32) + bias[0, 1:2].astype(F32)).astype(BF16)
    c_o[0] = c
    xh2_o[0] = xhat.astype(BF16)
    r2_o[0] = rstd
    hidden = w1.shape[2]
    bias1 = pick(b1, layer)
    step = 256
    total = mid_s[...] + pick(b2, layer)
    for f in range(0, hidden, step):
        pre = dot(c, w1[0, :, f : f + step]) + bias1[:, f : f + step]
        gh, gp = gelu_parts(pre)
        gh = gh.astype(BF16)
        gh_o[0, :, f : f + step] = gh
        gp_o[0, :, f : f + step] = gp.astype(BF16)
        total += dot(gh, w2[0, f : f + step, :])
    x_s[...] = total.reshape(images, padded, width)

    @pl.when(layer == pl.num_programs(0) - 1)
    def _():
        for i in range(images):
            kind = kinds[block * images + i]
            here = lax.broadcasted_iota(jnp.int32, (rows, 1), 0) < length_of(kind)
            mixed[i] = jnp.where(here, x_s[i, 0:rows, :], 0.0).astype(BF16)


def forward(kinds, tokens, interp, pos_base, ln_gain, ln_bias, w_qkv, qv_bias, w_out, out_bias, w_fc1, fc1_bias, w_fc2, fc2_bias, padded, per):
    count, rows, width = tokens.shape
    layers, _, hidden = w_fc1.shape
    blocks = count // per
    flat = per * padded
    whole = lambda shape: pl.BlockSpec(shape, lambda l, b, k: (0,) * len(shape))
    by_layer = lambda shape: pl.BlockSpec((1,) + shape, lambda l, b, k: (l,) + (0,) * len(shape))
    read_image = pl.BlockSpec((per, rows, width), lambda l, b, k: (jnp.where(l == 0, b, blocks - 1), 0, 0))
    write_image = pl.BlockSpec((per, rows, width), lambda l, b, k: (jnp.where(l == layers - 1, b, 0), 0, 0))
    saved = lambda feat: pl.BlockSpec((1, flat, feat), lambda l, b, k: (l, b, 0))
    shape = lambda feat, dtype: jax.ShapeDtypeStruct((layers, count * padded, feat), dtype)
    return pl.pallas_call(
        fwd_kernel,
        grid_spec=pltpu.PrefetchScalarGridSpec(
            num_scalar_prefetch=1,
            grid=(layers, blocks),
            in_specs=[
                read_image,
                whole(interp.shape),
                whole(pos_base.shape),
                by_layer((2, width)),
                by_layer((2, width)),
                by_layer((width, 3 * width)),
                by_layer((2, width)),
                by_layer((width, width)),
                whole(out_bias.shape),
                by_layer((width, hidden)),
                whole(fc1_bias.shape),
                by_layer((hidden, width)),
                whole(fc2_bias.shape),
            ],
            out_specs=[
                write_image,
                saved(width),
                saved(3 * width),
                pl.BlockSpec((1, per, 8, padded), lambda l, b, k: (l, b, 0, 0)),
                saved(width),
                saved(width),
                saved(hidden),
                saved(hidden),
                saved(width),
                saved(1),
                saved(width),
                saved(1),
            ],
            scratch_shapes=[
                pltpu.VMEM((blocks, per, padded, width), F32),
                pltpu.VMEM((3, padded, width), F32),
                pltpu.VMEM((flat, width), F32),
                pltpu.VMEM((flat, width), BF16),
            ],
        ),
        out_shape=[
            jax.ShapeDtypeStruct(tokens.shape, BF16),
            shape(width, BF16),
            shape(3 * width, BF16),
            jax.ShapeDtypeStruct((layers, count, 8, padded), F32),
            shape(width, BF16),
            shape(width, BF16),
            shape(hidden, BF16),
            shape(hidden, BF16),
            shape(width, BF16),
            shape(1, F32),
            shape(width, BF16),
            shape(1, F32),
        ],
        compiler_params=pltpu.CompilerParams(vmem_limit_bytes=VMEM_LIMIT),
        name="encoder_forward",
    )(kinds, tokens, interp, pos_base, ln_gain, ln_bias, w_qkv, qv_bias, w_out, out_bias, w_fc1, fc1_bias, w_fc2, fc2_bias)


PIECES = 32
HALF = PIECES // 2
GROUP = 4
MISC_ROWS = 256
MISC_BASE = 200
MISC_LAYER = 16


def spot(me, r, rows):
    j = lax.bitwise_xor(me, jnp.int32(r))
    return lax.shift_right_logical(j, 3), pl.multiple_of(lax.bitwise_and(j, 7) * rows, 8)


def emit(me, source, keep, send, first, sems):
    rows = source.shape[1] // 8
    copies = []
    for r in range(PIECES):
        block, row = spot(me[r // HALF], r % HALF, rows)
        target = (keep, send)[r // HALF].at[r % HALF, pl.ds(first, rows)]
        copies.append(pltpu.make_async_copy(source.at[block, pl.ds(row, rows)], target, sems.at[r]))
    for item in copies:
        item.start()
    return copies


def mlp_back_kernel(top, kinds, me, dx_ref, c, gh, gp, xh, rstd, gain, w1, w2, dmid, *rest):
    if top:
        keep, send, sums, gw1, sems, gw2, dx_s = rest
    else:
        keep, send, sums, gw1, sems = rest
    block = pl.program_id(0)

    @pl.when(block == 0)
    def _():
        gw1[...] = jnp.zeros_like(gw1)
        if top:
            gw2[...] = jnp.zeros_like(gw2)
        sums[...] = jnp.zeros_like(sums)

    if top:
        images, rows, width = dx_ref.shape
        padded = dx_s.shape[1]
        for i in range(images):
            kind = kinds[block * images + i]
            here = lax.broadcasted_iota(jnp.int32, (rows, 1), 0) < length_of(kind)
            dx_s[i] = jnp.zeros((padded, width), F32)
            dx_s[i, 0:rows, :] = jnp.where(here, dx_ref[i].astype(F32), 0.0)
        dx = dx_s[...].reshape(images * padded, width)
    else:
        dx = dx_ref[...]
    flat, width = dx.shape
    hidden = w1.shape[2]
    dz = dx.astype(BF16)
    sums[11:12, :] += jnp.sum(dz.astype(F32), 0, keepdims=True)
    if top:
        for k in range(gw2.shape[0]):
            gw2[k] += dot_at(gh[0, :, k * width : (k + 1) * width], dz)
    dgh = dot_bt(dz, w2[0])
    dpre = (dgh * gp[0].astype(F32)).astype(BF16)
    column = jnp.sum(dpre.astype(F32), 0, keepdims=True)
    grad = dot_at(c[0], dpre)
    for k in range(hidden // width):
        here = slice(k * width, (k + 1) * width)
        sums[7 + k : 8 + k, :] += column[:, here]
        gw1[k] += grad[:, here]
    dc = dot_bt(dpre, w1[0])
    xhat = xh[0].astype(F32)
    sums[1:2, :] += jnp.sum(dc * xhat, 0, keepdims=True)
    sums[3:4, :] += jnp.sum(dc, 0, keepdims=True)
    dmid[...] = dx + norm_back(dc, xhat, rstd[0], gain[0, 1:2].astype(F32))

    @pl.when(block == pl.num_programs(0) - 1)
    def _():
        copies = emit(me, gw1, keep, send, 0, sems)
        if top:
            copies += emit(me, gw2, keep, send, width // 8, sems.at[pl.ds(PIECES, PIECES)])
        for item in copies:
            item.wait()


def drop(kernel, fixed, first, count):
    def body(*refs):
        return kernel(*fixed, *refs[:first], *refs[first + count :])

    return body


def pieces_of(rows, width):
    return [jax.ShapeDtypeStruct((HALF, rows, width), F32)] * 2


def mlp_back(layer, top, kinds, me, dx, c, gh, gp, xh, rstd, gain, w1, w2, padded, per, after):
    layers, width, hidden = w1.shape
    total = c.shape[1]
    flat = per * padded
    saved = lambda feat: pl.BlockSpec((1, flat, feat), lambda b, k, m: (layer, b, 0))
    param = lambda *shape: pl.BlockSpec((1,) + shape, lambda b, k, m: (layer, 0, 0))
    fixed = lambda *shape: pl.BlockSpec(shape, lambda b, k, m: (0,) * len(shape))
    rows_spec = pl.BlockSpec((flat, width), lambda b, k, m: (b, 0))
    anywhere = pl.BlockSpec(memory_space=pl.ANY)
    if top:
        dx_spec = pl.BlockSpec((per,) + dx.shape[1:], lambda b, k, m: (b, 0, 0))
        scratch = [pltpu.VMEM((hidden // width, width, width), F32), pltpu.VMEM((per, padded, width), F32)]
    else:
        dx_spec = rows_spec
        scratch = []
    out_specs = [anywhere] * 2
    out_shape = pieces_of((2 if top else 1) * hidden // PIECES, width)
    scratch = [pltpu.VMEM((hidden // width, width, width), F32), pltpu.SemaphoreType.DMA((2 * PIECES,))] + scratch
    return pl.pallas_call(
        drop(mlp_back_kernel, (top,), 11, len(after)),
        grid_spec=pltpu.PrefetchScalarGridSpec(
            num_scalar_prefetch=2,
            grid=(total // flat,),
            in_specs=[
                dx_spec,
                saved(width),
                saved(hidden) if top else anywhere,
                saved(hidden),
                saved(width),
                saved(1),
                param(2, width),
                param(width, hidden),
                param(hidden, width),
            ]
            + [anywhere] * len(after),
            out_specs=[rows_spec] + out_specs + [fixed(16, width)],
            scratch_shapes=scratch,
        ),
        out_shape=[jax.ShapeDtypeStruct((total, width), F32)] + out_shape + [jax.ShapeDtypeStruct((16, width), F32)],
        compiler_params=pltpu.CompilerParams(vmem_limit_bytes=VMEM_LIMIT),
        cost_estimate=pl.CostEstimate(flops=8 * total * width * hidden, bytes_accessed=30 * total * width, transcendentals=0),
        name="mlp_backward",
    )(kinds, me, dx, c, gh, gp, xh, rstd, gain, w1, w2, *after)


def attn_back_kernel(bottom, layers, kinds, me, dmid, o, qkv, lse, a, xh, rstd, gain, w_qkv, w_out, *rest):
    if bottom:
        interp, dx_ref, keep, send, dqkv_s, do_s, gw, sems, sums, kind_s, misc = rest[:1] + rest[2 * layers :]
        others = rest[1 : 2 * layers]
    else:
        gh_next, dx_ref, keep, send, sums, dqkv_s, do_s, gw, sems, gw2 = rest
    block = pl.program_id(0)
    images = lse.shape[1]
    flat, width = dmid.shape
    padded = flat // images

    @pl.when(block == 0)
    def _():
        gw[...] = jnp.zeros_like(gw)
        sums[...] = jnp.zeros_like(sums)
        if bottom:
            kind_s[...] = jnp.zeros_like(kind_s)
        else:
            gw2[...] = jnp.zeros_like(gw2)

    dy = dmid[...].astype(BF16)
    sums[6:7, :] += jnp.sum(dy.astype(F32), 0, keepdims=True)
    do_s[...] = dot_bt(dy, w_out[0]).astype(BF16)
    gw[3] += dot_at(o[0], dy)
    pair_width = 2 * HEAD
    plain, scaled = head_masks()
    first = lax.broadcasted_iota(jnp.int32, (1, pair_width), 1) < HEAD
    for i in range(images):
        rows = slice(i * padded, (i + 1) * padded)
        length = length_of(kinds[block * images + i])
        key_ok = lax.broadcasted_iota(jnp.int32, (1, padded, 1), 1) < length
        for pair in range(HEADS // 2):
            c0 = pair * pair_width
            part = lambda base: slice(base + c0, base + c0 + pair_width)
            q2, k2, v2 = qkv[0, rows, part(0)], qkv[0, rows, part(width)], qkv[0, rows, part(2 * width)]
            do2 = do_s[rows, part(0)]
            ks = jnp.concatenate([k2 * keep for keep in scaled], 0)
            vs = jnp.concatenate([v2 * keep for keep in plain], 0)
            s = jnp.where(key_ok, dot_bt(ks, q2).reshape(2, padded, padded), -1e9)
            p = jnp.exp(s - lse[0, i, 2 * pair : 2 * pair + 2, :].reshape(2, 1, padded))
            dp = dot_bt(vs, do2).reshape(2, padded, padded)
            delta = jnp.sum(dp * p, 1, keepdims=True)
            ds = (p * (dp - delta)).astype(BF16).reshape(2 * padded, padded)
            dv = dot(p.astype(BF16).reshape(2 * padded, padded), do2)
            dk = dot(ds, q2)
            dqkv_s[rows, part(0)] = dot_at(ds, ks).astype(BF16)
            dqkv_s[rows, part(width)] = (jnp.where(first, dk[:padded], dk[padded:]) * HEAD**-0.5).astype(BF16)
            dqkv_s[rows, part(2 * width)] = jnp.where(first, dv[:padded], dv[padded:]).astype(BF16)
    d = dqkv_s[...]
    for index in (0, 2):
        row = 4 + index // 2
        sums[row : row + 1, :] += jnp.sum(d[:, index * width : (index + 1) * width].astype(F32), 0, keepdims=True)
    grad = dot_at(a[0], d)
    for index in range(3):
        gw[index] += grad[:, index * width : (index + 1) * width]
    da = dot_bt(d, w_qkv[0])
    xhat = xh[0].astype(F32)
    sums[0:1, :] += jnp.sum(da * xhat, 0, keepdims=True)
    sums[2:3, :] += jnp.sum(da, 0, keepdims=True)
    dx = dmid[...] + norm_back(da, xhat, rstd[0], gain[0, 0:1].astype(F32))
    if bottom:
        real = dx_ref.shape[1]
        for i in range(images):
            kind = kinds[block * images + i]
            here = lax.broadcasted_iota(jnp.int32, (padded, 1), 0) < length_of(kind)
            mine = jnp.where(here, dx[i * padded : (i + 1) * padded], 0.0)
            dx_ref[i] = mine[0:real]
            kind_s[kind] += mine
    else:
        dx_ref[...] = dx
        dz = dx.astype(BF16)
        for k in range(gw2.shape[0]):
            gw2[k] += dot_at(gh_next[0, :, k * width : (k + 1) * width], dz)

    @pl.when(block == pl.num_programs(0) - 1)
    def _():
        rows = width // 8
        copies = emit(me, gw, keep, send, 0, sems)
        if not bottom:
            copies += emit(me, gw2, keep, send, rows, sems.at[pl.ds(PIECES, PIECES)])
        if bottom:
            total = jnp.zeros((real, width), F32)
            for kind in range(interp.shape[0]):
                hi, mid, _ = split3(interp[kind])
                ghi, gmid, _ = split3(kind_s[kind, 0:real, :])
                total += dot_at(mid, ghi) + dot_at(hi, gmid) + dot_at(hi, ghi)
            misc[...] = jnp.zeros_like(misc)
            misc[0:real, :] = total
            misc[MISC_BASE : MISC_BASE + 16, :] = sums[...] + others[0][...]
            for layer in range(1, layers):
                start = MISC_BASE + MISC_LAYER * layer
                misc[start : start + 16, :] = others[2 * layer - 1][...] + others[2 * layer][...]
            tail = misc.shape[0] // PIECES
            for r in range(PIECES):
                j = lax.bitwise_xor(me[r // HALF], jnp.int32(r % HALF))
                target = (keep, send)[r // HALF].at[r % HALF, pl.ds(rows, tail)]
                item = pltpu.make_async_copy(misc.at[pl.ds(pl.multiple_of(j * tail, 8), tail)], target, sems.at[PIECES + r])
                item.start()
                copies.append(item)
        for item in copies:
            item.wait()


def attn_back(layer, bottom, kinds, me, dmid, o, qkv, lse, a, xh, rstd, gain, w_qkv, w_out, gh, interp, like, others, padded, per, after):
    width = dmid.shape[1]
    total = dmid.shape[0]
    layers = w_qkv.shape[0]
    flat = per * padded
    blocks = total // flat
    saved = lambda feat: pl.BlockSpec((1, flat, feat), lambda b, k, m: (layer, b, 0))
    param = lambda *shape: pl.BlockSpec((1,) + shape, lambda b, k, m: (layer, 0, 0))
    fixed = lambda *shape: pl.BlockSpec(shape, lambda b, k, m: (0,) * len(shape))
    anywhere = pl.BlockSpec(memory_space=pl.ANY)
    in_specs = [
        pl.BlockSpec((flat, width), lambda b, k, m: (b, 0)),
        saved(width),
        saved(3 * width),
        pl.BlockSpec((1, per, 8, padded), lambda b, k, m: (layer, b, 0, 0)),
        saved(width),
        saved(width),
        saved(1),
        param(2, width),
        param(width, 3 * width),
        param(width, width),
    ]
    tail = MISC_ROWS // PIECES if bottom else width // 8
    grads = pieces_of(width // 8 + tail, width)
    scratch = [
        pltpu.VMEM((flat, 3 * width), BF16),
        pltpu.VMEM((flat, width), BF16),
        pltpu.VMEM((4, width, width), F32),
        pltpu.SemaphoreType.DMA((2 * PIECES,)),
    ]
    args = [kinds, me, dmid, o, qkv, lse, a, xh, rstd, gain, w_qkv, w_out]
    if bottom:
        rows = like.shape[1]
        in_specs += [fixed(*interp.shape)] + [fixed(16, width)] * len(others)
        args += [interp] + others
        out_specs = [pl.BlockSpec((per, rows, width), lambda b, k, m: (b, 0, 0))] + [anywhere] * 2
        out_shape = [jax.ShapeDtypeStruct(like.shape, F32)] + grads
        scratch += [pltpu.VMEM((16, width), F32), pltpu.VMEM((3, padded, width), F32), pltpu.VMEM((MISC_ROWS, width), F32)]
    else:
        hidden = gh.shape[2]
        in_specs += [pl.BlockSpec((1, flat, hidden), lambda b, k, m: (layer - 1, b, 0))]
        args += [gh]
        out_specs = [pl.BlockSpec((flat, width), lambda b, k, m: (b, 0))] + [anywhere] * 2 + [fixed(16, width)]
        out_shape = [jax.ShapeDtypeStruct((total, width), F32)] + grads + [jax.ShapeDtypeStruct((16, width), F32)]
        scratch += [pltpu.VMEM((hidden // width, width, width), F32)]
    first = len(args)
    in_specs += [anywhere] * len(after)
    args += after
    return pl.pallas_call(
        drop(attn_back_kernel, (bottom, layers), first, len(after)),
        grid_spec=pltpu.PrefetchScalarGridSpec(
            num_scalar_prefetch=2,
            grid=(blocks,),
            in_specs=in_specs,
            out_specs=out_specs,
            scratch_shapes=scratch,
        ),
        out_shape=out_shape,
        compiler_params=pltpu.CompilerParams(vmem_limit_bytes=VMEM_LIMIT),
        cost_estimate=pl.CostEstimate(flops=32 * total * width * width, bytes_accessed=30 * total * width, transcendentals=0),
        name="attention_backward",
    )(*args)


def exchange(x, axis, bits, size):
    return lax.ppermute(x, axis, [(i, i ^ bits) for i in range(size)])


def combine(tasks, after, through):
    args = sum([list(inputs) for _, inputs, _ in tasks], [])
    shapes = sum([list(results) for _, _, results in tasks], [])
    parts = [(count,) + x.shape[1:] for x, _, count in args]

    def body(*refs):
        outs = refs[len(args) + len(through) + len(after) :]
        ins, sems = outs[len(shapes) + len(through) : -1], outs[-1]
        copies = []
        for k, (_, first, count) in enumerate(args):
            copies.append(pltpu.make_async_copy(refs[k].at[pl.ds(first, count)], ins[k], sems.at[k]))
            copies[-1].start()
        for function, inputs, results in tasks:
            for item in copies[: len(inputs)]:
                item.wait()
            function(ins[: len(inputs)], outs[: len(results)])
            copies, ins, outs = copies[len(inputs) :], ins[len(inputs) :], outs[len(results) :]

    vmem = pl.BlockSpec(memory_space=pltpu.VMEM)
    anywhere = pl.BlockSpec(memory_space=pl.ANY)
    moved = sum(x.size for x, _, _ in args) * 4
    out = pl.pallas_call(
        body,
        in_specs=[anywhere] * (len(args) + len(through) + len(after)),
        out_specs=[vmem] * len(shapes) + [anywhere] * len(through),
        out_shape=[jax.ShapeDtypeStruct(shape, F32) for shape in shapes] + [jax.ShapeDtypeStruct(x.shape, F32) for x in through],
        scratch_shapes=[pltpu.VMEM(part, F32) for part in parts] + [pltpu.SemaphoreType.DMA((max(len(args), 1),))],
        input_output_aliases={len(args) + k: len(shapes) + k for k in range(len(through))},
        compiler_params=pltpu.CompilerParams(vmem_limit_bytes=STEP_LIMIT),
        cost_estimate=pl.CostEstimate(flops=moved, bytes_accessed=2 * moved, transcendentals=0),
        name="combine",
    )(*[x for x, _, _ in args], *through, *after)
    result = []
    for _, _, results in tasks:
        result.append(list(out[: len(results)]))
        out = out[len(results) :]
    return result, list(out)


def sum_of(refs):
    total = refs[0][...]
    for ref in refs[1:]:
        total = total + ref[...]
    return total


def add(ins, outs):
    outs[0][...] = sum_of(ins)


def split_four(ins, outs):
    start = 0
    for group in range(0, len(ins), 4):
        rows = ins[group].shape[1]
        for k, out in enumerate(outs):
            out[start : start + rows] = sum_of([ref.at[k] for ref in ins[group : group + 4]])
        start += rows


def total_of(ins, outs):
    start = 0
    for a, b, c, d in zip(ins[::4], ins[1::4], ins[2::4], ins[3::4]):
        rows = a.shape[0]
        outs[0][start : start + rows] = (a[...] + b[...]) + (c[...] + d[...])
        start += rows


def stack(ins, outs):
    rows = ins[0].shape[0]
    for k in range(4):
        outs[0][k, :rows] = ins[k][...]
        if len(ins) > 4:
            outs[0][k, rows:] = ins[4][k]


class Round:
    def __init__(self, keep, send, sizes):
        self.keep, self.send, self.sizes, self.stage = keep, send, sizes, 0
        self.shape = keep.shape[1:]
        self.more = []
        self.parked = False

    def merge(self, other):
        assert self.stage == other.stage
        self.more = list(other.terms if self.stage == 3 else [other.keep, *other.got])
        self.shape = (self.shape[0] + other.shape[0], self.shape[1])
        return self

    def absorb(self, other):
        assert self.stage == 5 and other.parked
        self.more = [other.own]
        self.shape = (self.shape[0] + other.shape[0], self.shape[1])
        return self

    def across(self, x, which):
        bits = lambda i: (2, 4)[(i & 1) ^ which]
        return lax.ppermute(x, "grp", [(i, i ^ bits(i)) for i in range(self.sizes["grp"])])

    def swap(self, x, axis, bits):
        return exchange(x, axis, bits, self.sizes[axis])

    def tasks(self):
        stage, n = self.stage, self.shape
        if stage in (1, 2):
            half = PIECES >> (stage + 1)
            return [(add, [(x, half, half) for x in self.terms], ((half,) + n,))]
        if stage == 3:
            args, self.more = self.terms + self.more, []
            return [(split_four, [(x, 0, 4) for x in args], (n,) * 4)]
        if stage not in (4, 5):
            return []
        args, self.more = [self.keep, *self.got, *self.more], []
        args = [(x, 0, x.shape[0]) for x in args]
        if stage == 4:
            return [(total_of, args, (n,))]
        if stage == 5:
            return [(stack, args, ((4,) + n,))]
        return []

    def launch(self, done):
        stage = self.stage
        self.stage += 1
        if stage == 0:
            self.terms = [self.keep, self.swap(self.send, "grp", 1)]
        elif stage <= 2:
            self.terms = self.terms + [self.across(done[0], stage - 1)]
        elif stage == 3:
            self.keep, self.got = done[0], [self.swap(done[k], "dp", k) for k in range(1, 4)]
        elif stage == 4:
            total = done[0]
            for axis, bit in (("grp", 8), ("dp", 4)):
                while bit < self.sizes[axis]:
                    total = total + self.swap(total, axis, bit)
                    bit *= 2
            self.keep, self.got = total, [self.swap(total, "dp", k) for k in range(1, 4)]
        elif stage == 5:
            self.own = done[0]
            if self.parked:
                return
            self.second, self.first = self.across(self.own, 1), self.across(self.own, 0)
            self.pieces = [self.own, self.second, self.first, None, self.swap(self.own, "grp", 1)]
        elif stage == 6:
            self.pieces[3] = self.across(self.second, 0)
            self.pieces += [self.swap(self.second, "grp", 1), self.swap(self.first, "grp", 1)]
        else:
            self.pieces.append(self.swap(self.pieces[3], "grp", 1))


class Order:
    def __init__(self):
        self.after = []

    def step(self, *rounds, new=None):
        tasks = [item.tasks() for item in rounds]
        flat = sum(tasks, [])
        if flat:
            done, through = combine(flat, [] if new else self.after, [new.send] if new else [])
            self.after = [done[0][0]]
            for item, own in zip(rounds, tasks):
                item.launch([x for result in done[: len(own)] for x in result])
                done = done[len(own) :]
            if new:
                new.send = through[0]
        else:
            for item in rounds:
                item.launch([])
        if new:
            new.launch([])


def place(me, pieces, parts, shapes, before, after, small=()):
    names = sorted({name for name, _ in parts} | ({"out"} if "qkv" in dict(parts) else set()))
    old = [name for name in names if name in before]
    width = shapes["out"][-1]
    rows = width // 8
    count = len(pieces)

    def body(me, *refs):
        here = refs[:count]
        refs = refs[count + len(old) + len(after) :]
        outs = dict(zip(names, refs))
        smalls, (sems, *more) = refs[len(names) : len(names) + len(small)], refs[len(names) + len(small) :]
        waits = []
        if small:
            misc, tail_sems = more
            tail = MISC_ROWS // PIECES
            tails = []
            for r in range(PIECES):
                j = lax.bitwise_xor(me[r // HALF], jnp.int32(r % HALF))
                source = here[r // GROUP].at[r % GROUP, pl.ds(len(parts) * rows, tail)]
                item = pltpu.make_async_copy(source, misc.at[pl.ds(pl.multiple_of(j * tail, 8), tail)], tail_sems.at[r])
                item.start()
                tails.append(item)
        for index, (name, layer) in enumerate(parts):
            for r in range(PIECES):
                block, row = spot(me[r // HALF], r % HALF, rows)
                source = here[r // GROUP].at[r % GROUP, pl.ds(index * rows, rows)]
                sem = sems.at[index * PIECES + r]
                column = pl.ds(pl.multiple_of(block * width, 128), width)
                if name == "fc1":
                    item = pltpu.make_async_copy(source, outs[name].at[layer, pl.ds(row, rows), column], sem)
                    item.start()
                elif name == "fc2":
                    item = pltpu.make_async_copy(source, outs[name].at[layer, pl.ds(pl.multiple_of(block * width + row, 8), rows)], sem)
                    item.start()
                else:
                    item = pltpu.make_async_copy(source, outs["out"].at[layer, pl.ds(row, rows)], sem)

                    @pl.when(block < 3)
                    def _():
                        pltpu.make_async_copy(source, outs["qkv"].at[layer, pl.ds(row, rows), column], sem).start()

                    @pl.when(block == 3)
                    def _():
                        item.start()

                waits.append(item)
        if small:
            for item in tails:
                item.wait()
            gpos, ggain, gbias, gqvb, goutb, gb1, gb2 = smalls
            gpos[...] = misc[0 : gpos.shape[0], :]
            for index in range(ggain.shape[0]):
                base = MISC_BASE + MISC_LAYER * index
                ggain[index] = misc[base : base + 2, :]
                gbias[index] = misc[base + 2 : base + 4, :]
                gqvb[index] = misc[base + 4 : base + 6, :]
                goutb[index : index + 1, :] = misc[base + 6 : base + 7, :]
                for k in range(gb1.shape[1] // width):
                    gb1[index : index + 1, k * width : (k + 1) * width] = misc[base + 7 + k : base + 8 + k, :]
                gb2[index : index + 1, :] = misc[base + 11 : base + 12, :]
        for item in waits:
            item.wait()

    anywhere = pl.BlockSpec(memory_space=pl.ANY)
    vmem = pl.BlockSpec(memory_space=pltpu.VMEM)
    scratch = [pltpu.SemaphoreType.DMA((len(parts) * PIECES,))]
    if small:
        scratch += [pltpu.VMEM((MISC_ROWS, width), F32), pltpu.SemaphoreType.DMA((PIECES,))]
    out = pl.pallas_call(
        body,
        in_specs=[pl.BlockSpec(memory_space=pltpu.SMEM)] + [vmem] * count + [anywhere] * (len(old) + len(after)),
        out_specs=[anywhere] * len(names) + [vmem] * len(small),
        out_shape=[jax.ShapeDtypeStruct(shapes[name], F32) for name in names] + [jax.ShapeDtypeStruct(shape, F32) for shape in small],
        scratch_shapes=scratch,
        input_output_aliases={1 + count + index: names.index(name) for index, name in enumerate(old)},
        compiler_params=pltpu.CompilerParams(vmem_limit_bytes=2 * STEP_LIMIT),
        name="place",
    )(me, *pieces, *[before[name] for name in old], *after)
    return {**before, **dict(zip(names, out))}, list(out[len(names) :])


def on_device(sizes, tokens, kinds, interp, pos_base, ln_gain, ln_bias, w_qkv, qv_bias, w_out, out_bias, w_fc1, fc1_bias, w_fc2, fc2_bias, cotangent):
    count, rows, width = tokens.shape
    layers = w_qkv.shape[0]
    padded = -(-rows // 16) * 16
    per = 2 if count % 2 == 0 else 1
    g, d = lax.axis_index("grp"), lax.axis_index("dp")
    core, x, y = [lax.bitwise_and(lax.shift_right_logical(g, k), 1) for k in range(3)]
    low = lax.bitwise_and(d, 3)
    on_first, on_second = x * 8 + y * 4 + low, 16 + y * 8 + x * 4 + low
    me = jnp.where(core == 0, jnp.stack([on_first, on_second]), jnp.stack([on_second, on_first])).astype(jnp.int32)
    mixed, a, qkv, lse, o, c, gp, gh, xh1, r1, xh2, r2 = forward(
        kinds, tokens, interp, pos_base, ln_gain, ln_bias, w_qkv, qv_bias, w_out, out_bias, w_fc1, fc1_bias, w_fc2, fc2_bias, padded, per
    )
    small = (pos_base.shape, ln_gain.shape, ln_bias.shape, qv_bias.shape, out_bias.shape, fc1_bias.shape, fc2_bias.shape)
    shapes = {"fc1": w_fc1.shape, "fc2": w_fc2.shape, "qkv": w_qkv.shape, "out": w_out.shape}
    top = layers - 1

    def mlp(layer, dx, after):
        return mlp_back(layer, layer == top, kinds, me, dx, c, gh, gp, xh2, r2, ln_gain, w_fc1, w_fc2, padded, per, after)

    def attention(layer, dmid, sums, after):
        return attn_back(
            layer, layer == 0, kinds, me, dmid, o, qkv, lse, a, xh1, r1, ln_gain, w_qkv, w_out, gh, interp, tokens, sums, padded, per, after
        )

    order = Order()
    step = order.step
    parts = ((("fc1", 1), ("fc2", 1)), (("qkv", 1), ("fc2", 0)), (("fc1", 0),), (("qkv", 0),))
    done = {}
    rest = ()
    dmid, keep, send, sums1 = mlp(1, cotangent, [])
    q0 = Round(keep, send, sizes)
    step(q0)
    step(q0)
    dx, keep, send, sums2 = attention(1, dmid, [], order.after)
    q1 = Round(keep, send, sizes)
    step(q0, new=q1)
    dmid, keep, send, sums0 = mlp(0, dx, order.after)
    q2 = Round(keep, send, sizes)
    step(q1, q0, new=q2)
    dx, keep, send = attention(0, dmid, [sums0, sums1, sums2], order.after)
    q3 = Round(keep, send, sizes)
    step(q1, q2, q0, new=q3)
    step(q3)
    q0.parked = True
    step(q1, q0)
    step(q2, q3)
    lower = q2.merge(q3)
    step(lower, q1)
    step(lower)
    upper = q1.absorb(q0)
    step(upper)
    step(lower)
    step(upper)
    step(upper)
    done, _ = place(me, upper.pieces, (("qkv", 1), ("fc2", 0), ("fc1", 1), ("fc2", 1)), shapes, {}, order.after)
    step(lower)
    step(lower)
    done, rest = place(me, lower.pieces, (("fc1", 0), ("qkv", 0)), shapes, done, [], small)
    gpos, ggain, gbias, gqvb, goutb, gb1, gb2 = rest
    return mixed, dx, gpos, ggain, gbias, done["qkv"], gqvb, done["out"], goutb, done["fc1"], gb1, done["fc2"], gb2


def solution(mesh):
    split = P(("grp", "dp"), None, None)
    return jax.shard_map(
        partial(on_device, dict(mesh.shape)),
        mesh=mesh,
        in_specs=(split, P(("grp", "dp"))) + (P(),) * 12 + (split,),
        out_specs=(split, split) + (P(),) * 11,
        check_vma=False,
    )
```

```python
from functools import partial

import jax
import jax.numpy as jnp
from jax import lax
from jax.experimental import pallas as pl
from jax.experimental.pallas import tpu as pltpu
from jax.sharding import PartitionSpec as P

HEADS = 6
HEAD = 64
BASE = 197
CROP_B = 181
CROP_C = 193
EPS = 1e-06
F32 = jnp.float32
BF16 = jnp.bfloat16
VMEM_LIMIT = 60 * 1024 * 1024
STEP_LIMIT = 16 * 1024 * 1024

ERF_P = 0.39
ERF_C = (0.11766263, 0.04569411, 0.32477995, -0.31770045, 0.44333237, -0.11376861)


def dot(a, b):
    return lax.dot_general(a, b, (((1,), (0,)), ((), ())), preferred_element_type=F32)


def dot_bt(a, b):
    return lax.dot_general(a, b, (((1,), (1,)), ((), ())), preferred_element_type=F32)


def dot_at(a, b):
    return lax.dot_general(a, b, (((0,), (0,)), ((), ())), preferred_element_type=F32)


def split3(x):
    hi = x.astype(BF16)
    rest = x - hi.astype(F32)
    mid = rest.astype(BF16)
    low = (rest - mid.astype(F32)).astype(BF16)
    return hi, mid, low


def length_of(kind):
    return jnp.where(kind == 0, BASE, jnp.where(kind == 1, CROP_B, CROP_C)).astype(jnp.int32)


def pick(ref, layer):
    row = ref[0:1].astype(F32)
    for index in range(1, ref.shape[0]):
        row = jnp.where(layer == index, ref[index : index + 1].astype(F32), row)
    return row


def norm(x):
    width = x.shape[-1]
    mean = jnp.sum(x, -1, keepdims=True) * (1.0 / width)
    centered = x - mean
    var = jnp.sum(centered * centered, -1, keepdims=True) * (1.0 / width)
    rstd = lax.rsqrt(var + EPS)
    return centered * rstd, rstd


def norm_back(dc, xhat, rstd, gain):
    width = dc.shape[-1]
    dxh = dc * gain
    m1 = jnp.sum(dxh, -1, keepdims=True) * (1.0 / width)
    m2 = jnp.sum(dxh * xhat, -1, keepdims=True) * (1.0 / width)
    return rstd * (dxh - m1 - xhat * m2)


def gelu_parts(x):
    phi = 0.5 + 0.5 * lax.erf(x * 0.5**0.5)
    return x * phi, phi + x * (jnp.exp2(x * x * (-0.5 * 1.4426950408889634)) * 0.3989422804014327)


def head_masks():
    first = lax.broadcasted_iota(jnp.int32, (1, 2 * HEAD), 1) < HEAD
    plain = [jnp.where(first, 1.0, 0.0), jnp.where(first, 0.0, 1.0)]
    return [x.astype(BF16) for x in plain], [(x * HEAD**-0.5).astype(BF16) for x in plain]


def fwd_kernel(
    kinds, tok, interp, pos, gain, bias, w_qkv, qvb, w_out, outb, w1, b1, w2, b2,
    mixed, a_o, qkv_o, lse_o, o_o, c_o, gp_o, gh_o, xh1_o, r1_o, xh2_o, r2_o,
    x_all, table_s, mid_s, o_s,
):
    layer, block = pl.program_id(0), pl.program_id(1)
    x_s = x_all.at[block]
    images, rows, width = tok.shape
    padded = x_all.shape[2]
    flat = images * padded
    heads_pair = 2 * HEAD

    @pl.when((block == 0) & (layer == 0))
    def _():
        for kind in range(interp.shape[0]):
            total = jnp.zeros((rows, width), F32)
            for part in split3(interp[kind])[::-1]:
                total += dot(part, pos[...])
            table_s[kind, 0:rows, :] = total

    @pl.when(layer == 0)
    def _():
        for i in range(images):
            kind = kinds[block * images + i]
            here = lax.broadcasted_iota(jnp.int32, (rows, 1), 0) < length_of(kind)
            h0 = tok[i].astype(F32) + table_s[kind, 0:rows, :]
            x_s[i] = jnp.zeros((padded, width), F32)
            x_s[i, 0:rows, :] = jnp.where(here, h0, 0.0)

    x = x_s[...].reshape(flat, width)
    xhat, rstd = norm(x)
    a = (xhat * gain[0, 0:1].astype(F32) + bias[0, 0:1].astype(F32)).astype(BF16)
    a_o[0] = a
    xh1_o[0] = xhat.astype(BF16)
    r1_o[0] = rstd
    bias_row = qvb[0].astype(F32)
    bias_row = jnp.concatenate([bias_row[0:1], jnp.zeros((1, width), F32), bias_row[1:2]], 1)
    qkv_o[0] = (dot(a, w_qkv[0]) + bias_row).astype(BF16)
    plain, scaled = head_masks()
    for i in range(images):
        r0 = i * padded
        length = length_of(kinds[block * images + i])
        key_ok = lax.broadcasted_iota(jnp.int32, (1, padded, 1), 1) < length
        for pair in range(HEADS // 2):
            c0 = pair * heads_pair
            q2 = qkv_o[0, r0 : r0 + padded, c0 : c0 + heads_pair]
            k2 = qkv_o[0, r0 : r0 + padded, width + c0 : width + c0 + heads_pair]
            v2 = qkv_o[0, r0 : r0 + padded, 2 * width + c0 : 2 * width + c0 + heads_pair]
            ks = jnp.concatenate([k2 * keep for keep in scaled], 0)
            vs = jnp.concatenate([v2 * keep for keep in plain], 0)
            s = jnp.where(key_ok, dot_bt(ks, q2).reshape(2, padded, padded), -1e9)
            top = jnp.max(s, 1, keepdims=True)
            e = jnp.exp(s - top)
            total = jnp.sum(e, 1, keepdims=True)
            lse_o[0, i, 2 * pair : 2 * pair + 2, :] = (top + jnp.log(total)).reshape(2, padded)
            p = (e * (1.0 / total)).astype(BF16).reshape(2 * padded, padded)
            o_s[r0 : r0 + padded, c0 : c0 + heads_pair] = dot_at(p, vs).astype(BF16)
    o = o_s[...]
    o_o[0] = o
    mid = x_s[...].reshape(flat, width) + dot(o, w_out[0]) + pick(outb, layer)
    mid_s[...] = mid
    xhat, rstd = norm(mid)
    c = (xhat * gain[0, 1:2].astype(F32) + bias[0, 1:2].astype(F32)).astype(BF16)
    c_o[0] = c
    xh2_o[0] = xhat.astype(BF16)
    r2_o[0] = rstd
    hidden = w1.shape[2]
    bias1 = pick(b1, layer)
    step = 256
    total = mid_s[...] + pick(b2, layer)
    for f in range(0, hidden, step):
        pre = dot(c, w1[0, :, f : f + step]) + bias1[:, f : f + step]
        gh, gp = gelu_parts(pre)
        gh = gh.astype(BF16)
        gh_o[0, :, f : f + step] = gh
        gp_o[0, :, f : f + step] = gp.astype(BF16)
        total += dot(gh, w2[0, f : f + step, :])
    x_s[...] = total.reshape(images, padded, width)

    @pl.when(layer == pl.num_programs(0) - 1)
    def _():
        for i in range(images):
            kind = kinds[block * images + i]
            here = lax.broadcasted_iota(jnp.int32, (rows, 1), 0) < length_of(kind)
            mixed[i] = jnp.where(here, x_s[i, 0:rows, :], 0.0).astype(BF16)


def forward(kinds, tokens, interp, pos_base, ln_gain, ln_bias, w_qkv, qv_bias, w_out, out_bias, w_fc1, fc1_bias, w_fc2, fc2_bias, padded, per):
    count, rows, width = tokens.shape
    layers, _, hidden = w_fc1.shape
    blocks = count // per
    flat = per * padded
    whole = lambda shape: pl.BlockSpec(shape, lambda l, b, k: (0,) * len(shape))
    by_layer = lambda shape: pl.BlockSpec((1,) + shape, lambda l, b, k: (l,) + (0,) * len(shape))
    read_image = pl.BlockSpec((per, rows, width), lambda l, b, k: (jnp.where(l == 0, b, blocks - 1), 0, 0))
    write_image = pl.BlockSpec((per, rows, width), lambda l, b, k: (jnp.where(l == layers - 1, b, 0), 0, 0))
    saved = lambda feat: pl.BlockSpec((1, flat, feat), lambda l, b, k: (l, b, 0))
    shape = lambda feat, dtype: jax.ShapeDtypeStruct((layers, count * padded, feat), dtype)
    return pl.pallas_call(
        fwd_kernel,
        grid_spec=pltpu.PrefetchScalarGridSpec(
            num_scalar_prefetch=1,
            grid=(layers, blocks),
            in_specs=[
                read_image,
                whole(interp.shape),
                whole(pos_base.shape),
                by_layer((2, width)),
                by_layer((2, width)),
                by_layer((width, 3 * width)),
                by_layer((2, width)),
                by_layer((width, width)),
                whole(out_bias.shape),
                by_layer((width, hidden)),
                whole(fc1_bias.shape),
                by_layer((hidden, width)),
                whole(fc2_bias.shape),
            ],
            out_specs=[
                write_image,
                saved(width),
                saved(3 * width),
                pl.BlockSpec((1, per, 8, padded), lambda l, b, k: (l, b, 0, 0)),
                saved(width),
                saved(width),
                saved(hidden),
                saved(hidden),
                saved(width),
                saved(1),
                saved(width),
                saved(1),
            ],
            scratch_shapes=[
                pltpu.VMEM((blocks, per, padded, width), F32),
                pltpu.VMEM((3, padded, width), F32),
                pltpu.VMEM((flat, width), F32),
                pltpu.VMEM((flat, width), BF16),
            ],
        ),
        out_shape=[
            jax.ShapeDtypeStruct(tokens.shape, BF16),
            shape(width, BF16),
            shape(3 * width, BF16),
            jax.ShapeDtypeStruct((layers, count, 8, padded), F32),
            shape(width, BF16),
            shape(width, BF16),
            shape(hidden, BF16),
            shape(hidden, BF16),
            shape(width, BF16),
            shape(1, F32),
            shape(width, BF16),
            shape(1, F32),
        ],
        compiler_params=pltpu.CompilerParams(vmem_limit_bytes=VMEM_LIMIT),
        name="encoder_forward",
    )(kinds, tokens, interp, pos_base, ln_gain, ln_bias, w_qkv, qv_bias, w_out, out_bias, w_fc1, fc1_bias, w_fc2, fc2_bias)


PIECES = 32
HALF = PIECES // 2
GROUP = 4
MISC_ROWS = 256
MISC_BASE = 200
MISC_LAYER = 16


def spot(me, r, rows):
    j = lax.bitwise_xor(me, jnp.int32(r))
    return lax.shift_right_logical(j, 3), pl.multiple_of(lax.bitwise_and(j, 7) * rows, 8)


def moves(me, source, keep, send, first, sems):
    rows = source.shape[1] // 8
    copies = []
    for r in range(PIECES):
        block, row = spot(me[r // HALF], r % HALF, rows)
        target = (keep, send)[r // HALF].at[r % HALF, pl.ds(first, rows)]
        copies.append(pltpu.make_async_copy(source.at[block, pl.ds(row, rows)], target, sems.at[r]))
    return copies


def emit(me, source, keep, send, first, sems):
    copies = moves(me, source, keep, send, first, sems)
    for item in copies:
        item.start()
    return copies


def mlp_back_kernel(top, kinds, me, dx_ref, c, gh, gp, xh, rstd, gain, w1, w2, dmid, *rest):
    if top:
        keep, send, sums, gw1, sems, gw2, dx_s = rest
    else:
        keep, send, sums, gw1, sems = rest
    block = pl.program_id(0)

    @pl.when(block == 0)
    def _():
        gw1[...] = jnp.zeros_like(gw1)
        if top:
            gw2[...] = jnp.zeros_like(gw2)
        sums[...] = jnp.zeros_like(sums)

    if top:
        images, rows, width = dx_ref.shape
        padded = dx_s.shape[1]
        for i in range(images):
            kind = kinds[block * images + i]
            here = lax.broadcasted_iota(jnp.int32, (rows, 1), 0) < length_of(kind)
            dx_s[i] = jnp.zeros((padded, width), F32)
            dx_s[i, 0:rows, :] = jnp.where(here, dx_ref[i].astype(F32), 0.0)
        dx = dx_s[...].reshape(images * padded, width)
    else:
        dx = dx_ref[...]
    flat, width = dx.shape
    hidden = w1.shape[2]
    dz = dx.astype(BF16)
    sums[11:12, :] += jnp.sum(dz.astype(F32), 0, keepdims=True)
    if top:
        for k in range(gw2.shape[0]):
            gw2[k] += dot_at(gh[0, :, k * width : (k + 1) * width], dz)
    dgh = dot_bt(dz, w2[0])
    dpre = (dgh * gp[0].astype(F32)).astype(BF16)
    column = jnp.sum(dpre.astype(F32), 0, keepdims=True)
    grad = dot_at(c[0], dpre)
    for k in range(hidden // width):
        here = slice(k * width, (k + 1) * width)
        sums[7 + k : 8 + k, :] += column[:, here]
        gw1[k] += grad[:, here]
    last = block == pl.num_programs(0) - 1

    @pl.when(last)
    def _():
        emit(me, gw1, keep, send, 0, sems)
        if top:
            emit(me, gw2, keep, send, width // 8, sems.at[pl.ds(PIECES, PIECES)])

    dc = dot_bt(dpre, w1[0])
    xhat = xh[0].astype(F32)
    sums[1:2, :] += jnp.sum(dc * xhat, 0, keepdims=True)
    sums[3:4, :] += jnp.sum(dc, 0, keepdims=True)
    dmid[...] = dx + norm_back(dc, xhat, rstd[0], gain[0, 1:2].astype(F32))

    @pl.when(last)
    def _():
        copies = moves(me, gw1, keep, send, 0, sems)
        if top:
            copies += moves(me, gw2, keep, send, width // 8, sems.at[pl.ds(PIECES, PIECES)])
        for item in copies:
            item.wait()


def drop(kernel, fixed, first, count):
    def body(*refs):
        return kernel(*fixed, *refs[:first], *refs[first + count :])

    return body


def pieces_of(rows, width):
    return [jax.ShapeDtypeStruct((HALF, rows, width), F32)] * 2


def mlp_back(layer, top, kinds, me, dx, c, gh, gp, xh, rstd, gain, w1, w2, padded, per, after):
    layers, width, hidden = w1.shape
    total = c.shape[1]
    flat = per * padded
    saved = lambda feat: pl.BlockSpec((1, flat, feat), lambda b, k, m: (layer, b, 0))
    param = lambda *shape: pl.BlockSpec((1,) + shape, lambda b, k, m: (layer, 0, 0))
    fixed = lambda *shape: pl.BlockSpec(shape, lambda b, k, m: (0,) * len(shape))
    rows_spec = pl.BlockSpec((flat, width), lambda b, k, m: (b, 0))
    anywhere = pl.BlockSpec(memory_space=pl.ANY)
    if top:
        dx_spec = pl.BlockSpec((per,) + dx.shape[1:], lambda b, k, m: (b, 0, 0))
        scratch = [pltpu.VMEM((hidden // width, width, width), F32), pltpu.VMEM((per, padded, width), F32)]
    else:
        dx_spec = rows_spec
        scratch = []
    out_specs = [anywhere] * 2
    out_shape = pieces_of((2 if top else 1) * hidden // PIECES, width)
    scratch = [pltpu.VMEM((hidden // width, width, width), F32), pltpu.SemaphoreType.DMA((2 * PIECES,))] + scratch
    return pl.pallas_call(
        drop(mlp_back_kernel, (top,), 11, len(after)),
        grid_spec=pltpu.PrefetchScalarGridSpec(
            num_scalar_prefetch=2,
            grid=(total // flat,),
            in_specs=[
                dx_spec,
                saved(width),
                saved(hidden) if top else anywhere,
                saved(hidden),
                saved(width),
                saved(1),
                param(2, width),
                param(width, hidden),
                param(hidden, width),
            ]
            + [anywhere] * len(after),
            out_specs=[rows_spec] + out_specs + [fixed(16, width)],
            scratch_shapes=scratch,
        ),
        out_shape=[jax.ShapeDtypeStruct((total, width), F32)] + out_shape + [jax.ShapeDtypeStruct((16, width), F32)],
        compiler_params=pltpu.CompilerParams(vmem_limit_bytes=VMEM_LIMIT),
        cost_estimate=pl.CostEstimate(flops=8 * total * width * hidden, bytes_accessed=30 * total * width, transcendentals=0),
        name="mlp_backward",
    )(kinds, me, dx, c, gh, gp, xh, rstd, gain, w1, w2, *after)


def attn_back_kernel(bottom, layers, kinds, me, dmid, o, qkv, lse, a, xh, rstd, gain, w_qkv, w_out, *rest):
    if bottom:
        interp, dx_ref, keep, send, dqkv_s, do_s, gw, sems, sums, kind_s, misc = rest[:1] + rest[2 * layers :]
        others = rest[1 : 2 * layers]
    else:
        gh_next, dx_ref, keep, send, sums, dqkv_s, do_s, gw, sems, gw2 = rest
    block = pl.program_id(0)
    images = lse.shape[1]
    flat, width = dmid.shape
    padded = flat // images

    @pl.when(block == 0)
    def _():
        gw[...] = jnp.zeros_like(gw)
        sums[...] = jnp.zeros_like(sums)
        if bottom:
            kind_s[...] = jnp.zeros_like(kind_s)
        else:
            gw2[...] = jnp.zeros_like(gw2)

    dy = dmid[...].astype(BF16)
    sums[6:7, :] += jnp.sum(dy.astype(F32), 0, keepdims=True)
    do_s[...] = dot_bt(dy, w_out[0]).astype(BF16)
    gw[3] += dot_at(o[0], dy)
    pair_width = 2 * HEAD
    plain, scaled = head_masks()
    first = lax.broadcasted_iota(jnp.int32, (1, pair_width), 1) < HEAD
    for i in range(images):
        rows = slice(i * padded, (i + 1) * padded)
        length = length_of(kinds[block * images + i])
        key_ok = lax.broadcasted_iota(jnp.int32, (1, padded, 1), 1) < length
        for pair in range(HEADS // 2):
            c0 = pair * pair_width
            part = lambda base: slice(base + c0, base + c0 + pair_width)
            q2, k2, v2 = qkv[0, rows, part(0)], qkv[0, rows, part(width)], qkv[0, rows, part(2 * width)]
            do2 = do_s[rows, part(0)]
            ks = jnp.concatenate([k2 * keep for keep in scaled], 0)
            vs = jnp.concatenate([v2 * keep for keep in plain], 0)
            s = jnp.where(key_ok, dot_bt(ks, q2).reshape(2, padded, padded), -1e9)
            p = jnp.exp(s - lse[0, i, 2 * pair : 2 * pair + 2, :].reshape(2, 1, padded))
            dp = dot_bt(vs, do2).reshape(2, padded, padded)
            delta = jnp.sum(dp * p, 1, keepdims=True)
            ds = (p * (dp - delta)).astype(BF16).reshape(2 * padded, padded)
            dv = dot(p.astype(BF16).reshape(2 * padded, padded), do2)
            dk = dot(ds, q2)
            dqkv_s[rows, part(0)] = dot_at(ds, ks).astype(BF16)
            dqkv_s[rows, part(width)] = (jnp.where(first, dk[:padded], dk[padded:]) * HEAD**-0.5).astype(BF16)
            dqkv_s[rows, part(2 * width)] = jnp.where(first, dv[:padded], dv[padded:]).astype(BF16)
    d = dqkv_s[...]
    for index in (0, 2):
        row = 4 + index // 2
        sums[row : row + 1, :] += jnp.sum(d[:, index * width : (index + 1) * width].astype(F32), 0, keepdims=True)
    grad = dot_at(a[0], d)
    for index in range(3):
        gw[index] += grad[:, index * width : (index + 1) * width]
    da = dot_bt(d, w_qkv[0])
    xhat = xh[0].astype(F32)
    sums[0:1, :] += jnp.sum(da * xhat, 0, keepdims=True)
    sums[2:3, :] += jnp.sum(da, 0, keepdims=True)
    dx = dmid[...] + norm_back(da, xhat, rstd[0], gain[0, 0:1].astype(F32))
    if bottom:
        real = dx_ref.shape[1]
        for i in range(images):
            kind = kinds[block * images + i]
            here = lax.broadcasted_iota(jnp.int32, (padded, 1), 0) < length_of(kind)
            mine = jnp.where(here, dx[i * padded : (i + 1) * padded], 0.0)
            dx_ref[i] = mine[0:real]
            kind_s[kind] += mine
    else:
        dx_ref[...] = dx
        dz = dx.astype(BF16)
        for k in range(gw2.shape[0]):
            gw2[k] += dot_at(gh_next[0, :, k * width : (k + 1) * width], dz)

    @pl.when(block == pl.num_programs(0) - 1)
    def _():
        rows = width // 8
        copies = emit(me, gw, keep, send, 0, sems)
        if not bottom:
            copies += emit(me, gw2, keep, send, rows, sems.at[pl.ds(PIECES, PIECES)])
        if bottom:
            total = jnp.zeros((real, width), F32)
            for kind in range(interp.shape[0]):
                hi, mid, _ = split3(interp[kind])
                ghi, gmid, _ = split3(kind_s[kind, 0:real, :])
                total += dot_at(mid, ghi) + dot_at(hi, gmid) + dot_at(hi, ghi)
            misc[...] = jnp.zeros_like(misc)
            misc[0:real, :] = total
            misc[MISC_BASE : MISC_BASE + 16, :] = sums[...] + others[0][...]
            for layer in range(1, layers):
                start = MISC_BASE + MISC_LAYER * layer
                misc[start : start + 16, :] = others[2 * layer - 1][...] + others[2 * layer][...]
            tail = misc.shape[0] // PIECES
            for r in range(PIECES):
                j = lax.bitwise_xor(me[r // HALF], jnp.int32(r % HALF))
                target = (keep, send)[r // HALF].at[r % HALF, pl.ds(rows, tail)]
                item = pltpu.make_async_copy(misc.at[pl.ds(pl.multiple_of(j * tail, 8), tail)], target, sems.at[PIECES + r])
                item.start()
                copies.append(item)
        for item in copies:
            item.wait()


def attn_back(layer, bottom, kinds, me, dmid, o, qkv, lse, a, xh, rstd, gain, w_qkv, w_out, gh, interp, like, others, padded, per, after):
    width = dmid.shape[1]
    total = dmid.shape[0]
    layers = w_qkv.shape[0]
    flat = per * padded
    blocks = total // flat
    saved = lambda feat: pl.BlockSpec((1, flat, feat), lambda b, k, m: (layer, b, 0))
    param = lambda *shape: pl.BlockSpec((1,) + shape, lambda b, k, m: (layer, 0, 0))
    fixed = lambda *shape: pl.BlockSpec(shape, lambda b, k, m: (0,) * len(shape))
    anywhere = pl.BlockSpec(memory_space=pl.ANY)
    in_specs = [
        pl.BlockSpec((flat, width), lambda b, k, m: (b, 0)),
        saved(width),
        saved(3 * width),
        pl.BlockSpec((1, per, 8, padded), lambda b, k, m: (layer, b, 0, 0)),
        saved(width),
        saved(width),
        saved(1),
        param(2, width),
        param(width, 3 * width),
        param(width, width),
    ]
    tail = MISC_ROWS // PIECES if bottom else width // 8
    grads = pieces_of(width // 8 + tail, width)
    scratch = [
        pltpu.VMEM((flat, 3 * width), BF16),
        pltpu.VMEM((flat, width), BF16),
        pltpu.VMEM((4, width, width), F32),
        pltpu.SemaphoreType.DMA((2 * PIECES,)),
    ]
    args = [kinds, me, dmid, o, qkv, lse, a, xh, rstd, gain, w_qkv, w_out]
    if bottom:
        rows = like.shape[1]
        in_specs += [fixed(*interp.shape)] + [fixed(16, width)] * len(others)
        args += [interp] + others
        out_specs = [pl.BlockSpec((per, rows, width), lambda b, k, m: (b, 0, 0))] + [anywhere] * 2
        out_shape = [jax.ShapeDtypeStruct(like.shape, F32)] + grads
        scratch += [pltpu.VMEM((16, width), F32), pltpu.VMEM((3, padded, width), F32), pltpu.VMEM((MISC_ROWS, width), F32)]
    else:
        hidden = gh.shape[2]
        in_specs += [pl.BlockSpec((1, flat, hidden), lambda b, k, m: (layer - 1, b, 0))]
        args += [gh]
        out_specs = [pl.BlockSpec((flat, width), lambda b, k, m: (b, 0))] + [anywhere] * 2 + [fixed(16, width)]
        out_shape = [jax.ShapeDtypeStruct((total, width), F32)] + grads + [jax.ShapeDtypeStruct((16, width), F32)]
        scratch += [pltpu.VMEM((hidden // width, width, width), F32)]
    first = len(args)
    in_specs += [anywhere] * len(after)
    args += after
    return pl.pallas_call(
        drop(attn_back_kernel, (bottom, layers), first, len(after)),
        grid_spec=pltpu.PrefetchScalarGridSpec(
            num_scalar_prefetch=2,
            grid=(blocks,),
            in_specs=in_specs,
            out_specs=out_specs,
            scratch_shapes=scratch,
        ),
        out_shape=out_shape,
        compiler_params=pltpu.CompilerParams(vmem_limit_bytes=VMEM_LIMIT),
        cost_estimate=pl.CostEstimate(flops=32 * total * width * width, bytes_accessed=30 * total * width, transcendentals=0),
        name="attention_backward",
    )(*args)


def exchange(x, axis, bits, size):
    return lax.ppermute(x, axis, [(i, i ^ bits) for i in range(size)])


def combine(tasks, after, through):
    args = sum([list(inputs) for _, inputs, _ in tasks], [])
    shapes = sum([list(results) for _, _, results in tasks], [])
    parts = [(count,) + x.shape[1:] for x, _, count in args]

    def body(*refs):
        outs = refs[len(args) + len(through) + len(after) :]
        ins, sems = outs[len(shapes) + len(through) : -1], outs[-1]
        copies = []
        for k, (_, first, count) in enumerate(args):
            copies.append(pltpu.make_async_copy(refs[k].at[pl.ds(first, count)], ins[k], sems.at[k]))
            copies[-1].start()
        for function, inputs, results in tasks:
            for item in copies[: len(inputs)]:
                item.wait()
            function(ins[: len(inputs)], outs[: len(results)])
            copies, ins, outs = copies[len(inputs) :], ins[len(inputs) :], outs[len(results) :]

    vmem = pl.BlockSpec(memory_space=pltpu.VMEM)
    anywhere = pl.BlockSpec(memory_space=pl.ANY)
    moved = sum(x.size for x, _, _ in args) * 4
    out = pl.pallas_call(
        body,
        in_specs=[anywhere] * (len(args) + len(through) + len(after)),
        out_specs=[vmem] * len(shapes) + [anywhere] * len(through),
        out_shape=[jax.ShapeDtypeStruct(shape, F32) for shape in shapes] + [jax.ShapeDtypeStruct(x.shape, F32) for x in through],
        scratch_shapes=[pltpu.VMEM(part, F32) for part in parts] + [pltpu.SemaphoreType.DMA((max(len(args), 1),))],
        input_output_aliases={len(args) + k: len(shapes) + k for k in range(len(through))},
        compiler_params=pltpu.CompilerParams(vmem_limit_bytes=STEP_LIMIT),
        cost_estimate=pl.CostEstimate(flops=moved, bytes_accessed=2 * moved, transcendentals=0),
        name="combine",
    )(*[x for x, _, _ in args], *through, *after)
    result = []
    for _, _, results in tasks:
        result.append(list(out[: len(results)]))
        out = out[len(results) :]
    return result, list(out)


def sum_of(refs):
    total = refs[0][...]
    for ref in refs[1:]:
        total = total + ref[...]
    return total


def add(ins, outs):
    outs[0][...] = sum_of(ins)


def split_four(ins, outs):
    start = 0
    for group in range(0, len(ins), 4):
        rows = ins[group].shape[1]
        for k, out in enumerate(outs):
            out[start : start + rows] = sum_of([ref.at[k] for ref in ins[group : group + 4]])
        start += rows


def total_of(ins, outs):
    start = 0
    for a, b, c, d in zip(ins[::4], ins[1::4], ins[2::4], ins[3::4]):
        rows = a.shape[0]
        outs[0][start : start + rows] = (a[...] + b[...]) + (c[...] + d[...])
        start += rows


def stack(ins, outs):
    rows = ins[0].shape[0]
    for k in range(4):
        outs[0][k, :rows] = ins[k][...]
        if len(ins) > 4:
            outs[0][k, rows:] = ins[4][k]


class Round:
    def __init__(self, keep, send, sizes):
        self.keep, self.send, self.sizes, self.stage = keep, send, sizes, 0
        self.shape = keep.shape[1:]
        self.more = []
        self.parked = False

    def merge(self, other):
        assert self.stage == other.stage
        self.more = list(other.terms if self.stage == 3 else [other.keep, *other.got])
        self.shape = (self.shape[0] + other.shape[0], self.shape[1])
        return self

    def absorb(self, other):
        assert self.stage == 5 and other.parked
        self.more = [other.own]
        self.shape = (self.shape[0] + other.shape[0], self.shape[1])
        return self

    def across(self, x, which):
        bits = lambda i: (2, 4)[(i & 1) ^ which]
        return lax.ppermute(x, "grp", [(i, i ^ bits(i)) for i in range(self.sizes["grp"])])

    def swap(self, x, axis, bits):
        return exchange(x, axis, bits, self.sizes[axis])

    def tasks(self):
        stage, n = self.stage, self.shape
        if stage in (1, 2):
            half = PIECES >> (stage + 1)
            return [(add, [(x, half, half) for x in self.terms], ((half,) + n,))]
        if stage == 3:
            args, self.more = self.terms + self.more, []
            return [(split_four, [(x, 0, 4) for x in args], (n,) * 4)]
        if stage not in (4, 5):
            return []
        args, self.more = [self.keep, *self.got, *self.more], []
        args = [(x, 0, x.shape[0]) for x in args]
        if stage == 4:
            return [(total_of, args, (n,))]
        if stage == 5:
            return [(stack, args, ((4,) + n,))]
        return []

    def launch(self, done):
        stage = self.stage
        self.stage += 1
        if stage == 0:
            self.terms = [self.keep, self.swap(self.send, "grp", 1)]
        elif stage <= 2:
            self.terms = self.terms + [self.across(done[0], stage - 1)]
        elif stage == 3:
            self.keep, self.got = done[0], [self.swap(done[k], "dp", k) for k in range(1, 4)]
        elif stage == 4:
            total = done[0]
            for axis, bit in (("grp", 8), ("dp", 4)):
                while bit < self.sizes[axis]:
                    total = total + self.swap(total, axis, bit)
                    bit *= 2
            self.keep, self.got = total, [self.swap(total, "dp", k) for k in range(1, 4)]
        elif stage == 5:
            self.own = done[0]
            if self.parked:
                return
            self.second, self.first = self.across(self.own, 1), self.across(self.own, 0)
            self.pieces = [self.own, self.second, self.first, None, self.swap(self.own, "grp", 1)]
        elif stage == 6:
            self.pieces[3] = self.across(self.second, 0)
            self.pieces += [self.swap(self.second, "grp", 1), self.swap(self.first, "grp", 1)]
        else:
            self.pieces.append(self.swap(self.pieces[3], "grp", 1))


class Order:
    def __init__(self):
        self.after = []

    def step(self, *rounds, new=None):
        tasks = [item.tasks() for item in rounds]
        flat = sum(tasks, [])
        if flat:
            done, through = combine(flat, [] if new else self.after, [new.send] if new else [])
            self.after = [done[0][0]]
            for item, own in zip(rounds, tasks):
                item.launch([x for result in done[: len(own)] for x in result])
                done = done[len(own) :]
            if new:
                new.send = through[0]
        else:
            for item in rounds:
                item.launch([])
        if new:
            new.launch([])


def place(me, pieces, parts, shapes, before, after, small=()):
    names = sorted({name for name, _ in parts} | ({"out"} if "qkv" in dict(parts) else set()))
    old = [name for name in names if name in before]
    width = shapes["out"][-1]
    rows = width // 8
    count = len(pieces)

    def body(me, *refs):
        here = refs[:count]
        refs = refs[count + len(old) + len(after) :]
        outs = dict(zip(names, refs))
        smalls, (sems, *more) = refs[len(names) : len(names) + len(small)], refs[len(names) + len(small) :]
        waits = []
        if small:
            misc, tail_sems = more
            tail = MISC_ROWS // PIECES
            tails = []
            for r in range(PIECES):
                j = lax.bitwise_xor(me[r // HALF], jnp.int32(r % HALF))
                source = here[r // GROUP].at[r % GROUP, pl.ds(len(parts) * rows, tail)]
                item = pltpu.make_async_copy(source, misc.at[pl.ds(pl.multiple_of(j * tail, 8), tail)], tail_sems.at[r])
                item.start()
                tails.append(item)
        for index, (name, layer) in enumerate(parts):
            for r in range(PIECES):
                block, row = spot(me[r // HALF], r % HALF, rows)
                source = here[r // GROUP].at[r % GROUP, pl.ds(index * rows, rows)]
                sem = sems.at[index * PIECES + r]
                column = pl.ds(pl.multiple_of(block * width, 128), width)
                if name == "fc1":
                    item = pltpu.make_async_copy(source, outs[name].at[layer, pl.ds(row, rows), column], sem)
                    item.start()
                elif name == "fc2":
                    item = pltpu.make_async_copy(source, outs[name].at[layer, pl.ds(pl.multiple_of(block * width + row, 8), rows)], sem)
                    item.start()
                else:
                    item = pltpu.make_async_copy(source, outs["out"].at[layer, pl.ds(row, rows)], sem)

                    @pl.when(block < 3)
                    def _():
                        pltpu.make_async_copy(source, outs["qkv"].at[layer, pl.ds(row, rows), column], sem).start()

                    @pl.when(block == 3)
                    def _():
                        item.start()

                waits.append(item)
        if small:
            for item in tails:
                item.wait()
            gpos, ggain, gbias, gqvb, goutb, gb1, gb2 = smalls
            gpos[...] = misc[0 : gpos.shape[0], :]
            for index in range(ggain.shape[0]):
                base = MISC_BASE + MISC_LAYER * index
                ggain[index] = misc[base : base + 2, :]
                gbias[index] = misc[base + 2 : base + 4, :]
                gqvb[index] = misc[base + 4 : base + 6, :]
                goutb[index : index + 1, :] = misc[base + 6 : base + 7, :]
                for k in range(gb1.shape[1] // width):
                    gb1[index : index + 1, k * width : (k + 1) * width] = misc[base + 7 + k : base + 8 + k, :]
                gb2[index : index + 1, :] = misc[base + 11 : base + 12, :]
        for item in waits:
            item.wait()

    anywhere = pl.BlockSpec(memory_space=pl.ANY)
    vmem = pl.BlockSpec(memory_space=pltpu.VMEM)
    scratch = [pltpu.SemaphoreType.DMA((len(parts) * PIECES,))]
    if small:
        scratch += [pltpu.VMEM((MISC_ROWS, width), F32), pltpu.SemaphoreType.DMA((PIECES,))]
    out = pl.pallas_call(
        body,
        in_specs=[pl.BlockSpec(memory_space=pltpu.SMEM)] + [vmem] * count + [anywhere] * (len(old) + len(after)),
        out_specs=[anywhere] * len(names) + [vmem] * len(small),
        out_shape=[jax.ShapeDtypeStruct(shapes[name], F32) for name in names] + [jax.ShapeDtypeStruct(shape, F32) for shape in small],
        scratch_shapes=scratch,
        input_output_aliases={1 + count + index: names.index(name) for index, name in enumerate(old)},
        compiler_params=pltpu.CompilerParams(vmem_limit_bytes=2 * STEP_LIMIT),
        name="place",
    )(me, *pieces, *[before[name] for name in old], *after)
    return {**before, **dict(zip(names, out))}, list(out[len(names) :])


def on_device(sizes, tokens, kinds, interp, pos_base, ln_gain, ln_bias, w_qkv, qv_bias, w_out, out_bias, w_fc1, fc1_bias, w_fc2, fc2_bias, cotangent):
    count, rows, width = tokens.shape
    layers = w_qkv.shape[0]
    padded = -(-rows // 16) * 16
    per = 2 if count % 2 == 0 else 1
    g, d = lax.axis_index("grp"), lax.axis_index("dp")
    core, x, y = [lax.bitwise_and(lax.shift_right_logical(g, k), 1) for k in range(3)]
    low = lax.bitwise_and(d, 3)
    on_first, on_second = x * 8 + y * 4 + low, 16 + y * 8 + x * 4 + low
    me = jnp.where(core == 0, jnp.stack([on_first, on_second]), jnp.stack([on_second, on_first])).astype(jnp.int32)
    mixed, a, qkv, lse, o, c, gp, gh, xh1, r1, xh2, r2 = forward(
        kinds, tokens, interp, pos_base, ln_gain, ln_bias, w_qkv, qv_bias, w_out, out_bias, w_fc1, fc1_bias, w_fc2, fc2_bias, padded, per
    )
    small = (pos_base.shape, ln_gain.shape, ln_bias.shape, qv_bias.shape, out_bias.shape, fc1_bias.shape, fc2_bias.shape)
    shapes = {"fc1": w_fc1.shape, "fc2": w_fc2.shape, "qkv": w_qkv.shape, "out": w_out.shape}
    top = layers - 1

    def mlp(layer, dx, after):
        return mlp_back(layer, layer == top, kinds, me, dx, c, gh, gp, xh2, r2, ln_gain, w_fc1, w_fc2, padded, per, after)

    def attention(layer, dmid, sums, after):
        return attn_back(
            layer, layer == 0, kinds, me, dmid, o, qkv, lse, a, xh1, r1, ln_gain, w_qkv, w_out, gh, interp, tokens, sums, padded, per, after
        )

    order = Order()
    step = order.step
    parts = ((("fc1", 1), ("fc2", 1)), (("qkv", 1), ("fc2", 0)), (("fc1", 0),), (("qkv", 0),))
    done = {}
    rest = ()
    dmid, keep, send, sums1 = mlp(1, cotangent, [])
    q0 = Round(keep, send, sizes)
    step(q0)
    step(q0)
    dx, keep, send, sums2 = attention(1, dmid, [], order.after)
    q1 = Round(keep, send, sizes)
    step(q0, new=q1)
    dmid, keep, send, sums0 = mlp(0, dx, order.after)
    q2 = Round(keep, send, sizes)
    step(q1, q0, new=q2)
    dx, keep, send = attention(0, dmid, [sums0, sums1, sums2], order.after)
    q3 = Round(keep, send, sizes)
    step(q1, q2, q0, new=q3)
    step(q3)
    q0.parked = True
    step(q1, q0)
    step(q2, q3)
    lower = q2.merge(q3)
    step(lower, q1)
    step(lower)
    upper = q1.absorb(q0)
    step(upper)
    step(lower)
    step(upper)
    step(upper)
    done, _ = place(me, upper.pieces, (("qkv", 1), ("fc2", 0), ("fc1", 1), ("fc2", 1)), shapes, {}, order.after)
    step(lower)
    step(lower)
    done, rest = place(me, lower.pieces, (("fc1", 0), ("qkv", 0)), shapes, done, [], small)
    gpos, ggain, gbias, gqvb, goutb, gb1, gb2 = rest
    return mixed, dx, gpos, ggain, gbias, done["qkv"], gqvb, done["out"], goutb, done["fc1"], gb1, done["fc2"], gb2


def solution(mesh):
    split = P(("grp", "dp"), None, None)
    return jax.shard_map(
        partial(on_device, dict(mesh.shape)),
        mesh=mesh,
        in_specs=(split, P(("grp", "dp"))) + (P(),) * 12 + (split,),
        out_specs=(split, split) + (P(),) * 11,
        check_vma=False,
    )
```
